32 devices in a mesh: dp: 8 (over y, x, core), seq: 4 (over z).
Axes of the slice: x: 2, y: 2, z: 4, core: 2. Of those that a mesh axis runs over, the one named last changes fastest.
Arguments:
- tokens: bfloat16 [16, 1024, 2048], P('dp', 'seq'), may hold values from -6 to 6
- lengths: int32 [16, 4], P('dp'), may hold values from 1 to 1021, as said below
- w_qkv: bfloat16 [2048, 1920], P(('dp', 'seq')), may hold values from -0.125 to 0.125
- w_out: bfloat16 [1280, 2048], P(('dp', 'seq')), may hold values from -2.5 to 2.5
- w_gate_up: bfloat16 [2048, 12288], P(('dp', 'seq')), may hold values from -0.125 to 0.125
- w_down: bfloat16 [6144, 2048], P(('dp', 'seq')), may hold values from -0.078125 to 0.078125
- attn_gain: bfloat16 [2048], P(('dp', 'seq')), may hold values from 0.25 to 1.75
- ffn_gain: bfloat16 [2048], P(('dp', 'seq')), may hold values from 0.25 to 1.75
- head_gains: bfloat16 [128], P(('dp', 'seq')), may hold values from 0.25 to 1.75
- out_grad: bfloat16 [16, 1024, 2048], P('dp', 'seq'), may hold values from -6 to 6
Outputs:
- mixed: bfloat16 [16, 1024, 2048], P('dp', 'seq')
- tokens_grad: float32 [16, 1024, 2048], P('dp', 'seq')
- w_qkv_grad: float32 [2048, 1920], P(('dp', 'seq'))
- w_out_grad: float32 [1280, 2048], P(('dp', 'seq'))
- w_gate_up_grad: float32 [2048, 12288], P(('dp', 'seq'))
- w_down_grad: float32 [6144, 2048], P(('dp', 'seq'))
- attn_gain_grad: float32 [2048], P(('dp', 'seq'))
- ffn_gain_grad: float32 [2048], P(('dp', 'seq'))
- head_gains_grad: float32 [128], P(('dp', 'seq'))
The draws below stay inside these ranges and needn't reach their ends.
Inputs may be any that keep to these rules, and one draw needn't show every extreme that they name: Each row's 4 lengths are positive and sum to 1024; in every row one document, at a place drawn per row, begins within the row's first 256 positions and ends within its last 256; in one row, drawn from the seed, every other document has length 1.
All inputs are finite; a program needn't handle non-finite values.
Results may differ from the reference program's by a relative error of at most 0.018.
Values may be sent and summed in bfloat16 or wider, within the bound.
A program may use at most 384 MiB of HBM per device.

```python
import math
import jax
import jax.numpy as jnp
from jax import lax

D = 2048
QUERY_HEADS = 20
KEY_VALUE_HEADS = 5
HEAD_SIZE = 64
FF = 6144
PACKED_LENGTH = 1024
DOCS = 4
ROWS = 16
SHARD = 256
QKV_W = 1920


def draw_lengths(key, part):
    key = jax.random.fold_in(key, 11)
    first_key, second_key, third_key = jax.random.split(key, 3)
    pieces = jax.random.randint(first_key, (ROWS, DOCS - 1), 1, (SHARD - 1) // (DOCS - 1) + 1, dtype=jnp.int32)
    chosen_row = jax.random.randint(third_key, (), 0, ROWS, dtype=jnp.int32)
    row_numbers = jnp.arange(ROWS, dtype=jnp.int32)[:, None]
    pieces = jnp.where(row_numbers == chosen_row, jnp.ones_like(pieces), pieces)
    placed = jax.random.randint(second_key, (ROWS, 1), 0, DOCS, dtype=jnp.int32)
    longest = PACKED_LENGTH - jnp.sum(pieces, axis=1, keepdims=True)
    columns = jnp.arange(DOCS, dtype=jnp.int32)[None, :]
    sources = jnp.clip(jnp.where(columns < placed, columns, columns - 1), 0, DOCS - 2)
    shifted = jnp.take_along_axis(pieces, sources, axis=1)
    return jnp.where(columns == placed, longest, shifted).astype(jnp.int32)


def shard_levels(own_key, extent, cuts, low, high):
    gain = 1.0
    for position, blocks in cuts:
        draws = jax.random.uniform(jax.random.fold_in(jax.random.fold_in(own_key, 6), position), (blocks,), jnp.float32, low / len(cuts), high / len(cuts))
        gain = gain * jnp.repeat(jnp.exp(draws), extent[position] // blocks).reshape((-1,) + (1,) * (len(extent) - 1 - position))
    return gain


def centred(rng, shape, scale, most, cuts=(), kind=jnp.bfloat16):
    values = scale * jax.random.normal(rng, shape, jnp.float32)
    if cuts:
        values = values * shard_levels(rng, shape, cuts, -0.22, 0.18)
    return jnp.clip(values, -most, most).astype(kind)


def setup_inputs(seed: int = 0) -> dict:
    key_of = jax.random.split(jax.random.key(seed), 11)
    return {
        "tokens": centred(key_of[0], (ROWS, PACKED_LENGTH, D), 1.0, 6.0, ((0, 8), (1, 4))),
        "lengths": draw_lengths(jax.random.fold_in(key_of[10], 71), 0),
        "w_qkv": centred(key_of[2], (D, QKV_W), D ** -0.5, 0.125, ((0, 32),)),
        "w_out": centred(key_of[3], (QUERY_HEADS * HEAD_SIZE, D), (QUERY_HEADS * HEAD_SIZE * 4 // PACKED_LENGTH) ** -0.5, 2.5, ((0, 32),)),
        "w_gate_up": centred(key_of[4], (D, 2 * FF), D ** -0.5, 0.125, ((0, 32),)),
        "w_down": centred(key_of[5], (FF, D), FF ** -0.5, 0.078125, ((0, 32),)),
        "attn_gain": jnp.clip(1.0 + 0.15 * jax.random.normal(key_of[6], (D,), jnp.float32), 0.25, 1.75).astype(jnp.bfloat16),
        "ffn_gain": jnp.clip(1.0 + 0.15 * jax.random.normal(key_of[7], (D,), jnp.float32), 0.25, 1.75).astype(jnp.bfloat16),
        "head_gains": jnp.clip(1.0 + 0.15 * jax.random.normal(key_of[8], (2 * HEAD_SIZE,), jnp.float32), 0.25, 1.75).astype(jnp.bfloat16),
        "out_grad": centred(key_of[9], (ROWS, PACKED_LENGTH, D), 1.0, 6.0, ((0, 8), (1, 4))),
    }


@jax.custom_vjp
def lower_precision(v):
    return lax.optimization_barrier(v.astype(jnp.bfloat16)).astype(jnp.float32)

@jax.custom_vjp
def low_back(v):
    return v

def low_keep(v):
    return (lower_precision(v), None)

def low_pass(kept, grad):
    return (grad,)

def back_keep(v):
    return (v, None)

def back_low(kept, grad):
    return (lower_precision(grad),)
lower_precision.defvjp(low_keep, low_pass)
low_back.defvjp(back_keep, back_low)
epsilon = 1e-06

def norm_rows(inputs, scales):
    return inputs * lax.rsqrt(lax.optimization_barrier(jnp.mean(inputs * inputs, axis=-1, keepdims=True)) + epsilon) * scales

def rope_tables(positions):
    inverse_freq = 10000.0 ** (-(jnp.arange(HEAD_SIZE // 2, dtype=jnp.float32) * 2.0 / HEAD_SIZE))
    angles = positions.astype(jnp.float32)[:, None] * inverse_freq[None, :]
    return (jnp.cos(angles)[:, None, :], jnp.sin(angles)[:, None, :])

def rotate(head_rows, cosine_table, sine_table):
    first_half = head_rows[..., :HEAD_SIZE // 2]
    second_half = head_rows[..., HEAD_SIZE // 2:]
    return jnp.concatenate([first_half * cosine_table - second_half * sine_table, second_half * cosine_table + first_half * sine_table], axis=-1)

def prepare(projected_rows, gain_vec, cosine_table, sine_table):
    packed_row_count = projected_rows.shape[0]
    query_rows = projected_rows[:, :QUERY_HEADS * HEAD_SIZE].reshape(packed_row_count, QUERY_HEADS, HEAD_SIZE)
    key_head_rows = projected_rows[:, QUERY_HEADS * HEAD_SIZE:(QUERY_HEADS + KEY_VALUE_HEADS) * HEAD_SIZE].reshape(packed_row_count, KEY_VALUE_HEADS, HEAD_SIZE)
    value_rows = projected_rows[:, (QUERY_HEADS + KEY_VALUE_HEADS) * HEAD_SIZE:].reshape(packed_row_count, KEY_VALUE_HEADS, HEAD_SIZE)
    query_rows = rotate(norm_rows(query_rows, gain_vec[:HEAD_SIZE]), cosine_table, sine_table)
    key_head_rows = rotate(norm_rows(key_head_rows, gain_vec[HEAD_SIZE:]), cosine_table, sine_table)
    return (query_rows, key_head_rows, value_rows)

def document_ids(row_lengths, positions):
    doc_ends = jnp.cumsum(row_lengths, dtype=jnp.int32)
    return lax.optimization_barrier(jnp.sum((positions[:, None] >= doc_ends[None, :]).astype(jnp.int32), axis=1))

def soft_weights(scores, visible):
    masked = jnp.where(visible, scores, -1e+30)
    row_top = lax.optimization_barrier(jnp.max(masked, axis=-1, keepdims=True))
    exponent = jnp.exp(masked - row_top)
    return exponent / lax.optimization_barrier(jnp.sum(exponent, axis=-1, keepdims=True))

def gated(gate_up_in):
    return jax.nn.silu(gate_up_in[:, :FF]) * gate_up_in[:, FF:]

def layer_row(x_row, row_lengths, w_qkv, w_out, w_gate_up, w_down, attn_gain, ffn_gain, head_gains):
    highest = lax.Precision.HIGHEST
    positions = jnp.arange(PACKED_LENGTH, dtype=jnp.int32)
    cosine_table, sine_table = rope_tables(positions)
    documents = document_ids(row_lengths, positions)
    visible = (positions[None, :] <= positions[:, None]) & (documents[:, None] == documents[None, :])
    normed = lower_precision(norm_rows(x_row, attn_gain))
    projected_rows = low_back(jnp.dot(normed, w_qkv, precision=highest))
    query_rows, key_head_rows, value_rows = prepare(projected_rows, head_gains, cosine_table, sine_table)
    query_rows = lower_precision(query_rows).reshape(PACKED_LENGTH, KEY_VALUE_HEADS, QUERY_HEADS // KEY_VALUE_HEADS, HEAD_SIZE)
    key_head_rows = lower_precision(key_head_rows)
    value_rows = lower_precision(value_rows)
    scores = low_back(jnp.einsum('qhgd,khd->hgqk', query_rows, key_head_rows, precision=highest)) * (1.0 / math.sqrt(HEAD_SIZE))
    weights = lower_precision(soft_weights(scores, visible))
    heads_out = jnp.einsum('hgqk,khd->qhgd', weights, value_rows, precision=highest).reshape(PACKED_LENGTH, QUERY_HEADS * HEAD_SIZE)
    heads_out = low_back(lower_precision(heads_out))
    attended = low_back(jnp.dot(heads_out, w_out, precision=highest))
    middle = x_row + attended
    normed2 = lower_precision(norm_rows(middle, ffn_gain))
    gate_up = low_back(jnp.dot(normed2, w_gate_up, precision=highest))
    hidden = lower_precision(gated(gate_up))
    return middle + jnp.dot(hidden, w_down, precision=highest)

def reference(tokens, lengths, w_qkv, w_out, w_gate_up, w_down, attn_gain, ffn_gain, head_gains, out_grad):

    def forward(x_all, qkv_in, out_in, gate_up_in, down_in, attn_in, ffn_in, head_in):

        def one_row(pair):
            return layer_row(pair[0], pair[1], qkv_in, out_in, gate_up_in, down_in, attn_in, ffn_in, head_in)
        return lax.map(jax.checkpoint(one_row), (x_all, lengths))
    inputs = (tokens.astype(jnp.float32), w_qkv.astype(jnp.float32), w_out.astype(jnp.float32), w_gate_up.astype(jnp.float32), w_down.astype(jnp.float32), attn_gain.astype(jnp.float32), ffn_gain.astype(jnp.float32), head_gains.astype(jnp.float32))
    result, pullback = jax.vjp(forward, *inputs)
    grads = pullback(out_grad.astype(jnp.float32))
    return (result.astype(jnp.bfloat16), grads[0], grads[1], grads[2], grads[3], grads[4], grads[5], grads[6], grads[7])
```

```python
import math

import jax
import jax.numpy as jnp
from jax import lax
from jax.sharding import PartitionSpec as P

QUERY_HEADS = 20
KEY_VALUE_HEADS = 5
HEAD_SIZE = 64
GROUP = QUERY_HEADS // KEY_VALUE_HEADS
QW = QUERY_HEADS * HEAD_SIZE
KW = KEY_VALUE_HEADS * HEAD_SIZE
BOTH = ("dp", "seq")

epsilon = 1e-06
F32 = jnp.float32
BF16 = jnp.bfloat16


def norm_rows(inputs, scales):
    return inputs * lax.rsqrt(jnp.mean(inputs * inputs, axis=-1, keepdims=True) + epsilon) * scales


def rope_tables(positions):
    inverse_freq = 10000.0 ** (-(jnp.arange(HEAD_SIZE // 2, dtype=F32) * 2.0 / HEAD_SIZE))
    angles = positions.astype(F32)[:, None] * inverse_freq[None, :]
    return (jnp.cos(angles)[:, None, :], jnp.sin(angles)[:, None, :])


def rotate(head_rows, cosine_table, sine_table):
    first_half = head_rows[..., : HEAD_SIZE // 2]
    second_half = head_rows[..., HEAD_SIZE // 2 :]
    return jnp.concatenate(
        [
            first_half * cosine_table - second_half * sine_table,
            second_half * cosine_table + first_half * sine_table,
        ],
        axis=-1,
    )


def prepare(projected_rows, gain_vec, cosine_table, sine_table):
    count = projected_rows.shape[0]
    query_rows = projected_rows[:, :QW].reshape(count, QUERY_HEADS, HEAD_SIZE)
    key_rows = projected_rows[:, QW : QW + KW].reshape(count, KEY_VALUE_HEADS, HEAD_SIZE)
    value_rows = projected_rows[:, QW + KW :].reshape(count, KEY_VALUE_HEADS, HEAD_SIZE)
    query_rows = rotate(norm_rows(query_rows, gain_vec[:HEAD_SIZE]), cosine_table, sine_table)
    key_rows = rotate(norm_rows(key_rows, gain_vec[HEAD_SIZE:]), cosine_table, sine_table)
    return (query_rows, key_rows, value_rows)


def document_ids(row_lengths, positions):
    doc_ends = jnp.cumsum(row_lengths, axis=-1, dtype=jnp.int32)
    return jnp.sum((positions[None, :, None] >= doc_ends[:, None, :]).astype(jnp.int32), axis=2)


def soft_weights(scores, visible):
    masked = jnp.where(visible, scores, -1e30)
    row_top = jnp.max(masked, axis=-1, keepdims=True)
    exponent = jnp.exp(masked - row_top)
    return exponent / jnp.sum(exponent, axis=-1, keepdims=True)


def mm(a, b):
    return jnp.dot(a, b, preferred_element_type=F32)


def outer_sum(left, right):
    return lax.dot_general(left, right, (((0,), (0,)), ((), ())), preferred_element_type=F32)


def back_product(rows, weight):
    return lax.dot_general(rows, weight, (((1,), (1,)), ((), ())), preferred_element_type=F32)


def gather(x, axes):
    return lax.all_gather(x, axes, axis=0, tiled=True)


def scatter(x, axes):
    return lax.psum_scatter(x, axes, scatter_dimension=0, tiled=True)


def shards(
    tokens, lengths, w_qkv, w_out, w_gate_up, w_down, attn_gain, ffn_gain, head_gains, out_grad
):
    n_dp, n_seq = lax.axis_size("dp"), lax.axis_size("seq")
    rows, length, width = tokens.shape
    count = rows * length
    seq_len = length * n_seq
    ff = w_gate_up.shape[1] // 2
    part = ff // n_dp
    wr = w_gate_up.shape[0]
    scaling = 1.0 / math.sqrt(HEAD_SIZE)
    offset = lax.axis_index("seq") * length
    positions = jnp.arange(seq_len, dtype=jnp.int32)
    local_pos = offset + jnp.arange(length, dtype=jnp.int32)
    cosine_table, sine_table = rope_tables(local_pos)
    cosine_all = jnp.concatenate([cosine_table] * rows, axis=0)
    sine_all = jnp.concatenate([sine_table] * rows, axis=0)

    heads_column = jnp.pad(head_gains, (0, wr - head_gains.shape[0]))
    extra = jnp.stack([attn_gain, ffn_gain, heads_column], axis=1)
    extra = jnp.pad(extra, ((0, 0), (0, 125)))
    qkv_ext = gather(jnp.concatenate([w_qkv, extra], axis=1), BOTH)
    qkv_w = w_qkv.shape[1]
    qkv_full = qkv_ext[:, :qkv_w]
    attn_gain_full = qkv_ext[:, qkv_w].astype(F32)
    ffn_gain_full = qkv_ext[:, qkv_w + 1].astype(F32)
    head_full = (
        qkv_ext[:, qkv_w + 2]
        .reshape(n_dp * n_seq, wr)[:, : head_gains.shape[0]]
        .reshape(-1)
        .astype(F32)
    )
    out_full = gather(w_out, BOTH)

    spread = lax.all_to_all(w_gate_up.reshape(wr, 2, n_dp, part), "dp", 2, 0, tiled=False)
    spread = spread.reshape(n_dp * wr, 2 * part)
    gate_up_w = gather(spread, "seq").reshape(n_seq, n_dp, wr, 2 * part)
    gate_up_w = gate_up_w.transpose(1, 0, 2, 3).reshape(width, 2 * part)
    down_w = gather(w_down, "seq")

    cotangent_low = out_grad.reshape(count, width)
    cotangent_all = gather(cotangent_low, "dp")

    x_rows = tokens.reshape(count, width).astype(F32)
    normed, norm_pull = jax.vjp(norm_rows, x_rows, attn_gain_full)
    normed_low = normed.astype(BF16)
    projected_rows = mm(normed_low, qkv_full)

    def prep_local(projected_in, gain_vec):
        return prepare(projected_in, gain_vec, cosine_all, sine_all)

    (query_rows, key_rows, value_rows), prep_pull = jax.vjp(prep_local, projected_rows, head_full)
    queries = query_rows.astype(BF16).reshape(rows, length, KEY_VALUE_HEADS, GROUP, HEAD_SIZE)
    kv_low = jnp.concatenate(
        [key_rows.astype(BF16).reshape(count, KW), value_rows.astype(BF16).reshape(count, KW)],
        axis=1,
    )
    kv_all = gather(kv_low, "seq").reshape(n_seq, rows, length, 2, KEY_VALUE_HEADS, HEAD_SIZE)
    kv_all = kv_all.transpose(1, 3, 0, 2, 4, 5).reshape(
        rows, 2, seq_len, KEY_VALUE_HEADS, HEAD_SIZE
    )
    keys_all, values_all = kv_all[:, 0], kv_all[:, 1]
    documents = document_ids(lengths, positions)
    local_docs = lax.dynamic_slice_in_dim(documents, offset, length, axis=1)
    visible = (positions[None, None, :] <= local_pos[None, :, None]) & (
        local_docs[:, :, None] == documents[:, None, :]
    )
    visible = visible[:, None, None]
    scores = (
        jnp.einsum("rqhgd,rkhd->rhgqk", queries, keys_all, preferred_element_type=F32) * scaling
    )
    weights = soft_weights(scores, visible)
    weights_low = weights.astype(BF16)
    heads_out = (
        jnp.einsum("rhgqk,rkhd->rqhgd", weights_low, values_all, preferred_element_type=F32)
        .astype(BF16)
        .reshape(count, QW)
    )
    middle = x_rows + mm(heads_out, out_full)
    normed2, norm2_pull = jax.vjp(norm_rows, middle, ffn_gain_full)
    normed2_all = gather(normed2.astype(BF16), "dp")

    gate_up = mm(normed2_all, gate_up_w).astype(BF16)
    gate, up = gate_up[:, :part].astype(F32), gate_up[:, part:].astype(F32)
    sig = jax.nn.sigmoid(gate)
    hidden = (gate * sig * up).astype(BF16)
    mixed = middle + scatter(mm(hidden, down_w).astype(BF16), "dp").astype(F32)

    down_grad = scatter(outer_sum(hidden, cotangent_all).astype(BF16), "seq")
    dhidden = back_product(cotangent_all, down_w)
    dgate = dhidden * up * sig * (1.0 + gate * (1.0 - sig))
    dup = dhidden * gate * sig
    dgate_up = jnp.concatenate([dgate.astype(BF16), dup.astype(BF16)], axis=1)
    dnormed2 = scatter(back_product(dgate_up, gate_up_w).astype(BF16), "dp").astype(F32)
    gate_up_grad = outer_sum(normed2_all, dgate_up).astype(BF16)
    gate_up_grad = gate_up_grad.reshape(n_dp, n_seq, wr, 2 * part).transpose(1, 0, 2, 3)
    gate_up_grad = scatter(gate_up_grad.reshape(width, 2 * part), "seq")
    gate_up_grad = lax.all_to_all(
        gate_up_grad.reshape(n_dp, wr, 2, part), "dp", 0, 2, tiled=False
    ).reshape(wr, 2 * ff)

    dmiddle_norm, ffn_gain_grad = norm2_pull(dnormed2)
    dmiddle = cotangent_low.astype(F32) + dmiddle_norm
    dattend = dmiddle.astype(BF16)
    out_weight_grad = scatter(outer_sum(heads_out, dattend).astype(BF16), BOTH)
    dheads = (
        back_product(dattend, out_full)
        .astype(BF16)
        .reshape(rows, length, KEY_VALUE_HEADS, GROUP, HEAD_SIZE)
    )
    dweights = jnp.einsum("rqhgd,rkhd->rhgqk", dheads, values_all, preferred_element_type=F32)
    dscores = (
        weights * (dweights - jnp.sum(weights * dweights, axis=-1, keepdims=True))
    ).astype(BF16)
    dqueries = (
        jnp.einsum("rhgqk,rkhd->rqhgd", dscores, keys_all, preferred_element_type=F32).reshape(
            count, QUERY_HEADS, HEAD_SIZE
        )
        * scaling
    )
    dkeys = (
        jnp.einsum("rhgqk,rqhgd->rkhd", dscores, queries, preferred_element_type=F32) * scaling
    )
    dvalues = jnp.einsum("rhgqk,rqhgd->rkhd", weights_low, dheads, preferred_element_type=F32)
    dkv = jnp.concatenate(
        [dkeys.reshape(rows, n_seq, length, KW), dvalues.reshape(rows, n_seq, length, KW)], axis=3
    ).astype(BF16)
    dkv = scatter(dkv.transpose(1, 0, 2, 3).reshape(n_seq * count, 2 * KW), "seq").astype(F32)
    dprojected, head_grad = prep_pull(
        (
            dqueries,
            dkv[:, :KW].reshape(count, KEY_VALUE_HEADS, HEAD_SIZE),
            dkv[:, KW:].reshape(count, KEY_VALUE_HEADS, HEAD_SIZE),
        )
    )
    dprojected_low = dprojected.astype(BF16)
    qkv_grad = outer_sum(normed_low, dprojected_low).astype(BF16)
    qkv_grad = scatter(scatter(qkv_grad, "dp"), "seq")
    dnormed = back_product(dprojected_low, qkv_full)
    dx_norm, attn_gain_grad = norm_pull(dnormed)
    tokens_grad = dmiddle + dx_norm

    n_all = n_dp * n_seq
    small = jnp.concatenate(
        [
            attn_gain_grad.reshape(n_all, -1),
            ffn_gain_grad.reshape(n_all, -1),
            head_grad.reshape(n_all, -1),
        ],
        axis=1,
    )
    small = jnp.sum(lax.all_to_all(small, BOTH, 0, 0, tiled=False), axis=0)
    attn_gain_out = small[:wr]
    ffn_gain_out = small[wr : 2 * wr]
    head_out = small[2 * wr :]
    return (
        mixed.astype(BF16).reshape(rows, length, width),
        tokens_grad.reshape(rows, length, width),
        qkv_grad.astype(F32),
        out_weight_grad.astype(F32),
        gate_up_grad.astype(F32),
        down_grad.astype(F32),
        attn_gain_out,
        ffn_gain_out,
        head_out,
    )


def solution(mesh):
    in_specs = (
        P("dp", "seq", None),
        P("dp", None),
        P(("dp", "seq"), None),
        P(("dp", "seq"), None),
        P(("dp", "seq"), None),
        P(("dp", "seq"), None),
        P(("dp", "seq")),
        P(("dp", "seq")),
        P(("dp", "seq")),
        P("dp", "seq", None),
    )
    out_specs = (
        P("dp", "seq", None),
        P("dp", "seq", None),
        P(("dp", "seq"), None),
        P(("dp", "seq"), None),
        P(("dp", "seq"), None),
        P(("dp", "seq"), None),
        P(("dp", "seq")),
        P(("dp", "seq")),
        P(("dp", "seq")),
    )
    return jax.shard_map(shards, mesh=mesh, in_specs=in_specs, out_specs=out_specs, check_vma=False)
```

```python
import functools

import jax
import jax.numpy as jnp
from jax import lax
from jax.experimental import pallas as pl
from jax.experimental.pallas import tpu as pltpu
from jax.sharding import PartitionSpec as P

QUERY_HEADS = 20
KEY_VALUE_HEADS = 5
HEAD_SIZE = 64
GROUP = QUERY_HEADS // KEY_VALUE_HEADS
QW = QUERY_HEADS * HEAD_SIZE
KW = KEY_VALUE_HEADS * HEAD_SIZE
BOTH = ("dp", "seq")

epsilon = 1e-06
F32 = jnp.float32
BF16 = jnp.bfloat16
MESH = pl.DeviceIdType.MESH


def norm_rows(inputs, scales):
    return inputs * lax.rsqrt(jnp.mean(inputs * inputs, axis=-1, keepdims=True) + epsilon) * scales


def rope_tables(positions):
    inverse_freq = 10000.0 ** (-(jnp.arange(HEAD_SIZE // 2, dtype=F32) * 2.0 / HEAD_SIZE))
    angles = inverse_freq[:, None] * positions.astype(F32)[None, :]
    return (jnp.cos(angles)[None], jnp.sin(angles)[None])


def turn(heads, gain, cosine, sine):
    inverse = lax.rsqrt(jnp.mean(heads * heads, axis=1, keepdims=True) + epsilon)
    heads = heads * inverse * gain[None, :, None]
    first, second = heads[:, : HEAD_SIZE // 2], heads[:, HEAD_SIZE // 2 :]
    return jnp.concatenate([first * cosine - second * sine, second * cosine + first * sine], axis=1)


def prepare(projected, gains, cosine, sine):
    tokens = projected.shape[1]
    queries = projected[:QW].reshape(QUERY_HEADS, HEAD_SIZE, tokens)
    pairs = projected[QW:].reshape(KEY_VALUE_HEADS, 2, HEAD_SIZE, tokens)
    queries = turn(queries, gains[:HEAD_SIZE], cosine, sine) * (HEAD_SIZE**-0.5)
    keys = turn(pairs[:, 0], gains[HEAD_SIZE:], cosine, sine)
    pairs = jnp.stack([keys, pairs[:, 1]], axis=1)
    return queries.reshape(QW, tokens), pairs.reshape(2 * KW, tokens)


def dot(a, b):
    return jnp.dot(a, b, preferred_element_type=F32)


def seen(back, me, start, length):
    key = lax.broadcasted_iota(jnp.int32, (length, length), 0)
    found = key + (me - back) * length >= start
    if back == 0:
        found &= key <= lax.broadcasted_iota(jnp.int32, (length, length), 1)
    return found


def attend_kernel(blocks, me_ref, start_ref, q_ref, *refs):
    kv_refs, (o_ref, lse_ref, o_acc, l_acc) = refs[:blocks], refs[blocks:]
    me = me_ref[0]
    length = q_ref.shape[1]
    start = start_ref[0:1, :]
    for back in range(blocks):

        def block(back=back):
            keys = kv_refs[back][:HEAD_SIZE, :].T
            values = kv_refs[back][HEAD_SIZE:, :]
            visible = seen(back, me, start, length)
            for g in range(GROUP):
                rows = slice(g * HEAD_SIZE, (g + 1) * HEAD_SIZE)
                p = jnp.where(visible, jnp.exp(dot(keys, q_ref[rows, :])), 0.0)
                total = jnp.sum(p, axis=0, keepdims=True)
                out = dot(values, p.astype(BF16))
                if back == 0:
                    l_acc[g : g + 1, :] = total
                    o_acc[rows, :] = out
                else:
                    l_acc[g : g + 1, :] += total
                    o_acc[rows, :] += out

        if back == 0:
            block()
        else:
            pl.when(me >= back)(block)
    for g in range(GROUP):
        rows = slice(g * HEAD_SIZE, (g + 1) * HEAD_SIZE)
        o_ref[rows, :] = (o_acc[rows, :] / l_acc[g : g + 1, :]).astype(BF16)
        lse_ref[g : g + 1, :] = jnp.log(l_acc[g : g + 1, :])


def attend_back_kernel(blocks, me_ref, start_ref, q_ref, do_ref, o_ref, lse_ref, *refs):
    kv_refs, dq_ref = refs[:blocks], refs[blocks]
    dkv_refs, (dq_acc, dk_acc, dv_acc) = refs[blocks + 1 : 2 * blocks + 1], refs[2 * blocks + 1 :]
    me = me_ref[0]
    length = q_ref.shape[1]
    start = start_ref[0:1, :]
    for back in range(blocks):

        def block(back=back):
            keys_t = kv_refs[back][:HEAD_SIZE, :]
            keys = keys_t.T
            values = kv_refs[back][HEAD_SIZE:, :].T
            visible = seen(back, me, start, length)
            for g in range(GROUP):
                rows = slice(g * HEAD_SIZE, (g + 1) * HEAD_SIZE)
                q, do = q_ref[rows, :], do_ref[rows, :]
                p = jnp.exp(dot(keys, q) - lse_ref[g : g + 1, :])
                p = jnp.where(visible, p, 0.0)
                inner = jnp.sum(
                    do.astype(F32) * o_ref[rows, :].astype(F32), axis=0, keepdims=True
                )
                ds = (p * (dot(values, do) - inner)).astype(BF16)
                dv = dot(p.astype(BF16), do.T)
                dk = dot(ds, q.T)
                dq = dot(keys_t, ds)
                if g == 0:
                    dk_acc[...] = dk
                    dv_acc[...] = dv
                else:
                    dk_acc[...] += dk
                    dv_acc[...] += dv
                if back == 0:
                    dq_acc[rows, :] = dq
                else:
                    dq_acc[rows, :] += dq
            dkv_refs[back][:HEAD_SIZE, :] = dk_acc[...].T.astype(BF16)
            dkv_refs[back][HEAD_SIZE:, :] = dv_acc[...].T.astype(BF16)

        if back == 0:
            block()
        else:
            pl.when(me >= back)(block)

            @pl.when(me < back)
            def _(back=back):
                dkv_refs[back][...] = jnp.zeros_like(dkv_refs[back])

    dq_ref[...] = dq_acc[...]


def attend(me, start, queries, pairs, rows):
    blocks, length = len(pairs), queries.shape[1] // rows
    spec = lambda height: pl.BlockSpec((height, length), lambda r, h, m: (h, r))
    return pl.pallas_call(
        functools.partial(attend_kernel, blocks),
        grid_spec=pltpu.PrefetchScalarGridSpec(
            num_scalar_prefetch=1,
            grid=(rows, KEY_VALUE_HEADS),
            in_specs=[
                pl.BlockSpec((8, length), lambda r, h, m: (0, r)),
                spec(GROUP * HEAD_SIZE),
                *[spec(2 * HEAD_SIZE)] * blocks,
            ],
            out_specs=[spec(GROUP * HEAD_SIZE), spec(8)],
            scratch_shapes=[
                pltpu.VMEM((GROUP * HEAD_SIZE, length), F32),
                pltpu.VMEM((8, length), F32),
            ],
        ),
        out_shape=[
            jax.ShapeDtypeStruct(queries.shape, BF16),
            jax.ShapeDtypeStruct((8 * KEY_VALUE_HEADS, queries.shape[1]), F32),
        ],
        compiler_params=pltpu.CompilerParams(vmem_limit_bytes=48 * 2**20),
        name="attend",
    )(me, start, queries, *pairs)


def attend_back(me, start, queries, pairs, dheads, heads, lse, rows):
    blocks, length = len(pairs), queries.shape[1] // rows
    spec = lambda height: pl.BlockSpec((height, length), lambda r, h, m: (h, r))
    wide, pair = spec(GROUP * HEAD_SIZE), spec(2 * HEAD_SIZE)
    return pl.pallas_call(
        functools.partial(attend_back_kernel, blocks),
        grid_spec=pltpu.PrefetchScalarGridSpec(
            num_scalar_prefetch=1,
            grid=(rows, KEY_VALUE_HEADS),
            in_specs=[
                pl.BlockSpec((8, length), lambda r, h, m: (0, r)),
                *[wide] * 3,
                spec(8),
                *[pair] * blocks,
            ],
            out_specs=[wide, *[pair] * blocks],
            scratch_shapes=[
                pltpu.VMEM((GROUP * HEAD_SIZE, length), F32),
                pltpu.VMEM((length, HEAD_SIZE), F32),
                pltpu.VMEM((length, HEAD_SIZE), F32),
            ],
        ),
        out_shape=[
            jax.ShapeDtypeStruct(queries.shape, F32),
            *[jax.ShapeDtypeStruct(pairs[0].shape, BF16)] * blocks,
        ],
        compiler_params=pltpu.CompilerParams(vmem_limit_bytes=48 * 2**20),
        name="attend_back",
    )(me, start, queries, dheads, heads, lse, *pairs)


def places():
    d, s = lax.axis_index("dp"), lax.axis_index("seq")
    core, column, line = d % 2, (d // 2) % 2, d // 4
    return d, s, d + 1 - 2 * core, d + 2 - 4 * column, d + 4 - 8 * line, line


def greet(peers, line=None):
    barrier = pltpu.get_barrier_semaphore()

    def signal(peer):
        pl.semaphore_signal(barrier, inc=1, device_id=peer, device_id_type=MESH)

    for peer in peers:
        signal(peer)
    if line is None:
        pl.semaphore_wait(barrier, len(peers))
        return
    d, s = line
    pl.when(s < 3)(lambda: signal((d, s + 1)))
    pl.when(s > 0)(lambda: signal((d, s - 1)))
    pl.semaphore_wait(barrier, len(peers) + 1 - s // 3 + (s + 2) // 3)


def remote(src, dst, sent, got, peer):
    return pltpu.make_async_remote_copy(
        src_ref=src,
        dst_ref=dst,
        send_sem=sent,
        recv_sem=got,
        device_id=peer,
        device_id_type=MESH,
    )


def weights_kernel(n, *refs):
    x_refs, out_refs = refs[:n], refs[n : 2 * n]
    own_sem, recv, send_z, send_x, send_y, send_d, send_c = refs[2 * n :]
    d, s, d_c, d_x, d_y, line = places()
    d_d = d_x + 4 - 8 * line
    greet([(d_c, s), (d_x, s), (d_y, s)], (d, s))

    def copies(slot, sent, got, peer, own=False):
        return [
            remote(
                x_refs[i] if own else out_refs[i].at[slot],
                out_refs[i].at[slot],
                sent(i),
                got(i),
                peer,
            )
            for i in range(n)
        ]

    def start(group):
        for one in group:
            one.start()

    def sent(group):
        for one in group:
            one.wait_send()

    def each(visit):
        visit(s, 0)
        for far in (1, 2, 3):
            pl.when(s >= far)(lambda far=far: visit(s - far, 1))
            pl.when(s + far <= 3)(lambda far=far: visit(s + far, -1))

    def got(k, b):
        return lambda i: recv.at[i, k, b]

    def arrived(k, b):
        for one in copies(d * 4 + b, lambda i: send_x.at[i, b], got(k, b), (d_x, s)):
            one.wait_recv()

    own = [
        pltpu.make_async_copy(x_refs[i], out_refs[i].at[d * 4 + s], own_sem.at[i])
        for i in range(n)
    ]
    start(own)

    def up(b, own=False):
        return copies(d * 4 + b, lambda i: send_z.at[i, 0, b], got(0, b), (d, s + 1), own)

    def down(b, own=False):
        return copies(d * 4 + b, lambda i: send_z.at[i, 1, b], got(0, b), (d, s - 1), own)

    def spread(b, own=False):
        return (
            copies(d * 4 + b, lambda i: send_x.at[i, b], got(2, b), (d_x, s), own)
            + copies(d * 4 + b, lambda i: send_y.at[i, b], got(4, b), (d_y, s), own)
            + copies(d * 4 + b, lambda i: send_c.at[i, 0, b], got(1, b), (d_c, s), own)
        )

    def column_block(b, direction):
        own = direction == 0
        if direction:
            arrived(0, b)
        if direction >= 0:
            pl.when(s < 3)(lambda: start(up(b, own)))
        if direction <= 0:
            pl.when(s > 0)(lambda: start(down(b, own)))
        start(spread(b, own))

    each(column_block)

    def over_y(b):
        return copies(d_x * 4 + b, lambda i: send_d.at[i, b], got(6, b), (d_y, s))

    def over_x(b):
        return copies(d_y * 4 + b, lambda i: send_d.at[i, b], got(6, b), (d_x, s))

    def to_core(index, holder, b):
        return copies(
            holder * 4 + b, lambda i: send_c.at[i, index, b], got(2 * index + 1, b), (d_c, s)
        )

    def side_blocks(b, direction):
        arrived(2, b)
        pl.when(b % 2 == 0)(lambda: start(over_y(b)))
        start(to_core(1, d_x, b))
        arrived(4, b)
        pl.when(b % 2 == 1)(lambda: start(over_x(b)))
        start(to_core(2, d_y, b))

    each(side_blocks)

    def far_block(b, direction):
        arrived(6, b)
        start(to_core(3, d_d, b))

    each(far_block)

    def finish(b, direction):
        for k in (1, 3, 5, 7):
            arrived(k, b)
        if direction >= 0:
            pl.when(s < 3)(lambda: sent(up(b)))
        if direction <= 0:
            pl.when(s > 0)(lambda: sent(down(b)))
        sent(spread(b))
        sent(over_y(b))
        sent(to_core(1, d_x, b))
        sent(to_core(2, d_y, b))
        sent(to_core(3, d_d, b))

    each(finish)
    for one in own:
        one.wait()


def gather_weights(arrays, n_dp, n_seq):
    if (n_dp, n_seq) != (8, 4):
        return [lax.all_gather(x, BOTH, axis=0, tiled=False) for x in arrays]
    n = len(arrays)
    dma = pltpu.SemaphoreType.DMA
    return pl.pallas_call(
        functools.partial(weights_kernel, n),
        out_shape=[jax.ShapeDtypeStruct((n_dp * n_seq, *x.shape), x.dtype) for x in arrays],
        in_specs=[pl.BlockSpec(memory_space=pl.ANY)] * n,
        out_specs=[pl.BlockSpec(memory_space=pl.ANY)] * n,
        scratch_shapes=[
            dma((n,)),
            dma((n, 8, 4)),
            dma((n, 2, 4)),
            dma((n, 4)),
            dma((n, 4)),
            dma((n, 4)),
            dma((n, 4, 4)),
        ],
        compiler_params=pltpu.CompilerParams(collective_id=1, has_side_effects=True),
        name="gather_weights",
    )(*arrays)


def sum_weights_kernel(g_ref, out_ref, kept, rcv_c, rcv_d, rcv_x, rcv_y, rcv_z, *sems):
    load, sent_c, got_c, sent_p, got_p, sent_z, got_z = sems
    d, s, d_c, d_x, d_y, line = places()
    d_d = d_x + 4 - 8 * line
    holders = (d, d_x, d_y, d_d)
    greet([(d_c, s), (d_x, s), (d_y, s)], (d, s))
    swapped = d_c - d
    loads, crossing = [], []
    for i in (3, 1, 2, 0):
        one = remote(
            g_ref.at[pl.ds((holders[i] + swapped) * 4, 4)],
            rcv_c.at[i],
            sent_c.at[i],
            got_c.at[i],
            (d_c, s),
        )
        one.start()
        crossing.append(one)
        one = pltpu.make_async_copy(
            g_ref.at[pl.ds(holders[i] * 4, 4)], kept.at[i], load.at[i]
        )
        one.start()
        loads.append(one)

    def plus(ref, *others):
        total = ref[...].astype(F32)
        for other in others:
            total += other[...].astype(F32)
        ref[...] = total.astype(BF16)

    def merge(turn, i):
        loads[turn].wait()
        crossing[turn].wait_recv()
        plus(kept.at[i], rcv_c.at[i])

    low, high = pl.ds(0, 2), pl.ds(2, 2)

    def pushed(src, dst, n, peer):
        one = remote(src, dst, sent_p.at[n], got_p.at[n], (peer, s))
        one.start()
        return one

    merge(0, 3)
    far_x = pushed(kept.at[3, low], rcv_d.at[low], 0, d_x)
    far_y = pushed(kept.at[3, high], rcv_d.at[high], 1, d_y)
    merge(1, 1)
    x_low = pushed(kept.at[1, low], rcv_x.at[low], 2, d_x)
    merge(2, 2)
    y_high = pushed(kept.at[2, high], rcv_y.at[high], 3, d_y)
    merge(3, 0)
    far_x.wait_recv()
    plus(kept.at[2, low], rcv_d.at[low])
    y_low = pushed(kept.at[2, low], rcv_y.at[low], 4, d_y)
    far_y.wait_recv()
    plus(kept.at[1, high], rcv_d.at[high])
    x_high = pushed(kept.at[1, high], rcv_x.at[high], 5, d_x)
    x_low.wait_recv()
    y_low.wait_recv()
    plus(kept.at[0, low], rcv_x.at[low], rcv_y.at[low])
    x_high.wait_recv()
    y_high.wait_recv()
    plus(kept.at[0, high], rcv_x.at[high], rcv_y.at[high])

    def up(b):
        return remote(
            kept.at[0, b], rcv_z.at[0, b], sent_z.at[0, b], got_z.at[0, b], (d, s + 1)
        )

    def down(b):
        return remote(
            kept.at[0, b], rcv_z.at[1, b], sent_z.at[1, b], got_z.at[1, b], (d, s - 1)
        )

    def send_up(b):
        @pl.when(s > 0)
        def _():
            up(b).wait_recv()
            plus(kept.at[0, b], rcv_z.at[0, b])

        up(b).start()

    def send_down(b):
        @pl.when(s < 3)
        def _():
            down(b).wait_recv()
            plus(kept.at[0, b], rcv_z.at[1, b])

        down(b).start()

    for b in (3, 2, 1):
        pl.when(s < b)(functools.partial(send_up, b))
        pl.when(s > 3 - b)(functools.partial(send_down, 3 - b))
    out_ref[...] = kept[0, s].astype(F32)

    @pl.when(s > 0)
    def _():
        up(s).wait_recv()
        out_ref[...] += rcv_z[0, s].astype(F32)

    @pl.when(s < 3)
    def _():
        down(s).wait_recv()
        out_ref[...] += rcv_z[1, s].astype(F32)

    for b in (3, 2, 1):
        pl.when(s < b)(lambda b=b: up(b).wait_send())
        pl.when(s > 3 - b)(lambda b=b: down(3 - b).wait_send())
    for one in crossing + [far_x, far_y, x_low, y_high, y_low, x_high]:
        one.wait_send()


def sum_weights(g, n_dp, n_seq, number):
    if (n_dp, n_seq) != (8, 4):
        flat = g.reshape(-1, g.shape[2])
        return scatter(scatter(flat, "dp"), "seq").astype(F32)
    _, rows, columns = g.shape
    dma = pltpu.SemaphoreType.DMA
    buffer = lambda *lead: pltpu.VMEM((*lead, rows, columns), BF16)
    return pl.pallas_call(
        sum_weights_kernel,
        out_shape=jax.ShapeDtypeStruct((rows, columns), F32),
        in_specs=[pl.BlockSpec(memory_space=pl.ANY)],
        out_specs=pl.BlockSpec(memory_space=pltpu.VMEM),
        scratch_shapes=[
            buffer(4, 4),
            buffer(4, 4),
            buffer(4),
            buffer(4),
            buffer(4),
            buffer(2, 4),
            dma((4,)),
            dma((4,)),
            dma((4,)),
            dma((6,)),
            dma((6,)),
            dma((2, 4)),
            dma((2, 4)),
        ],
        compiler_params=pltpu.CompilerParams(
            collective_id=number, has_side_effects=True, vmem_limit_bytes=40 * 2**20
        ),
        name="sum_weights",
    )(g)


def plane_kernel(x_ref, out_ref, own_sem, sent, got):
    d, s, d_c, d_x, d_y, line = places()
    greet([(d_c, s), (d_x, s), (d_y, s)])
    half = x_ref.shape[0] // 2
    halves = (pl.ds(0, half), pl.ds(half, half))

    def piece(k, h, peer, first=False):
        source = {1: 0, 2: 0, 4: 0, 3: 2, 5: 4, 7: 6}
        back = source[k] if k in source else (4 if h == 0 else 2)
        src = x_ref.at[halves[h]] if back == 0 else out_ref.at[back, halves[h]]
        return remote(src, out_ref.at[k, halves[h]], sent.at[k, h], got.at[k, h], (peer, s))

    own = pltpu.make_async_copy(x_ref, out_ref.at[0], own_sem)
    own.start()
    to = {1: d_c, 2: d_x, 4: d_y, 3: d_c, 5: d_c, 7: d_c}
    for h in (0, 1):
        for k in (2, 4, 1):
            piece(k, h, to[k]).start()
    piece(4, 0, d_y).wait_recv()
    piece(6, 0, d_x).start()
    piece(5, 0, d_c).start()
    piece(2, 0, d_x).wait_recv()
    piece(3, 0, d_c).start()
    piece(2, 1, d_x).wait_recv()
    piece(6, 1, d_y).start()
    piece(3, 1, d_c).start()
    piece(4, 1, d_y).wait_recv()
    piece(5, 1, d_c).start()
    piece(6, 0, d_x).wait_recv()
    piece(7, 0, d_c).start()
    piece(6, 1, d_y).wait_recv()
    piece(7, 1, d_c).start()
    for k in (1, 3, 5, 7):
        for h in (0, 1):
            piece(k, h, d_c).wait_recv()
    for k in range(1, 8):
        for h in (0, 1):
            piece(k, h, d_c).wait_send()
    own.wait()


def plane_gather_now(x, n_dp, n_seq):
    if (n_dp, n_seq) != (8, 4):
        return lax.all_gather(x, "dp", axis=0, tiled=True)
    dma = pltpu.SemaphoreType.DMA
    return pl.pallas_call(
        plane_kernel,
        out_shape=jax.ShapeDtypeStruct((n_dp, *x.shape), x.dtype),
        in_specs=[pl.BlockSpec(memory_space=pl.ANY)],
        out_specs=pl.BlockSpec(memory_space=pl.ANY),
        scratch_shapes=[dma, dma((8, 2)), dma((8, 2))],
        compiler_params=pltpu.CompilerParams(collective_id=4, has_side_effects=True),
        name="plane_gather",
    )(x).reshape(n_dp * x.shape[0], x.shape[1])


def plane_sum_kernel(
    g_ref, w_ref, x_ref, out_ref, grad_ref, w_v, g_v, kept, leaving, rcv_c, rcv_d, rcv_x, rcv_y,
    acc, w_sem, g_sem, sent_c, got_c, sent_p, got_p, out_sem,
):
    d, s, d_c, d_x, d_y, line = places()
    rows, deep = g_v.shape[1], g_v.shape[2]
    width = w_v.shape[0]
    order = (7, 6, 3, 2, 5, 4, 1, 0)
    w_load = pltpu.make_async_copy(w_ref, w_v, w_sem)
    w_load.start()

    def g_load(turn):
        return pltpu.make_async_copy(
            g_ref.at[pl.ds(order[turn] * rows, rows)], g_v.at[turn % 2], g_sem.at[turn % 2]
        )

    g_load(0).start()
    greet([(d_c, s), (d_x, s), (d_y, s)])
    w_load.wait()
    chunk = 512

    def product(turn, dst):
        if turn + 1 < 8:
            g_load(turn + 1).start()
        g_load(turn).wait()

        @pl.loop(0, width // chunk)
        def _(c):
            span = pl.ds(pl.multiple_of(c * chunk, chunk), chunk)
            dst[:, span] = back_product(g_v[turn % 2], w_v[span, :]).astype(BF16)

    def plus(ref, *others):
        total = ref[...].astype(F32)
        for other in others:
            total += other[...].astype(F32)
        ref[...] = total.astype(BF16)

    def crossing(i):
        return remote(leaving.at[i], rcv_c.at[i], sent_c.at[i], got_c.at[i], (d_c, s))

    def pair(turn, i):
        product(turn, leaving.at[i])
        crossing(i).start()
        product(turn + 1, kept.at[i])

    def merge(i):
        crossing(i).wait_recv()
        plus(kept.at[i], rcv_c.at[i])

    low, high = pl.ds(0, rows // 2), pl.ds(rows // 2, rows // 2)

    def pushed(src, dst, n, peer):
        one = remote(src, dst, sent_p.at[n], got_p.at[n], (peer, s))
        one.start()
        return one

    pair(0, 3)
    pair(2, 1)
    merge(3)
    far_x = pushed(kept.at[3, low], rcv_d.at[low], 0, d_x)
    far_y = pushed(kept.at[3, high], rcv_d.at[high], 1, d_y)
    pair(4, 2)
    merge(1)
    x_low = pushed(kept.at[1, low], rcv_x.at[low], 2, d_x)
    pair(6, 0)
    merge(2)
    y_high = pushed(kept.at[2, high], rcv_y.at[high], 3, d_y)
    merge(0)

    tokens = g_ref.shape[0]
    depth, tall = 1024, 512

    def grad_body(x_tile, g_tile, grad_tile):
        k = pl.program_id(1)
        term = outer_sum(x_tile[...], g_tile[...])

        @pl.when(k == 0)
        def _():
            acc[...] = term

        @pl.when(k > 0)
        def _():
            acc[...] += term

        @pl.when(k == tokens // depth - 1)
        def _():
            grad_tile[...] = acc[...].astype(BF16)

    def grad_tiles(first, count):
        pltpu.emit_pipeline(
            grad_body,
            grid=(count, tokens // depth),
            in_specs=[
                pl.BlockSpec((depth, tall), lambda i, k: (k, first + i)),
                pl.BlockSpec((depth, deep), lambda i, k: (k, 0)),
            ],
            out_specs=[pl.BlockSpec((tall, deep), lambda i, k: (first + i, 0))],
        )(x_ref, g_ref, grad_ref)

    grad_tiles(0, 1)
    far_x.wait_recv()
    plus(kept.at[2, low], rcv_d.at[low])
    y_low = pushed(kept.at[2, low], rcv_y.at[low], 4, d_y)
    far_y.wait_recv()
    plus(kept.at[1, high], rcv_d.at[high])
    x_high = pushed(kept.at[1, high], rcv_x.at[high], 5, d_x)
    grad_tiles(1, width // tall - 1)
    x_low.wait_recv()
    y_low.wait_recv()
    x_high.wait_recv()
    y_high.wait_recv()
    plus(kept.at[0], rcv_x, rcv_y)
    out = pltpu.make_async_copy(kept.at[0], out_ref, out_sem)
    out.start()
    for one in [far_x, far_y, x_low, y_high, y_low, x_high] + [crossing(i) for i in range(4)]:
        one.wait_send()
    out.wait()


def plane_sum(g, w, x, rows):
    dma = pltpu.SemaphoreType.DMA
    width, deep = w.shape
    buffer = lambda *lead: pltpu.VMEM((*lead, width), BF16)
    return pl.pallas_call(
        plane_sum_kernel,
        out_shape=[
            jax.ShapeDtypeStruct((rows, width), BF16),
            jax.ShapeDtypeStruct((width, deep), BF16),
        ],
        in_specs=[pl.BlockSpec(memory_space=pl.ANY)] * 3,
        out_specs=[pl.BlockSpec(memory_space=pl.ANY)] * 2,
        scratch_shapes=[
            pltpu.VMEM((width, deep), BF16),
            pltpu.VMEM((2, rows, deep), BF16),
            buffer(4, rows),
            buffer(4, rows),
            buffer(4, rows),
            buffer(rows),
            buffer(rows),
            buffer(rows),
            pltpu.VMEM((512, deep), F32),
            dma,
            dma((2,)),
            dma((4,)),
            dma((4,)),
            dma((6,)),
            dma((6,)),
            dma,
        ],
        compiler_params=pltpu.CompilerParams(
            collective_id=5, has_side_effects=True, vmem_limit_bytes=62 * 2**20
        ),
        name="plane_sum",
    )(g, w, x)


def swap(x, mask, size):
    return lax.ppermute(x, "dp", [(i, i ^ mask) for i in range(size)])


def plane_gather(x, n_dp):
    if n_dp != 8:
        return lax.all_gather(x, "dp", axis=0, tiled=True)
    half = x.shape[0] // 2
    b1, b2, b4 = swap(x, 1, 8), swap(x, 2, 8), swap(x, 4, 8)
    b6 = jnp.concatenate([swap(b4[:half], 2, 8), swap(b2[half:], 4, 8)], axis=0)
    b3, b5, b7 = swap(b2, 1, 8), swap(b4, 1, 8), swap(b6, 1, 8)
    return jnp.concatenate([x, b1, b2, b3, b4, b5, b6, b7], axis=0)


def add(a, b):
    return (a.astype(F32) + b.astype(F32)).astype(BF16)


def plane_scatter(make, rows, n_dp):
    if n_dp != 8:
        return lax.psum_scatter(make(0, n_dp), "dp", scatter_dimension=0, tiled=True).astype(F32)
    half = rows // 2
    kept = {}
    for c in (6, 2, 4, 0):
        part = make(c, c + 2)
        kept[c] = add(part[:rows], swap(part[rows:], 1, 8))
    from_x = swap(kept[6][:half], 2, 8)
    from_y = swap(kept[6][half:], 4, 8)
    x_first = swap(kept[2][:half], 2, 8)
    y_last = swap(kept[4][half:], 4, 8)
    x_last = swap(add(kept[2][half:], from_y), 2, 8)
    y_first = swap(add(kept[4][:half], from_x), 4, 8)
    first = kept[0][:half].astype(F32) + x_first.astype(F32) + y_first.astype(F32)
    last = kept[0][half:].astype(F32) + x_last.astype(F32) + y_last.astype(F32)
    return jnp.concatenate([first, last], axis=0)


def sigmoid(v):
    return 1.0 / (1.0 + jnp.exp(-v))


def gate_up_kernel(x_ref, w_ref, gu_ref, hidden_ref):
    part = hidden_ref.shape[1]
    step = 256 if part % 256 == 0 else 128
    for c in range(0, part, step):
        gate = dot(x_ref[...], w_ref[:, c : c + step])
        up = dot(x_ref[...], w_ref[:, part + c : part + c + step])
        gu_ref[:, c : c + step] = gate.astype(BF16)
        gu_ref[:, part + c : part + c + step] = up.astype(BF16)
        hidden_ref[:, c : c + step] = (gate * sigmoid(gate) * up).astype(BF16)


def gate_up_product(x, w):
    tokens, width = x.shape
    wide = w.shape[1]
    block = 512
    return pl.pallas_call(
        gate_up_kernel,
        grid=(tokens // block,),
        in_specs=[
            pl.BlockSpec((block, width), lambda i: (i, 0)),
            pl.BlockSpec((width, wide), lambda i: (0, 0)),
        ],
        out_specs=[
            pl.BlockSpec((block, wide), lambda i: (i, 0)),
            pl.BlockSpec((block, wide // 2), lambda i: (i, 0)),
        ],
        out_shape=[
            jax.ShapeDtypeStruct((tokens, wide), BF16),
            jax.ShapeDtypeStruct((tokens, wide // 2), BF16),
        ],
        compiler_params=pltpu.CompilerParams(vmem_limit_bytes=56 * 2**20),
        cost_estimate=pl.CostEstimate(
            flops=2 * tokens * width * wide,
            bytes_accessed=2 * (tokens * width + width * wide + tokens * wide * 3 // 2),
            transcendentals=tokens * wide // 2,
        ),
        name="gate_up",
    )(x, w)


def gate_up_back_kernel(g_ref, w_ref, gu_ref, out_ref):
    part = w_ref.shape[0]
    step = 256 if part % 256 == 0 else 128
    for c in range(0, part, step):
        dhidden = back_product(g_ref[...], w_ref[c : c + step, :])
        gate = gu_ref[:, c : c + step].astype(F32)
        up = gu_ref[:, part + c : part + c + step].astype(F32)
        sig = sigmoid(gate)
        rest = dhidden * sig
        out_ref[:, c : c + step] = (rest * up * (1.0 + gate * (1.0 - sig))).astype(BF16)
        out_ref[:, part + c : part + c + step] = (rest * gate).astype(BF16)


def gate_up_back(g, w, gu):
    tokens, width = g.shape
    wide = gu.shape[1]
    block = 512
    return pl.pallas_call(
        gate_up_back_kernel,
        grid=(tokens // block,),
        in_specs=[
            pl.BlockSpec((block, width), lambda i: (i, 0)),
            pl.BlockSpec(w.shape, lambda i: (0, 0)),
            pl.BlockSpec((block, wide), lambda i: (i, 0)),
        ],
        out_specs=pl.BlockSpec((block, wide), lambda i: (i, 0)),
        out_shape=jax.ShapeDtypeStruct((tokens, wide), BF16),
        compiler_params=pltpu.CompilerParams(vmem_limit_bytes=56 * 2**20),
        cost_estimate=pl.CostEstimate(
            flops=tokens * width * wide,
            bytes_accessed=2 * (tokens * width + width * wide // 2 + tokens * wide * 2),
            transcendentals=tokens * wide // 2,
        ),
        name="gate_up_back",
    )(g, w, gu)


def shift(x, by, size):
    pairs = [(i, i + by) for i in range(size) if 0 <= i + by < size]
    return lax.ppermute(x, "seq", pairs)


def mm(a, b):
    return jnp.dot(a, b, preferred_element_type=F32)


def outer_sum(left, right):
    return lax.dot_general(left, right, (((0,), (0,)), ((), ())), preferred_element_type=F32)


def back_product(rows, weight):
    return lax.dot_general(rows, weight, (((1,), (1,)), ((), ())), preferred_element_type=F32)


def gather(x, axes):
    return lax.all_gather(x, axes, axis=0, tiled=True)


def scatter(x, axes):
    return lax.psum_scatter(x, axes, scatter_dimension=0, tiled=True)


def shards(
    tokens, lengths, w_qkv, w_out, w_gate_up, w_down, attn_gain, ffn_gain, head_gains, out_grad
):
    n_dp, n_seq = lax.axis_size("dp"), lax.axis_size("seq")
    rows, length, width = tokens.shape
    count = rows * length
    ff = w_gate_up.shape[1] // 2
    part = ff // n_dp
    wr = w_gate_up.shape[0]
    me = lax.axis_index("seq")
    offset = me * length
    me = me.reshape(1).astype(jnp.int32)
    local_pos = offset + jnp.arange(length, dtype=jnp.int32)
    cosine, sine = rope_tables(jnp.concatenate([local_pos] * rows))
    ends = jnp.cumsum(lengths, axis=1, dtype=jnp.int32)
    start = jnp.sum(
        jnp.where(local_pos[None, :, None] >= ends[:, None, :], lengths[:, None, :], 0), axis=2
    ).reshape(1, count)
    start = jnp.broadcast_to(start, (8, count))

    out_rows = w_out.shape[0]
    gains = jnp.concatenate([attn_gain, ffn_gain, head_gains])
    gains = jnp.pad(gains, (0, width - gains.shape[0]))[None]
    fill = -(out_rows + 1) % 16
    own_rest = jnp.concatenate([w_out, gains, jnp.zeros((fill, width), BF16)], axis=0)
    qkv_w = w_qkv.shape[1]
    paired = w_qkv[:, QW:].reshape(wr, 2, KEY_VALUE_HEADS, HEAD_SIZE).transpose(0, 2, 1, 3)
    own_qkv = jnp.concatenate([w_qkv[:, :QW], paired.reshape(wr, 2 * KW)], axis=1)
    all_qkv, all_rest = gather_weights([own_qkv, own_rest], n_dp, n_seq)
    qkv_full = all_qkv.reshape(width, qkv_w)
    out_full = all_rest[:, :out_rows].reshape(QW, width)
    gains = all_rest[:, out_rows]
    attn_gain_full = gains[:, :wr].reshape(-1).astype(F32)
    ffn_gain_full = gains[:, wr : 2 * wr].reshape(-1).astype(F32)
    head_full = gains[:, 2 * wr : 2 * wr + head_gains.shape[0]].reshape(-1).astype(F32)

    down_w = gather(w_down, "seq")
    w_gate_up, qkv_full = lax.optimization_barrier((w_gate_up, qkv_full))
    spread = lax.all_to_all(w_gate_up.reshape(wr, 2, n_dp, part), "dp", 2, 0, tiled=False)
    spread = spread.reshape(n_dp * wr, 2 * part)
    cotangent_low = out_grad.reshape(count, width)
    cotangent_low, qkv_full = lax.optimization_barrier((cotangent_low, qkv_full))
    cotangent_all = plane_gather(cotangent_low, n_dp)

    x_rows = tokens.reshape(count, width).astype(F32)
    normed, norm_pull = jax.vjp(norm_rows, x_rows, attn_gain_full)
    normed_low = normed.astype(BF16)
    projected = lax.dot_general(
        qkv_full, normed_low, (((0,), (1,)), ((), ())), preferred_element_type=F32
    )

    def prep_local(projected_in, gain_vec):
        return prepare(projected_in, gain_vec, cosine, sine)

    (queries, pairs), prep_pull = jax.vjp(prep_local, projected, head_full)
    queries = queries.astype(BF16)
    pairs = [pairs.astype(BF16)]
    for _ in range(n_seq - 1):
        pairs.append(shift(pairs[-1], 1, n_seq))
    spread, pairs[-1] = lax.optimization_barrier((spread, pairs[-1]))
    gate_up_w = gather(spread, "seq").reshape(n_seq, n_dp, wr, 2 * part)
    gate_up_w = gate_up_w.transpose(1, 0, 2, 3).reshape(width, 2 * part)
    heads_out, lse = attend(me, start, queries, pairs, rows)
    middle = x_rows + outer_sum(heads_out, out_full)
    normed2, norm2_pull = jax.vjp(norm_rows, middle, ffn_gain_full)
    normed2_all = plane_gather_now(normed2.astype(BF16), n_dp, n_seq)
    gate_up, hidden = gate_up_product(normed2_all, gate_up_w)
    down_grad = outer_sum(hidden, cotangent_all).astype(BF16)
    gate_up, down_grad = lax.optimization_barrier((gate_up, down_grad))
    down_grad = scatter(down_grad, "seq")
    dgate_up = gate_up_back(cotangent_all, down_w, gate_up)
    if (n_dp, n_seq) == (8, 4):
        dnormed2, gate_up_grad = plane_sum(dgate_up, gate_up_w, normed2_all, count)
    else:
        dnormed2 = scatter(back_product(dgate_up, gate_up_w).astype(BF16), "dp")
        gate_up_grad = outer_sum(normed2_all, dgate_up).astype(BF16)
    dnormed2 = dnormed2.astype(F32)
    gate_up_grad = gate_up_grad.reshape(n_dp, n_seq, wr, 2 * part).transpose(1, 0, 2, 3)
    gate_up_grad = gate_up_grad.reshape(width, 2 * part)
    gate_up_grad, dnormed2 = lax.optimization_barrier((gate_up_grad, dnormed2))
    gate_up_grad = scatter(gate_up_grad, "seq")
    gate_up_grad = lax.all_to_all(
        gate_up_grad.reshape(n_dp, wr, 2, part), "dp", 0, 2, tiled=False
    ).reshape(wr, 2 * ff)
    hidden, dnormed2 = lax.optimization_barrier((hidden, dnormed2))

    def mixed_part(first, last):
        return mm(hidden[first * count : last * count], down_w).astype(BF16)

    mixed = middle + plane_scatter(mixed_part, count, n_dp)

    dmiddle_norm, ffn_gain_grad = norm2_pull(dnormed2)
    dmiddle = cotangent_low.astype(F32) + dmiddle_norm
    dattend = dmiddle.astype(BF16)
    out_weight_grad = mm(heads_out, dattend).astype(BF16).reshape(n_dp * n_seq, out_rows, width)
    out_weight_grad = jnp.pad(out_weight_grad, ((0, 0), (0, -out_rows % 16), (0, 0)))
    out_weight_grad = sum_weights(out_weight_grad, n_dp, n_seq, 6)[:out_rows]
    dheads = back_product(out_full, dattend).astype(BF16)
    dqueries, *dpairs = attend_back(me, start, queries, pairs, dheads, heads_out, lse, rows)
    dpair = dpairs[-1]
    for back in range(n_seq - 2, -1, -1):
        dpair = dpairs[back].astype(F32) + shift(dpair, -1, n_seq).astype(F32)
        if back:
            dpair = dpair.astype(BF16)
    dprojected, head_grad = prep_pull((dqueries, dpair))
    dprojected_low = dprojected.astype(BF16)
    qkv_grad = lax.dot_general(
        normed_low, dprojected_low, (((0,), (1,)), ((), ())), preferred_element_type=F32
    ).astype(BF16)
    qkv_grad = sum_weights(qkv_grad.reshape(n_dp * n_seq, wr, qkv_w), n_dp, n_seq, 7)
    unpaired = qkv_grad[:, QW:].reshape(wr, KEY_VALUE_HEADS, 2, HEAD_SIZE).transpose(0, 2, 1, 3)
    qkv_grad = jnp.concatenate([qkv_grad[:, :QW], unpaired.reshape(wr, 2 * KW)], axis=1)
    dnormed = lax.dot_general(
        dprojected_low, qkv_full, (((0,), (1,)), ((), ())), preferred_element_type=F32
    )
    dx_norm, attn_gain_grad = norm_pull(dnormed)
    tokens_grad = dmiddle + dx_norm

    n_all = n_dp * n_seq
    small = jnp.concatenate(
        [
            attn_gain_grad.reshape(n_all, -1),
            ffn_gain_grad.reshape(n_all, -1),
            head_grad.reshape(n_all, -1),
        ],
        axis=1,
    )
    small = jnp.sum(lax.all_to_all(small, BOTH, 0, 0, tiled=False), axis=0)
    attn_gain_out = small[:wr]
    ffn_gain_out = small[wr : 2 * wr]
    head_out = small[2 * wr :]
    return (
        mixed.astype(BF16).reshape(rows, length, width),
        tokens_grad.reshape(rows, length, width),
        qkv_grad,
        out_weight_grad,
        gate_up_grad.astype(F32),
        down_grad.astype(F32),
        attn_gain_out,
        ffn_gain_out,
        head_out,
    )


def solution(mesh):
    in_specs = (
        P("dp", "seq", None),
        P("dp", None),
        P(("dp", "seq"), None),
        P(("dp", "seq"), None),
        P(("dp", "seq"), None),
        P(("dp", "seq"), None),
        P(("dp", "seq")),
        P(("dp", "seq")),
        P(("dp", "seq")),
        P("dp", "seq", None),
    )
    out_specs = (
        P("dp", "seq", None),
        P("dp", "seq", None),
        P(("dp", "seq"), None),
        P(("dp", "seq"), None),
        P(("dp", "seq"), None),
        P(("dp", "seq"), None),
        P(("dp", "seq")),
        P(("dp", "seq")),
        P(("dp", "seq")),
    )
    return jax.shard_map(shards, mesh=mesh, in_specs=in_specs, out_specs=out_specs, check_vma=False)
```

```python
import functools

import jax
import jax.numpy as jnp
from jax import lax
from jax.experimental import pallas as pl
from jax.experimental.pallas import tpu as pltpu
from jax.sharding import PartitionSpec as P

QUERY_HEADS = 20
KEY_VALUE_HEADS = 5
HEAD_SIZE = 64
GROUP = QUERY_HEADS // KEY_VALUE_HEADS
QW = QUERY_HEADS * HEAD_SIZE
KW = KEY_VALUE_HEADS * HEAD_SIZE
BOTH = ("dp", "seq")

epsilon = 1e-06
F32 = jnp.float32
BF16 = jnp.bfloat16
MESH = pl.DeviceIdType.MESH


def norm_rows(inputs, scales):
    return inputs * lax.rsqrt(jnp.mean(inputs * inputs, axis=-1, keepdims=True) + epsilon) * scales


def rope_tables(positions):
    inverse_freq = 10000.0 ** (-(jnp.arange(HEAD_SIZE // 2, dtype=F32) * 2.0 / HEAD_SIZE))
    angles = inverse_freq[:, None] * positions.astype(F32)[None, :]
    return (jnp.cos(angles), jnp.sin(angles))


def head_rows(i):
    return pl.ds(pl.multiple_of(i * HEAD_SIZE, HEAD_SIZE), HEAD_SIZE)


def key_rows(i):
    return head_rows(2 * i), head_rows(2 * i + 1)


def unit(v):
    inverse = lax.rsqrt(jnp.mean(v * v, axis=0, keepdims=True) + epsilon)
    return v * inverse, inverse


def prepare_kernel(p_ref, gain_ref, cos_ref, sin_ref, q_ref, kv_ref):
    cosine, sine = cos_ref[...], sin_ref[...]

    def turned(v, gain):
        v = unit(v)[0] * gain
        first, second = v[: HEAD_SIZE // 2], v[HEAD_SIZE // 2 :]
        return jnp.concatenate(
            [first * cosine - second * sine, second * cosine + first * sine], axis=0
        )

    @pl.loop(0, KEY_VALUE_HEADS)
    def _(i):
        key, value = key_rows(i)
        keys_in = p_ref[head_rows(QUERY_HEADS + 2 * i), :]
        kv_ref[key, :] = turned(keys_in, gain_ref[HEAD_SIZE:, :]).astype(BF16)
        kv_ref[value, :] = p_ref[head_rows(QUERY_HEADS + 2 * i + 1), :].astype(BF16)

    @pl.loop(0, QUERY_HEADS)
    def _(i):
        rows = head_rows(i)
        queries = turned(p_ref[rows, :], gain_ref[:HEAD_SIZE, :]) * HEAD_SIZE**-0.5
        q_ref[rows, :] = queries.astype(BF16)


def prepare(projected, gains, cosine, sine):
    tokens = projected.shape[1]
    return pl.pallas_call(
        prepare_kernel,
        out_shape=[
            jax.ShapeDtypeStruct((QW, tokens), BF16),
            jax.ShapeDtypeStruct((2 * KW, tokens), BF16),
        ],
        compiler_params=pltpu.CompilerParams(vmem_limit_bytes=40 * 2**20),
        name="prepare",
    )(projected, gains, cosine, sine)


def prepare_back_kernel(p_ref, gain_ref, cos_ref, sin_ref, dq_ref, dkv_ref, out_ref, dg_ref, acc):
    cosine, sine = cos_ref[...], sin_ref[...]
    acc[...] = jnp.zeros_like(acc)

    def back(v, gain, dy, lines):
        u, inverse = unit(v)
        first, second = dy[: HEAD_SIZE // 2], dy[HEAD_SIZE // 2 :]
        dz = jnp.concatenate(
            [first * cosine + second * sine, second * cosine - first * sine], axis=0
        )
        acc[lines, :] += dz * u
        du = dz * gain
        return inverse * (du - u * jnp.mean(du * u, axis=0, keepdims=True))

    @pl.loop(0, KEY_VALUE_HEADS)
    def _(i):
        key, value = key_rows(i)
        rows = head_rows(QUERY_HEADS + 2 * i)
        dv = back(p_ref[rows, :], gain_ref[HEAD_SIZE:, :], dkv_ref[key, :], slice(HEAD_SIZE, None))
        out_ref[rows, :] = dv.astype(BF16)
        out_ref[head_rows(QUERY_HEADS + 2 * i + 1), :] = dkv_ref[value, :].astype(BF16)

    @pl.loop(0, QUERY_HEADS)
    def _(i):
        rows = head_rows(i)
        dy = dq_ref[rows, :] * HEAD_SIZE**-0.5
        dv = back(p_ref[rows, :], gain_ref[:HEAD_SIZE, :], dy, slice(0, HEAD_SIZE))
        out_ref[rows, :] = dv.astype(BF16)

    rest = out_ref.shape[0] - QW - 2 * KW
    out_ref[QW + 2 * KW :, :] = jnp.zeros((rest, out_ref.shape[1]), BF16)
    total = jnp.sum(acc[...], axis=1, keepdims=True)
    dg_ref[...] = jnp.broadcast_to(total, dg_ref.shape)


def prepare_back(projected, gains, cosine, sine, dqueries, dpairs):
    tokens = projected.shape[1]
    dprojected, dgains = pl.pallas_call(
        prepare_back_kernel,
        out_shape=[
            jax.ShapeDtypeStruct(projected.shape, BF16),
            jax.ShapeDtypeStruct((2 * HEAD_SIZE, 128), F32),
        ],
        scratch_shapes=[pltpu.VMEM((2 * HEAD_SIZE, tokens), F32)],
        compiler_params=pltpu.CompilerParams(vmem_limit_bytes=40 * 2**20),
        name="prepare_back",
    )(projected, gains, cosine, sine, dqueries, dpairs)
    return dprojected, dgains[:, 0]


def dot(a, b):
    return jnp.dot(a, b, preferred_element_type=F32)


def places():
    d, s = lax.axis_index("dp"), lax.axis_index("seq")
    core, column, line = d % 2, (d // 2) % 2, d // 4
    return d, s, d + 1 - 2 * core, d + 2 - 4 * column, d + 4 - 8 * line, line


def greet(peers, line=None):
    barrier = pltpu.get_barrier_semaphore()

    def signal(peer):
        pl.semaphore_signal(barrier, inc=1, device_id=peer, device_id_type=MESH)

    for peer in peers:
        signal(peer)
    if line is None:
        pl.semaphore_wait(barrier, len(peers))
        return
    d, s = line
    last = lax.axis_size("seq") - 1
    pl.when(s < last)(lambda: signal((d, s + 1)))
    pl.when(s > 0)(lambda: signal((d, s - 1)))
    pl.semaphore_wait(barrier, len(peers) + 1 - s // last + (s + last - 1) // last)


def remote(src, dst, sent, got, peer):
    return pltpu.make_async_remote_copy(
        src_ref=src,
        dst_ref=dst,
        send_sem=sent,
        recv_sem=got,
        device_id=peer,
        device_id_type=MESH,
    )


def plane_stages(x_ref, out_ref, own_sem, sent, got, place, ordered=False):
    d, s, d_c, d_x, d_y, line = place
    flip, d_d = d_c - d, d_x + d_y - d
    slots = list(range(8))
    if ordered:
        slots = [d, d_c, d_x, d_x + flip, d_y, d_y + flip, d_d, d_d + flip]
    half = x_ref.shape[0] // 2
    halves = (pl.ds(0, half), pl.ds(half, half))
    source = {1: 0, 2: 0, 4: 0, 3: 2, 5: 4, 7: 6}

    def piece(k, h, peer):
        back = source[k] if k in source else (4 if h == 0 else 2)
        src = x_ref.at[halves[h]] if back == 0 else out_ref.at[slots[back], halves[h]]
        dst = out_ref.at[slots[back] if ordered else k, halves[h]]
        return remote(src, dst, sent.at[k, h], got.at[k, h], (peer, s))

    own = pltpu.make_async_copy(x_ref, out_ref.at[slots[0]], own_sem)

    def begin():
        own.start()
        for h in (0, 1):
            for k, peer in ((2, d_x), (4, d_y), (1, d_c)):
                piece(k, h, peer).start()

    def first():
        piece(4, 0, d_y).wait_recv()
        piece(6, 0, d_x).start()
        piece(5, 0, d_c).start()
        piece(2, 0, d_x).wait_recv()
        piece(3, 0, d_c).start()

    def second():
        piece(2, 1, d_x).wait_recv()
        piece(6, 1, d_y).start()
        piece(3, 1, d_c).start()
        piece(4, 1, d_y).wait_recv()
        piece(5, 1, d_c).start()

    def end():
        for h in (0, 1):
            piece(6, h, d_x).wait_recv()
            piece(7, h, d_c).start()
        for k in (1, 3, 5, 7):
            for h in (0, 1):
                piece(k, h, d_c).wait_recv()
        for k in range(1, 8):
            for h in (0, 1):
                piece(k, h, d_c).wait_send()
        own.wait()

    return begin, first, second, end


def abreast(block):
    return jnp.concatenate(
        [block[i * HEAD_SIZE : (i + 1) * HEAD_SIZE] for i in range(GROUP)], axis=1
    )


def across(rows):
    return jnp.concatenate([rows[i : i + 1] for i in range(GROUP)], axis=1)


def seen(back, me, start):
    length = start.shape[1]
    key = lax.broadcasted_iota(jnp.int32, (length, length), 0)
    found = key + (me - back) * length >= start
    if back == 0:
        found &= key <= lax.broadcasted_iota(jnp.int32, (length, length), 1)
    bias = jnp.where(found, 0.0, -1e30)
    return jnp.concatenate([bias] * GROUP, axis=1)


def spans(i, length):
    row, head = i // KEY_VALUE_HEADS, i % KEY_VALUE_HEADS
    wide, pair = GROUP * HEAD_SIZE, 2 * HEAD_SIZE
    tokens = pl.ds(pl.multiple_of(row * length, length), length)
    return (
        tokens,
        pl.ds(pl.multiple_of(head * wide, wide), wide),
        pl.ds(pl.multiple_of(head * pair, pair), pair),
        head,
    )


def attend_kernel(n, rows, planes, start_ref, q_ref, kv_ref, *refs):
    x_refs, refs = refs[:planes], refs[planes:]
    o_ref, lse_ref, held, *refs = refs
    out_refs, refs = refs[:planes], refs[planes:]
    o_acc, l_acc, sent, got, *refs = refs
    d, me = lax.axis_index("dp"), lax.axis_index("seq")
    length = q_ref.shape[1] // rows
    if planes:
        place = places()
        d, me, d_c, d_x, d_y, _ = place
        greet([(d_c, me), (d_x, me), (d_y, me)], (d, me))
        each = [
            plane_stages(x_refs[i], out_refs[i], *refs[3 * i : 3 * i + 3], place, i > 0)
            for i in range(planes)
        ]
    else:
        greet([], (d, me))
        each = []

    def climb(step, head):
        lines = pl.ds(head * 2 * HEAD_SIZE, 2 * HEAD_SIZE)
        src = kv_ref.at[lines] if step == 1 else held.at[step - 2, lines]
        dst = held.at[step - 1, lines]
        return remote(src, dst, sent.at[step - 1, head], got.at[step - 1, head], (d, me + 1))

    heads = range(KEY_VALUE_HEADS)

    def climbs(step):
        for head in heads:
            climb(step, head).start()

    def level(back):
        @pl.loop(0, rows * KEY_VALUE_HEADS)
        def _(i):
            tokens, wide, pair, head = spans(i, length)
            block = kv_ref[pair, tokens] if back == 0 else held[back - 1, pair, tokens]
            keys, values = block[:HEAD_SIZE].T, block[HEAD_SIZE:]
            bias = seen(back, me, start_ref[0:1, tokens])
            p = jnp.exp(dot(keys, abreast(q_ref[wide, tokens])) + bias)
            total = jnp.sum(p, axis=0, keepdims=True)
            out = dot(values, p.astype(BF16))
            for g in range(GROUP):
                own = slice(g * length, (g + 1) * length)
                line = slice(g, g + 1)
                part = pl.ds(wide.start + g * HEAD_SIZE, HEAD_SIZE)
                if back == 0:
                    l_acc[head, line, tokens] = total[:, own]
                    o_acc[part, tokens] = out[:, own]
                else:
                    l_acc[head, line, tokens] += total[:, own]
                    o_acc[part, tokens] += out[:, own]

    pl.when(me < n - 1)(lambda: climbs(1))
    for stages in each:
        stages[0]()
    level(0)
    for back in range(1, n):

        def step(back=back):
            for head in heads:
                climb(back, head).wait_recv()
                if back < n - 1:
                    pl.when(me < n - 1)(lambda head=head: climb(back + 1, head).start())
            level(back)

        pl.when(me >= back)(step)
        if back <= 2:
            for stages in each:
                stages[back]()

    @pl.loop(0, rows * KEY_VALUE_HEADS)
    def _(i):
        tokens, wide, pair, head = spans(i, length)
        for g in range(GROUP):
            line = slice(g, g + 1)
            part = pl.ds(wide.start + g * HEAD_SIZE, HEAD_SIZE)
            o_ref[part, tokens] = (o_acc[part, tokens] / l_acc[head, line, tokens]).astype(BF16)
            lse_ref[head, line, tokens] = jnp.log(l_acc[head, line, tokens])

    for back in range(1, n):
        for head in heads:
            pl.when((me >= back - 1) & (me < n - 1))(
                lambda back=back, head=head: climb(back, head).wait_send()
            )
    for stages in each:
        stages[3]()


def attend(start, queries, pairs, rows, n, more):
    vmem, dma = pl.BlockSpec(memory_space=pltpu.VMEM), pltpu.SemaphoreType.DMA
    anywhere = pl.BlockSpec(memory_space=pl.ANY)
    count = queries.shape[1]
    lines = (KEY_VALUE_HEADS, 8, count)
    out_shape = [
        jax.ShapeDtypeStruct(queries.shape, BF16),
        jax.ShapeDtypeStruct(lines, F32),
        jax.ShapeDtypeStruct((n - 1, *pairs.shape), BF16),
    ]
    scratch = [
        pltpu.VMEM(queries.shape, F32),
        pltpu.VMEM(lines, F32),
        dma((n - 1, KEY_VALUE_HEADS)),
        dma((n - 1, KEY_VALUE_HEADS)),
    ]
    for extra in more:
        out_shape.append(jax.ShapeDtypeStruct((8, *extra.shape), BF16))
        scratch += [dma, dma((8, 2)), dma((8, 2))]
    return pl.pallas_call(
        functools.partial(attend_kernel, n, rows, len(more)),
        in_specs=[vmem] * 3 + [anywhere] * len(more),
        out_specs=[vmem] * 3 + [anywhere] * len(more),
        out_shape=out_shape,
        scratch_shapes=scratch,
        compiler_params=pltpu.CompilerParams(
            collective_id=2, has_side_effects=True, vmem_limit_bytes=40 * 2**20
        ),
        name="attend",
    )(start, queries, pairs, *more)


def plus(ref, *others):
    total = ref[...].astype(F32)
    for other in others:
        total += other[...].astype(F32)
    ref[...] = total.astype(BF16)


def attend_back_kernel(n, rows, summed, *refs):
    start_ref, q_ref, do_ref, o_ref, lse_ref, kv_ref, held, *refs = refs
    if summed:
        h_ref, w_ref, *refs = refs
    dq_ref, dkv_ref, *refs = refs
    if summed:
        mixed_ref, *refs = refs
    inner, part, rcv, sent, got, *refs = refs
    d, me = lax.axis_index("dp"), lax.axis_index("seq")
    length = q_ref.shape[1] // rows
    if summed:
        place = places()
        d, me, d_c, d_x, d_y, _ = place
        w_v, h_v, w_sem, h_sem, *refs = refs
        kept, leaving = refs[:2]
        load, product = block_products(h_ref, h_v, h_sem, lambda h, span: dot(h, w_v[:, span]))
        load(0).start()
        w_load = pltpu.make_async_copy(w_ref, w_v, w_sem)
        w_load.start()
        greet([(d_c, me), (d_x, me), (d_y, me)], (d, me))
        crossing, far, near, pass_on, end = plane_sums(*refs, place)

        def pair(turn, i):
            slot = turn // 2 % 2
            if turn >= 4:
                crossing(3 if slot == 0 else 1, slot).wait_send()
            product(turn, leaving.at[slot])
            crossing(i, slot).start()
            product(turn + 1, kept.at[i])

        def stage(i):
            if i == 0:
                w_load.wait()
                pair(0, 3)
                far()
                pair(2, 1)
            elif i == 1:
                near(1)
                pair(4, 2)
                pair(6, 0)
                near(2)
                near(0)
            elif i == 2:
                pass_on()
            else:
                end()
                mixed_ref[...] = kept[0]
                crossing(2, 0).wait_send()
                crossing(0, 1).wait_send()
    else:
        greet([], (d, me))

        def stage(i):
            pass

    def descend(back):
        return remote(
            part.at[back - 1], rcv.at[back - 1], sent.at[back - 1], got.at[back - 1], (d, me - 1)
        )

    def level(back):
        @pl.loop(0, rows * KEY_VALUE_HEADS)
        def _(i):
            tokens, wide, pair, head = spans(i, length)
            block = kv_ref[pair, tokens] if back == 0 else held[back - 1, pair, tokens]
            keys_t = block[:HEAD_SIZE]
            keys, values = keys_t.T, block[HEAD_SIZE:].T
            q, do = abreast(q_ref[wide, tokens]), abreast(do_ref[wide, tokens])
            bias = seen(back, me, start_ref[0:1, tokens])
            p = jnp.exp(dot(keys, q) + (bias - across(lse_ref[head, :, tokens])))
            ds = (p * (dot(values, do) - across(inner[head, :, tokens]))).astype(BF16)
            dv = back_product(p.astype(BF16), do)
            dk = back_product(ds, q)
            dq = dot(keys_t, ds)
            if back == 0:
                dkv_ref[pair, tokens] = jnp.concatenate([dk.T, dv.T], axis=0)
            else:
                part[back - 1, pair, tokens] = jnp.concatenate([dk.T, dv.T], axis=0).astype(BF16)
            for g in range(GROUP):
                own = slice(g * length, (g + 1) * length)
                line = pl.ds(wide.start + g * HEAD_SIZE, HEAD_SIZE)
                dq_ref[line, tokens] += dq[:, own]

    def finish(back):
        def more():
            descend(back + 1).wait_recv()
            if back == 0:
                dkv_ref[...] += rcv[0].astype(F32)
            else:
                plus(part.at[back - 1], rcv.at[back])

        if back < n - 1:
            pl.when(me < n - 1)(more)
        if back > 0:
            descend(back).start()

    stage(0)
    dq_ref[...] = jnp.zeros_like(dq_ref)

    @pl.loop(0, rows * KEY_VALUE_HEADS)
    def _(i):
        tokens, wide, pair, head = spans(i, length)
        for g in range(GROUP):
            line = slice(g, g + 1)
            own = pl.ds(wide.start + g * HEAD_SIZE, HEAD_SIZE)
            product = do_ref[own, tokens].astype(F32) * o_ref[own, tokens].astype(F32)
            inner[head, line, tokens] = jnp.sum(product, axis=0, keepdims=True)

    for back in range(n - 1, -1, -1):

        def run(back=back):
            level(back)
            pl.when(me == n - 1)(lambda: finish(back))

        if back:
            pl.when(me >= back)(run)
        else:
            level(0)
            pl.when(me == n - 1)(lambda: finish(0))
        if back + 1 < n - 1:
            pl.when((me >= back + 1) & (me < n - 1))(lambda back=back: finish(back + 1))
        if n - 1 - back in (1, 2):
            stage(n - 1 - back)
    pl.when(me < n - 1)(lambda: finish(0))
    stage(3)
    for back in range(1, n):
        pl.when(me >= back)(lambda back=back: descend(back).wait_send())


def attend_back(start, queries, dheads, heads, lse, pairs, held, rows, n, more):
    vmem, dma = pl.BlockSpec(memory_space=pltpu.VMEM), pltpu.SemaphoreType.DMA
    anywhere = pl.BlockSpec(memory_space=pl.ANY)
    count = queries.shape[1]
    out_shape = [
        jax.ShapeDtypeStruct(queries.shape, F32),
        jax.ShapeDtypeStruct(pairs.shape, F32),
    ]
    scratch = [
        pltpu.VMEM((KEY_VALUE_HEADS, 8, count), F32),
        pltpu.VMEM((n - 1, *pairs.shape), BF16),
        pltpu.VMEM((n - 1, *pairs.shape), BF16),
        dma((n - 1,)),
        dma((n - 1,)),
    ]
    if more:
        (tokens, deep), (_, width) = more[0].shape, more[1].shape
        block = tokens // 8
        out_shape.append(jax.ShapeDtypeStruct((block, width), BF16))
        scratch += [
            pltpu.VMEM((deep, width), BF16),
            pltpu.VMEM((2, block, deep), BF16),
            dma,
            dma((2,)),
            *sums_scratch(block, width),
        ]
    return pl.pallas_call(
        functools.partial(attend_back_kernel, n, rows, bool(more)),
        in_specs=[vmem] * 7 + [anywhere] * len(more),
        out_specs=[vmem] * len(out_shape),
        out_shape=out_shape,
        scratch_shapes=scratch,
        compiler_params=pltpu.CompilerParams(
            collective_id=3, has_side_effects=True, vmem_limit_bytes=62 * 2**20
        ),
        name="attend_back",
    )(start, queries, dheads, heads, lse, pairs, held, *more)


def weights_kernel(n, *refs):
    x_refs, (w_ref, *out_refs), refs = refs[:n], refs[n : 2 * n + 1], refs[2 * n + 1 :]
    spread_ref, own_sem, recv, send_z, send_x, send_y, send_d, send_c, own_w, sent_w, got_w = refs
    d, s, d_c, d_x, d_y, line = places()
    d_d = d_x + 4 - 8 * line
    flip = d_c - d
    plane = (d, d_c, d_x, d_x + flip, d_y, d_y + flip, d_d, d_d + flip)
    greet([(other, s) for other in plane[1:]], (d, s))
    part = spread_ref.shape[2] // 2

    def columns(k, half):
        begin = half * 8 * part + plane[k] * part
        src = w_ref.at[:, pl.ds(pl.multiple_of(begin, 128), part)]
        dst = spread_ref.at[d, :, pl.ds(half * part, part)]
        if k == 0:
            return pltpu.make_async_copy(src, dst, own_w.at[half])
        return remote(src, dst, sent_w.at[k, half], got_w.at[k, half], (plane[k], s))

    def copies(slot, sent, got, peer, own=False, many=1):
        return [
            remote(
                x_refs[i] if own else out_refs[i].at[slot if i == 0 else slot % 4],
                out_refs[i].at[slot if i == 0 else slot % 4],
                sent(i),
                got(i),
                peer,
            )
            for i in range(many)
        ]

    def start(group):
        for one in group:
            one.start()

    def sent(group):
        for one in group:
            one.wait_send()

    def each(visit, between=lambda: None):
        visit(s, 0)
        between()
        for far in (1, 2, 3):
            pl.when(s >= far)(lambda far=far: visit(s - far, 1))
            pl.when(s + far <= 3)(lambda far=far: visit(s + far, -1))

    def got(k, b):
        return lambda i: recv.at[i, k, b]

    def arrived(k, b):
        many = 1 if k else n
        for one in copies(d * 4 + b, lambda i: send_x.at[i, b], got(k, b), (d_x, s), many=many):
            one.wait_recv()

    own = [
        pltpu.make_async_copy(x_refs[i], out_refs[i].at[d * 4 + s if i == 0 else s], own_sem.at[i])
        for i in range(n)
    ]
    start(own)

    def up(b, own=False):
        return copies(d * 4 + b, lambda i: send_z.at[i, 0, b], got(0, b), (d, s + 1), own, n)

    def down(b, own=False):
        return copies(d * 4 + b, lambda i: send_z.at[i, 1, b], got(0, b), (d, s - 1), own, n)

    def spread(b, own=False):
        return (
            copies(d * 4 + b, lambda i: send_x.at[i, b], got(2, b), (d_x, s), own)
            + copies(d * 4 + b, lambda i: send_y.at[i, b], got(4, b), (d_y, s), own)
            + copies(d * 4 + b, lambda i: send_c.at[i, 0, b], got(1, b), (d_c, s), own)
        )

    def column_block(b, direction):
        own = direction == 0
        if direction:
            arrived(0, b)
        if direction >= 0:
            pl.when(s < 3)(lambda: start(up(b, own)))
        if direction <= 0:
            pl.when(s > 0)(lambda: start(down(b, own)))
        start(spread(b, own))

    def start_columns():
        for k in range(8):
            for half in (0, 1):
                columns(k, half).start()

    each(column_block, start_columns)

    def over_y(b):
        return copies(d_x * 4 + b, lambda i: send_d.at[i, b], got(6, b), (d_y, s))

    def over_x(b):
        return copies(d_y * 4 + b, lambda i: send_d.at[i, b], got(6, b), (d_x, s))

    def to_core(index, holder, b):
        return copies(
            holder * 4 + b, lambda i: send_c.at[i, index, b], got(2 * index + 1, b), (d_c, s)
        )

    def side_blocks(b, direction):
        arrived(2, b)
        pl.when(b % 2 == 0)(lambda: start(over_y(b)))
        start(to_core(1, d_x, b))
        arrived(4, b)
        pl.when(b % 2 == 1)(lambda: start(over_x(b)))
        start(to_core(2, d_y, b))

    each(side_blocks)

    def far_block(b, direction):
        arrived(6, b)
        start(to_core(3, d_d, b))

    each(far_block)

    def finish(b, direction):
        for k in (1, 3, 5, 7):
            arrived(k, b)
        if direction >= 0:
            pl.when(s < 3)(lambda: sent(up(b)))
        if direction <= 0:
            pl.when(s > 0)(lambda: sent(down(b)))
        sent(spread(b))
        sent(over_y(b))
        sent(to_core(1, d_x, b))
        sent(to_core(2, d_y, b))
        sent(to_core(3, d_d, b))

    each(finish)
    for one in own:
        one.wait()
    for k in range(8):
        for half in (0, 1):
            if k:
                columns(k, half).wait_recv()
                columns(k, half).wait_send()
            else:
                columns(k, half).wait()


def gather_weights(first, others, wide, n_dp, n_seq):
    rows, part = wide.shape[0], wide.shape[1] // (2 * n_dp)
    if (n_dp, n_seq) != (8, 4):
        spread = lax.all_to_all(wide.reshape(rows, 2, n_dp, part), "dp", 2, 0, tiled=False)
        spread = spread.reshape(n_dp, rows, 2 * part)
        return [lax.all_gather(x, BOTH, axis=0, tiled=False) for x in (first, *others)] + [spread]
    arrays = [first, *others]
    n = len(arrays)
    dma = pltpu.SemaphoreType.DMA
    return pl.pallas_call(
        functools.partial(weights_kernel, n),
        out_shape=[
            jax.ShapeDtypeStruct((n_seq if i else n_dp * n_seq, *x.shape), x.dtype)
            for i, x in enumerate(arrays)
        ]
        + [jax.ShapeDtypeStruct((n_dp, rows, 2 * part), wide.dtype)],
        in_specs=[pl.BlockSpec(memory_space=pl.ANY)] * (n + 1),
        out_specs=[pl.BlockSpec(memory_space=pl.ANY)] * (n + 1),
        scratch_shapes=[
            dma((n,)),
            dma((n, 8, 4)),
            dma((n, 2, 4)),
            dma((n, 4)),
            dma((n, 4)),
            dma((n, 4)),
            dma((n, 4, 4)),
            dma((2,)),
            dma((8, 2)),
            dma((8, 2)),
        ],
        compiler_params=pltpu.CompilerParams(collective_id=1, has_side_effects=True),
        name="gather_weights",
    )(*arrays, wide)


def weight_sums(g_ref, out_ref, refs, place):
    kept, rcv_c, rcv_d, rcv_x, rcv_y, rcv_z, load, sent_c, got_c, sent_p, got_p, sent_z, got_z = refs
    d, s, d_c, d_x, d_y, line = place
    holders = (d, d_x, d_y, d_x + d_y - d)
    flip = d_c - d
    low, high = pl.ds(0, 2), pl.ds(2, 2)

    def crossing(i):
        src = g_ref.at[pl.ds((holders[i] + flip) * 4, 4)]
        return remote(src, rcv_c.at[i], sent_c.at[i], got_c.at[i], (d_c, s))

    def loading(i):
        return pltpu.make_async_copy(
            g_ref.at[pl.ds(holders[i] * 4, 4)], kept.at[i], load.at[i]
        )

    def merge(i):
        loading(i).wait()
        crossing(i).wait_recv()
        plus(kept.at[i], rcv_c.at[i])

    def push(i):
        src, dst, peer = (
            (kept.at[3, low], rcv_d.at[low], d_x),
            (kept.at[3, high], rcv_d.at[high], d_y),
            (kept.at[1, low], rcv_x.at[low], d_x),
            (kept.at[2, high], rcv_y.at[high], d_y),
            (kept.at[2, low], rcv_y.at[low], d_y),
            (kept.at[1, high], rcv_x.at[high], d_x),
        )[i]
        return remote(src, dst, sent_p.at[i], got_p.at[i], (peer, s))

    def up(b):
        return remote(
            kept.at[0, b], rcv_z.at[0, b], sent_z.at[0, b], got_z.at[0, b], (d, s + 1)
        )

    def down(b):
        return remote(
            kept.at[0, b], rcv_z.at[1, b], sent_z.at[1, b], got_z.at[1, b], (d, s - 1)
        )

    def begin():
        for i in (3, 1, 2, 0):
            crossing(i).start()
            loading(i).start()

    def far():
        merge(3)
        push(0).start()
        push(1).start()

    def near():
        merge(1)
        push(2).start()
        merge(2)
        push(3).start()
        merge(0)

    def pass_on():
        push(0).wait_recv()
        plus(kept.at[2, low], rcv_d.at[low])
        push(4).start()
        push(1).wait_recv()
        plus(kept.at[1, high], rcv_d.at[high])
        push(5).start()

    def send_up(b):
        @pl.when(s > 0)
        def _():
            up(b).wait_recv()
            plus(kept.at[0, b], rcv_z.at[0, b])

        up(b).start()

    def send_down(b):
        @pl.when(s < 3)
        def _():
            down(b).wait_recv()
            plus(kept.at[0, b], rcv_z.at[1, b])

        down(b).start()

    def along():
        for i in (2, 3, 4, 5):
            push(i).wait_recv()
        plus(kept.at[0], rcv_x, rcv_y)
        for b in (3, 2, 1):
            pl.when(s < b)(functools.partial(send_up, b))
            pl.when(s > 3 - b)(functools.partial(send_down, 3 - b))

    def end():
        out_ref[...] = kept[0, s].astype(F32)

        @pl.when(s > 0)
        def _():
            up(s).wait_recv()
            out_ref[...] += rcv_z[0, s].astype(F32)

        @pl.when(s < 3)
        def _():
            down(s).wait_recv()
            out_ref[...] += rcv_z[1, s].astype(F32)

        for b in (3, 2, 1):
            pl.when(s < b)(lambda: up(b).wait_send())
            pl.when(s > 3 - b)(lambda: down(3 - b).wait_send())
        for i in range(4):
            crossing(i).wait_send()
        for i in range(6):
            push(i).wait_send()

    return begin, far, near, pass_on, along, end


def weight_sums_scratch(rows, columns):
    dma = pltpu.SemaphoreType.DMA
    buffer = lambda *lead: pltpu.VMEM((*lead, rows, columns), BF16)
    return [
        buffer(4, 4),
        buffer(4, 4),
        buffer(4),
        buffer(4),
        buffer(4),
        buffer(2, 4),
        dma((4,)),
        dma((4,)),
        dma((4,)),
        dma((6,)),
        dma((6,)),
        dma((2, 4)),
        dma((2, 4)),
    ]


def normed_back(dy, x, gain):
    inverse = lax.rsqrt(jnp.mean(x * x, axis=1, keepdims=True) + epsilon)
    gy = dy * gain
    x = x * inverse
    return inverse * (gy - x * jnp.mean(gy * x, axis=1, keepdims=True))


def sum_weights_kernel(n, *refs):
    g_refs, refs = refs[:n], refs[n:]
    p_ref, w_ref, x_ref, dm_ref, gain_ref, back_ref, wide_ref, *refs = refs
    out_refs, (dx_ref, wide_out, dg_ref), refs = refs[:n], refs[n : n + 3], refs[n + 3 :]
    p_v, w_v, p_sem, w_sem, *refs = refs
    w_load = pltpu.make_async_copy(w_ref, w_v, w_sem)
    p_load = pltpu.make_async_copy(p_ref, p_v, p_sem)
    w_load.start()
    p_load.start()
    place = places()
    d, s, d_c, d_x, d_y, line = place
    greet([(d_c, s), (d_x, s), (d_y, s)], (d, s))
    each = [
        weight_sums(g_refs[i], out_refs[i], refs[13 * i : 13 * i + 13], place) for i in range(n)
    ]
    block = 128

    def body(x_tile, dm_tile, dx_tile):
        i = pl.program_id(0) + offset
        span = pl.ds(pl.multiple_of(i * block, block), block)
        dy = back_product(p_v[:, span].T, w_v[...])
        dx_tile[...] = dm_tile[...] + normed_back(dy, x_tile[...].astype(F32), gain_ref[...])

    count = x_ref.shape[0] // block
    half = count // 2
    spec = lambda: pl.BlockSpec((block, x_ref.shape[1]), lambda i: (i + offset, 0))
    for i in range(6):
        for stages in each:
            stages[i]()
        if i == 0:
            w_load.wait()
            p_load.wait()
        if i in (1, 2):
            offset = (i - 1) * half
            pltpu.emit_pipeline(
                body, grid=(half,), in_specs=[spec(), spec()], out_specs=[spec()]
            )(x_ref, dm_ref, dx_ref)
        if i == 3:
            part = back_ref.shape[2] // 2
            total = jnp.zeros((dg_ref.shape[0], 1), F32)
            for j in range(16):
                half_j, holder = j // 8, j % 8
                span = slice(j * part, (j + 1) * part)
                grad = back_ref[holder, :, half_j * part : (half_j + 1) * part].astype(F32)
                wide_out[:, span] = grad
                total += jnp.sum(grad * wide_ref[:, span].astype(F32), axis=1, keepdims=True)
            dg_ref[...] = jnp.broadcast_to(total, dg_ref.shape)


def sum_weights(arrays, dprojected, w, x, dmiddle, gain, back, wide):
    dma, anywhere = pltpu.SemaphoreType.DMA, pl.BlockSpec(memory_space=pl.ANY)
    vmem = pl.BlockSpec(memory_space=pltpu.VMEM)
    n = len(arrays)
    scratch = [pltpu.VMEM(dprojected.shape, BF16), pltpu.VMEM(w.shape, BF16), dma, dma]
    for g in arrays:
        scratch += weight_sums_scratch(*g.shape[1:])
    return pl.pallas_call(
        functools.partial(sum_weights_kernel, n),
        out_shape=[jax.ShapeDtypeStruct(g.shape[1:], F32) for g in arrays]
        + [
            jax.ShapeDtypeStruct(dmiddle.shape, F32),
            jax.ShapeDtypeStruct(wide.shape, F32),
            jax.ShapeDtypeStruct((wide.shape[0], 128), F32),
        ],
        in_specs=[anywhere] * (n + 4) + [vmem] * 3,
        out_specs=[vmem] * n + [anywhere, vmem, vmem],
        scratch_shapes=scratch,
        compiler_params=pltpu.CompilerParams(
            collective_id=6, has_side_effects=True, vmem_limit_bytes=60 * 2**20
        ),
        name="sum_weights",
    )(*arrays, dprojected, w, x, dmiddle, gain, back, wide)


def plane_kernel(x_ref, g_ref, w_ref, out_ref, dh_ref, w_v, w_sem, own_sem, sent, got):
    place = places()
    d, s, d_c, d_x, d_y, line = place
    load = pltpu.make_async_copy(w_ref, w_v, w_sem)
    load.start()
    greet([(d_c, s), (d_x, s), (d_y, s)])
    begin, first, second, end = plane_stages(x_ref, out_ref, own_sem, sent, got, place)
    begin()
    load.wait()

    def body(g_tile, dh_tile):
        dh_tile[...] = back_product(g_tile[...], w_v[...]).astype(BF16)

    def some(start, count):
        pltpu.emit_pipeline(
            body,
            grid=(count,),
            in_specs=[pl.BlockSpec((512, w_v.shape[1]), lambda i: (start + i, 0))],
            out_specs=[pl.BlockSpec((512, w_v.shape[0]), lambda i: (start + i, 0))],
        )(g_ref, dh_ref)

    blocks = g_ref.shape[0] // 512
    some(0, blocks)
    first()
    second()
    end()


def plane_gather_now(x, g, w, n_dp, n_seq):
    if (n_dp, n_seq) != (8, 4):
        everyone = lax.all_gather(x, "dp", axis=0, tiled=True)
        return everyone, back_product(g, w).astype(BF16)
    dma, anywhere = pltpu.SemaphoreType.DMA, pl.BlockSpec(memory_space=pl.ANY)
    everyone, dhidden = pl.pallas_call(
        plane_kernel,
        out_shape=[
            jax.ShapeDtypeStruct((n_dp, *x.shape), x.dtype),
            jax.ShapeDtypeStruct((g.shape[0], w.shape[0]), BF16),
        ],
        in_specs=[anywhere] * 3,
        out_specs=[anywhere] * 2,
        scratch_shapes=[pltpu.VMEM(w.shape, BF16), dma, dma, dma((8, 2)), dma((8, 2))],
        compiler_params=pltpu.CompilerParams(
            collective_id=4, has_side_effects=True, vmem_limit_bytes=40 * 2**20
        ),
        name="plane_gather",
    )(x, g, w)
    return everyone.reshape(n_dp * x.shape[0], x.shape[1]), dhidden


def transposed_kernel(x_ref, g_ref, out_ref):
    n_seq, n_dp, rows, _ = out_ref.shape
    total = outer_sum(x_ref[...], g_ref[...])
    for i in range(n_dp * n_seq):
        out_ref[i % n_seq, i // n_seq] = total[i * rows : (i + 1) * rows].astype(BF16)


def transposed_product(x, g, n_dp, n_seq):
    (tokens, width), wide = x.shape, g.shape[1]
    rows, tall = width // (n_dp * n_seq), 512
    return pl.pallas_call(
        transposed_kernel,
        grid=(width // tall,),
        in_specs=[
            pl.BlockSpec((tokens, tall), lambda i: (0, i)),
            pl.BlockSpec((tokens, wide), lambda i: (0, 0)),
        ],
        out_specs=pl.BlockSpec(
            (n_seq, tall // (n_seq * rows), rows, wide), lambda i: (0, i, 0, 0)
        ),
        out_shape=jax.ShapeDtypeStruct((n_seq, n_dp, rows, wide), BF16),
        compiler_params=pltpu.CompilerParams(vmem_limit_bytes=60 * 2**20),
        cost_estimate=pl.CostEstimate(
            flops=2 * tokens * width * wide,
            bytes_accessed=2 * (tokens * width + tokens * wide + width * wide),
            transcendentals=0,
        ),
        name="transposed_product",
    )(x, g)


def plane_sums(kept, leaving, rcv_c, rcv_d, rcv_x, rcv_y, sent_c, got_c, sent_p, got_p, place):
    d, s, d_c, d_x, d_y, line = place
    rows = kept.shape[1]
    low, high = pl.ds(0, rows // 2), pl.ds(rows // 2, rows // 2)

    def crossing(i, slot):
        return remote(leaving.at[slot], rcv_c.at[i], sent_c.at[i], got_c.at[i], (d_c, s))

    def merge(i):
        crossing(i, 0).wait_recv()
        plus(kept.at[i], rcv_c.at[i])

    def push(i):
        src, dst, peer = (
            (kept.at[3, low], rcv_d.at[low], d_x),
            (kept.at[3, high], rcv_d.at[high], d_y),
            (kept.at[1, low], rcv_x.at[low], d_x),
            (kept.at[2, high], rcv_y.at[high], d_y),
            (kept.at[2, low], rcv_y.at[low], d_y),
            (kept.at[1, high], rcv_x.at[high], d_x),
        )[i]
        return remote(src, dst, sent_p.at[i], got_p.at[i], (peer, s))

    def far():
        merge(3)
        push(0).start()
        push(1).start()

    def near(i):
        merge(i)
        if i:
            push(i + 1).start()

    def pass_on():
        push(0).wait_recv()
        plus(kept.at[2, low], rcv_d.at[low])
        push(4).start()
        push(1).wait_recv()
        plus(kept.at[1, high], rcv_d.at[high])
        push(5).start()

    def end():
        for i in (2, 3, 4, 5):
            push(i).wait_recv()
        plus(kept.at[0], rcv_x, rcv_y)
        for i in range(6):
            push(i).wait_send()

    return crossing, far, near, pass_on, end


def sums_scratch(rows, width):
    dma = pltpu.SemaphoreType.DMA
    buffer = lambda *lead: pltpu.VMEM((*lead, rows, width), BF16)
    return [
        buffer(4),
        buffer(2),
        buffer(4),
        buffer(),
        buffer(),
        buffer(),
        dma((4,)),
        dma((4,)),
        dma((6,)),
        dma((6,)),
    ]


ORDER = (7, 6, 3, 2, 5, 4, 1, 0)


def block_products(g_ref, g_v, g_sem, multiply):
    rows = g_v.shape[1]

    def load(turn):
        block = pl.ds(ORDER[turn] * rows, rows)
        return pltpu.make_async_copy(g_ref.at[block], g_v.at[turn % 2], g_sem.at[turn % 2])

    def product(turn, dst):
        if turn + 1 < 8:
            load(turn + 1).start()
        load(turn).wait()
        chunk = 512

        @pl.loop(0, dst.shape[1] // chunk)
        def _(c):
            span = pl.ds(pl.multiple_of(c * chunk, chunk), chunk)
            dst[:, span] = multiply(g_v[turn % 2], span).astype(BF16)

    return load, product


def plane_sum_kernel(g_ref, w_ref, h_ref, t_ref, out_ref, grad_ref, w_v, g_v, h_v, *refs):
    w_sem, g_sem, h_sem, out_sem, *refs = refs
    place = places()
    d, s, d_c, d_x, d_y, line = place
    kept, leaving = refs[:2]
    w_wait = load_rows(w_ref, w_v, w_sem, 8, 4)
    load, product = block_products(
        g_ref, g_v, g_sem, lambda g, span: back_product(g, w_v[span, :])
    )
    load(0).start()
    h_load = pltpu.make_async_copy(h_ref, h_v, h_sem)
    h_load.start()
    greet([(d_c, s), (d_x, s), (d_y, s)])
    crossing, far, near, pass_on, end = plane_sums(*refs, place)
    w_wait()

    def pair(turn, i):
        slot = turn // 2 % 2
        if turn >= 4:
            crossing(3 if slot == 0 else 1, slot).wait_send()
        product(turn, leaving.at[slot])
        crossing(i, slot).start()
        product(turn + 1, kept.at[i])

    pair(0, 3)
    far()
    pair(2, 1)
    pair(4, 2)
    near(1)
    pair(6, 0)
    near(2)
    near(0)
    h_load.wait()

    def grad_body(t_tile, grad_tile):
        grad_tile[...] = outer_sum(h_v[...], t_tile[...]).astype(BF16)

    tokens, deep = h_v.shape
    wide = 256

    def grad_tiles(first, count):
        pltpu.emit_pipeline(
            grad_body,
            grid=(count,),
            in_specs=[pl.BlockSpec((tokens, wide), lambda i: (0, first + i))],
            out_specs=[pl.BlockSpec((deep, wide), lambda i: (0, first + i))],
        )(t_ref, grad_ref)

    grad_tiles(0, 2)
    pass_on()
    grad_tiles(2, t_ref.shape[1] // wide - 2)
    end()
    out = pltpu.make_async_copy(kept.at[0], out_ref, out_sem)
    out.start()
    crossing(2, 0).wait_send()
    crossing(0, 1).wait_send()
    out.wait()


def plane_sum(g, w, h, t, rows):
    dma, anywhere = pltpu.SemaphoreType.DMA, pl.BlockSpec(memory_space=pl.ANY)
    width, deep = w.shape
    return pl.pallas_call(
        plane_sum_kernel,
        out_shape=[
            jax.ShapeDtypeStruct((rows, width), BF16),
            jax.ShapeDtypeStruct((h.shape[1], t.shape[1]), BF16),
        ],
        in_specs=[anywhere] * 4,
        out_specs=[anywhere] * 2,
        scratch_shapes=[
            pltpu.VMEM((width, deep), BF16),
            pltpu.VMEM((2, rows, deep), BF16),
            pltpu.VMEM(h.shape, BF16),
            dma,
            dma((2,)),
            dma,
            dma,
            *sums_scratch(rows, width),
        ],
        compiler_params=pltpu.CompilerParams(
            collective_id=5, has_side_effects=True, vmem_limit_bytes=62 * 2**20
        ),
        name="plane_sum",
    )(g, w, h, t)


def sigmoid(v):
    return 1.0 / (1.0 + jnp.exp(-v))


def load_rows(w_ref, w_v, sem, n_dp, n_seq):
    rows = w_v.shape[0] // (n_dp * n_seq)

    @pl.loop(0, n_dp * n_seq)
    def _(i):
        src = pl.ds(pl.multiple_of(i * rows, rows), rows)
        place = (i % n_dp) * n_seq + i // n_dp
        dst = pl.ds(pl.multiple_of(place * rows, rows), rows)
        pltpu.make_async_copy(w_ref.at[src], w_v.at[dst], sem).start()

    return pltpu.make_async_copy(w_ref, w_v, sem).wait


def gate_up_kernel(n_dp, n_seq, x_ref, dh_ref, w_ref, hidden_ref, dgu_ref, w_v, sem):
    pl.when(pl.program_id(0) == 0)(lambda: load_rows(w_ref, w_v, sem, n_dp, n_seq)())
    part = hidden_ref.shape[1]
    step = 256 if part % 256 == 0 else 128
    for c in range(0, part, step):
        first, second = slice(c, c + step), slice(part + c, part + c + step)
        gate, up = dot(x_ref[...], w_v[:, first]), dot(x_ref[...], w_v[:, second])
        dhidden = dh_ref[:, first].astype(F32)
        sig = sigmoid(gate)
        silu = gate * sig
        hidden_ref[:, first] = (silu * up).astype(BF16)
        dgu_ref[:, first] = (dhidden * up * (sig + silu * (1.0 - sig))).astype(BF16)
        dgu_ref[:, second] = (dhidden * silu).astype(BF16)


def gate_up_product(x, dhidden, w, n_dp, n_seq):
    tokens, width = x.shape
    wide = w.shape[1]
    block = 512
    span = lambda columns: pl.BlockSpec((block, columns), lambda i: (i, 0))
    return pl.pallas_call(
        functools.partial(gate_up_kernel, n_dp, n_seq),
        grid=(tokens // block,),
        in_specs=[span(width), span(wide // 2), pl.BlockSpec(memory_space=pl.ANY)],
        out_specs=[span(wide // 2), span(wide)],
        out_shape=[
            jax.ShapeDtypeStruct((tokens, wide // 2), BF16),
            jax.ShapeDtypeStruct((tokens, wide), BF16),
        ],
        scratch_shapes=[pltpu.VMEM(w.shape, BF16), pltpu.SemaphoreType.DMA],
        compiler_params=pltpu.CompilerParams(vmem_limit_bytes=56 * 2**20),
        cost_estimate=pl.CostEstimate(
            flops=2 * tokens * width * wide,
            bytes_accessed=2 * (tokens * width + width * wide + tokens * wide * 2),
            transcendentals=tokens * wide // 2,
        ),
        name="gate_up",
    )(x, dhidden, w)


def mm(a, b):
    return jnp.dot(a, b, preferred_element_type=F32)


def outer_sum(left, right):
    return lax.dot_general(left, right, (((0,), (0,)), ((), ())), preferred_element_type=F32)


def back_product(rows, weight):
    return lax.dot_general(rows, weight, (((1,), (1,)), ((), ())), preferred_element_type=F32)


def gather(x, axes):
    return lax.all_gather(x, axes, axis=0, tiled=True)


def scatter(x, axes):
    return lax.psum_scatter(x, axes, scatter_dimension=0, tiled=True)


def shards(
    tokens, lengths, w_qkv, w_out, w_gate_up, w_down, attn_gain, ffn_gain, head_gains, out_grad
):
    n_dp, n_seq = lax.axis_size("dp"), lax.axis_size("seq")
    rows, length, width = tokens.shape
    count = rows * length
    ff = w_gate_up.shape[1] // 2
    part = ff // n_dp
    wr = w_gate_up.shape[0]
    offset = lax.axis_index("seq") * length
    local_pos = offset + jnp.arange(length, dtype=jnp.int32)
    cosine, sine = rope_tables(jnp.concatenate([local_pos] * rows))
    ends = jnp.cumsum(lengths, axis=1, dtype=jnp.int32)
    start = jnp.sum(
        jnp.where(local_pos[None, :, None] >= ends[:, None, :], lengths[:, None, :], 0), axis=2
    ).reshape(1, count)
    start = jnp.broadcast_to(start, (8, count))

    full = (n_dp, n_seq) == (8, 4)
    qkv_w = w_qkv.shape[1]
    paired = w_qkv[:, QW:].reshape(wr, 2, KEY_VALUE_HEADS, HEAD_SIZE).transpose(0, 2, 1, 3)
    spare = width - qkv_w
    gains = jnp.concatenate([attn_gain, ffn_gain])
    gains = [jnp.pad(g, (0, spare - g.shape[0]))[None] for g in (gains, head_gains)]
    gains.append(jnp.zeros((wr - 2, spare), BF16))
    own_qkv = jnp.concatenate(
        [w_qkv[:, :QW], paired.reshape(wr, 2 * KW), jnp.concatenate(gains, axis=0)], axis=1
    )
    out_rows = w_out.shape[0]
    own_out = jnp.pad(w_out, ((0, -out_rows % 16), (0, 0)))
    all_qkv, some_out, spread = gather_weights(own_qkv, [own_out], w_gate_up, n_dp, n_seq)
    qkv_full = all_qkv.reshape(width, width)
    attn_gain_full = all_qkv[:, 0, qkv_w : qkv_w + wr].reshape(-1).astype(F32)
    ffn_gain_full = all_qkv[:, 0, qkv_w + wr : qkv_w + 2 * wr].reshape(-1).astype(F32)
    head_full = all_qkv[:, 1, qkv_w : qkv_w + head_gains.shape[0]].reshape(-1).astype(F32)

    w_down, qkv_full = lax.optimization_barrier((w_down, qkv_full))
    down_w = gather(w_down, "seq")
    cotangent_low = out_grad.reshape(count, width)

    x_rows = tokens.reshape(count, width).astype(F32)
    normed_low = norm_rows(x_rows, attn_gain_full).astype(BF16)
    projected = lax.dot_general(
        qkv_full, normed_low, (((0,), (1,)), ((), ())), preferred_element_type=F32
    )

    queries, pairs = prepare(projected, head_full[:, None], cosine, sine)
    more = [cotangent_low, some_out] if full else []
    heads_out, lse, held, *planes = attend(start, queries, pairs, rows, n_seq, more)
    gate_up_w = gather(spread.reshape(n_dp * wr, 2 * part), "seq")
    if full:
        cotangent_all = planes[0].reshape(n_dp * count, width)
        all_out = planes[1].reshape(n_dp * n_seq, -1, width)
    else:
        cotangent_all, all_out = gather(cotangent_low, "dp"), some_out
    out_full = all_out.reshape(-1, width)
    fill = ((0, 0), (0, all_out.shape[1] - out_rows), (0, 0))
    heads_full = jnp.pad(heads_out.reshape(n_dp * n_seq, out_rows, count), fill)
    heads_full = heads_full.reshape(-1, count)
    middle = x_rows + outer_sum(heads_full, out_full)
    normed2, norm2_pull = jax.vjp(norm_rows, middle, ffn_gain_full)
    normed2_all, dhidden = plane_gather_now(
        normed2.astype(BF16), cotangent_all, down_w, n_dp, n_seq
    )
    hidden, dgate_up = gate_up_product(normed2_all, dhidden, gate_up_w, n_dp, n_seq)
    gate_up_grad = transposed_product(normed2_all, dgate_up, n_dp, n_seq)
    gate_up_grad, dgate_up = lax.optimization_barrier((gate_up_grad, dgate_up))
    gate_up_grad = scatter(gate_up_grad.reshape(width, 2 * part), "seq")
    if full:
        dnormed2, down_grad = plane_sum(dgate_up, gate_up_w, hidden, cotangent_all, count)
    else:
        ordered = gate_up_w.reshape(n_seq, n_dp, wr, 2 * part).transpose(1, 0, 2, 3)
        ordered = ordered.reshape(width, 2 * part)
        dnormed2 = scatter(back_product(dgate_up, ordered).astype(BF16), "dp")
        down_grad = outer_sum(hidden, cotangent_all).astype(BF16)
    dnormed2 = dnormed2.astype(F32)

    dmiddle_norm = norm2_pull(dnormed2)[0]
    dmiddle = cotangent_low.astype(F32) + dmiddle_norm
    dattend = dmiddle.astype(BF16)
    dheads = back_product(out_full, dattend).astype(BF16).reshape(n_dp * n_seq, -1, count)
    dheads = dheads[:, :out_rows].reshape(QW, count)
    if full:
        dqueries, dpairs, mixed = attend_back(
            start, queries, dheads, heads_out, lse, pairs, held, rows, n_seq, [hidden, down_w]
        )
    else:
        dqueries, dpairs = attend_back(
            start, queries, dheads, heads_out, lse, pairs, held, rows, n_seq, []
        )
        mixed = scatter(mm(hidden, down_w).astype(BF16), "dp")
    mixed = middle + mixed.astype(F32)
    gate_up_grad, dqueries = lax.optimization_barrier((gate_up_grad, dqueries))
    gate_up_grad = lax.all_to_all(
        gate_up_grad.reshape(n_dp, wr, 2 * part), "dp", 0, 0, tiled=True
    )
    down_grad, dqueries = lax.optimization_barrier((down_grad, dqueries))
    down_grad = scatter(down_grad, "seq")
    dprojected_low, head_grad = prepare_back(
        projected, head_full[:, None], cosine, sine, dqueries, dpairs
    )
    qkv_grad = lax.dot_general(
        normed_low, dprojected_low, (((0,), (1,)), ((), ())), preferred_element_type=F32
    ).astype(BF16)
    few = head_gains.shape[0]
    head_grad = head_grad.astype(BF16).reshape(n_dp * n_seq, 1, few)
    qkv_grad = lax.dynamic_update_slice(
        qkv_grad.reshape(n_dp * n_seq, wr, width), head_grad, (0, 0, qkv_w)
    )
    dattend, qkv_grad = lax.optimization_barrier((dattend, qkv_grad))
    out_grads = mm(heads_full, dattend).astype(BF16).reshape(n_dp * n_seq, -1, width)
    if full:
        qkv_grad, out_weight_grad, tokens_grad, gate_up_grad, ffn_products = sum_weights(
            [qkv_grad, out_grads],
            dprojected_low,
            qkv_full,
            tokens.reshape(count, width),
            dmiddle,
            attn_gain_full[None],
            gate_up_grad,
            w_gate_up,
        )
        ffn_products = ffn_products[:, 0]
    else:
        qkv_grad, out_weight_grad = (
            scatter(scatter(g.reshape(-1, width), "dp"), "seq").astype(F32)
            for g in (qkv_grad, out_grads)
        )
        gate_up_grad = gate_up_grad.reshape(n_dp, wr, 2, part).transpose(1, 2, 0, 3)
        gate_up_grad = gate_up_grad.reshape(wr, 2 * ff).astype(F32)
        ffn_products = jnp.sum(w_gate_up.astype(F32) * gate_up_grad, axis=1)
        dnormed = back_product(dprojected_low.T, qkv_full)
        tokens_grad = dmiddle + normed_back(dnormed, x_rows, attn_gain_full)
    head_out = qkv_grad[0, qkv_w : qkv_w + few]
    unpaired = qkv_grad[:, QW:qkv_w].reshape(wr, KEY_VALUE_HEADS, 2, HEAD_SIZE).transpose(0, 2, 1, 3)
    qkv_grad = jnp.concatenate([qkv_grad[:, :QW], unpaired.reshape(wr, 2 * KW)], axis=1)
    attn_gain_out = jnp.sum(w_qkv.astype(F32) * qkv_grad, axis=1) / attn_gain.astype(F32)
    ffn_gain_out = ffn_products / ffn_gain.astype(F32)
    return (
        mixed.astype(BF16).reshape(rows, length, width),
        tokens_grad.reshape(rows, length, width),
        qkv_grad,
        out_weight_grad[:out_rows],
        gate_up_grad,
        down_grad.astype(F32),
        attn_gain_out,
        ffn_gain_out,
        head_out,
    )


def solution(mesh):
    in_specs = (
        P("dp", "seq", None),
        P("dp", None),
        P(("dp", "seq"), None),
        P(("dp", "seq"), None),
        P(("dp", "seq"), None),
        P(("dp", "seq"), None),
        P(("dp", "seq")),
        P(("dp", "seq")),
        P(("dp", "seq")),
        P("dp", "seq", None),
    )
    out_specs = (
        P("dp", "seq", None),
        P("dp", "seq", None),
        P(("dp", "seq"), None),
        P(("dp", "seq"), None),
        P(("dp", "seq"), None),
        P(("dp", "seq"), None),
        P(("dp", "seq")),
        P(("dp", "seq")),
        P(("dp", "seq")),
    )
    return jax.shard_map(shards, mesh=mesh, in_specs=in_specs, out_specs=out_specs, check_vma=False)
```

```python
import functools

import jax
import jax.numpy as jnp
from jax import lax
from jax.experimental import pallas as pl
from jax.experimental.pallas import tpu as pltpu
from jax.sharding import PartitionSpec as P

QUERY_HEADS = 20
KEY_VALUE_HEADS = 5
HEAD_SIZE = 64
GROUP = QUERY_HEADS // KEY_VALUE_HEADS
QW = QUERY_HEADS * HEAD_SIZE
KW = KEY_VALUE_HEADS * HEAD_SIZE
BOTH = ("dp", "seq")

epsilon = 1e-06
F32 = jnp.float32
BF16 = jnp.bfloat16
MESH = pl.DeviceIdType.MESH


def norm_rows(inputs, scales):
    return inputs * lax.rsqrt(jnp.mean(inputs * inputs, axis=-1, keepdims=True) + epsilon) * scales


def rope_tables(positions):
    inverse_freq = 10000.0 ** (-(jnp.arange(HEAD_SIZE // 2, dtype=F32) * 2.0 / HEAD_SIZE))
    angles = inverse_freq[:, None] * positions.astype(F32)[None, :]
    return (jnp.cos(angles), jnp.sin(angles))


def head_rows(i):
    return pl.ds(pl.multiple_of(i * HEAD_SIZE, HEAD_SIZE), HEAD_SIZE)


def key_rows(i):
    return head_rows(2 * i), head_rows(2 * i + 1)


def unit(v):
    inverse = lax.rsqrt(jnp.mean(v * v, axis=0, keepdims=True) + epsilon)
    return v * inverse, inverse


def prepare_kernel(p_ref, gain_ref, cos_ref, sin_ref, q_ref, kv_ref):
    cosine, sine = cos_ref[...], sin_ref[...]

    def turned(v, gain):
        v = unit(v)[0] * gain
        first, second = v[: HEAD_SIZE // 2], v[HEAD_SIZE // 2 :]
        return jnp.concatenate(
            [first * cosine - second * sine, second * cosine + first * sine], axis=0
        )

    @pl.loop(0, KEY_VALUE_HEADS)
    def _(i):
        key, value = key_rows(i)
        keys_in = p_ref[head_rows(QUERY_HEADS + i), :]
        kv_ref[key, :] = turned(keys_in, gain_ref[HEAD_SIZE:, :]).astype(BF16)
        values_in = p_ref[head_rows(QUERY_HEADS + KEY_VALUE_HEADS + i), :]
        kv_ref[value, :] = values_in.astype(BF16)

    @pl.loop(0, QUERY_HEADS)
    def _(i):
        rows = head_rows(i)
        queries = turned(p_ref[rows, :], gain_ref[:HEAD_SIZE, :]) * HEAD_SIZE**-0.5
        q_ref[rows, :] = queries.astype(BF16)


def prepare(projected, gains, cosine, sine):
    tokens = projected.shape[1]
    return pl.pallas_call(
        prepare_kernel,
        out_shape=[
            jax.ShapeDtypeStruct((QW, tokens), BF16),
            jax.ShapeDtypeStruct((2 * KW, tokens), BF16),
        ],
        compiler_params=pltpu.CompilerParams(vmem_limit_bytes=40 * 2**20),
        name="prepare",
    )(projected, gains, cosine, sine)


def prepare_back_kernel(p_ref, gain_ref, cos_ref, sin_ref, dq_ref, dkv_ref, out_ref, dg_ref, acc):
    cosine, sine = cos_ref[...], sin_ref[...]
    acc[...] = jnp.zeros_like(acc)

    def back(v, gain, dy, lines):
        u, inverse = unit(v)
        first, second = dy[: HEAD_SIZE // 2], dy[HEAD_SIZE // 2 :]
        dz = jnp.concatenate(
            [first * cosine + second * sine, second * cosine - first * sine], axis=0
        )
        acc[lines, :] += dz * u
        du = dz * gain
        return inverse * (du - u * jnp.mean(du * u, axis=0, keepdims=True))

    @pl.loop(0, KEY_VALUE_HEADS)
    def _(i):
        key, value = key_rows(i)
        rows = head_rows(QUERY_HEADS + i)
        dv = back(p_ref[rows, :], gain_ref[HEAD_SIZE:, :], dkv_ref[key, :], slice(HEAD_SIZE, None))
        out_ref[rows, :] = dv.astype(BF16)
        out_ref[head_rows(QUERY_HEADS + KEY_VALUE_HEADS + i), :] = dkv_ref[value, :].astype(BF16)

    @pl.loop(0, QUERY_HEADS)
    def _(i):
        rows = head_rows(i)
        dy = dq_ref[rows, :] * HEAD_SIZE**-0.5
        dv = back(p_ref[rows, :], gain_ref[:HEAD_SIZE, :], dy, slice(0, HEAD_SIZE))
        out_ref[rows, :] = dv.astype(BF16)

    rest = out_ref.shape[0] - QW - 2 * KW
    out_ref[QW + 2 * KW :, :] = jnp.zeros((rest, out_ref.shape[1]), BF16)
    total = jnp.sum(acc[...], axis=1, keepdims=True)
    dg_ref[...] = jnp.broadcast_to(total, dg_ref.shape)


def prepare_back(projected, gains, cosine, sine, dqueries, dpairs):
    tokens = projected.shape[1]
    dprojected, dgains = pl.pallas_call(
        prepare_back_kernel,
        out_shape=[
            jax.ShapeDtypeStruct(projected.shape, BF16),
            jax.ShapeDtypeStruct((2 * HEAD_SIZE, 128), F32),
        ],
        scratch_shapes=[pltpu.VMEM((2 * HEAD_SIZE, tokens), F32)],
        compiler_params=pltpu.CompilerParams(vmem_limit_bytes=40 * 2**20),
        name="prepare_back",
    )(projected, gains, cosine, sine, dqueries, dpairs)
    return dprojected, dgains[:, 0]


def dot(a, b):
    return jnp.dot(a, b, preferred_element_type=F32)


def places():
    d, s = lax.axis_index("dp"), lax.axis_index("seq")
    core, column, line = d % 2, (d // 2) % 2, d // 4
    return d, s, d + 1 - 2 * core, d + 2 - 4 * column, d + 4 - 8 * line, line


def greet(peers, line=None):
    barrier = pltpu.get_barrier_semaphore()

    def signal(peer):
        pl.semaphore_signal(barrier, inc=1, device_id=peer, device_id_type=MESH)

    for peer in peers:
        signal(peer)
    if line is None:
        pl.semaphore_wait(barrier, len(peers))
        return
    d, s = line
    last = lax.axis_size("seq") - 1
    pl.when(s < last)(lambda: signal((d, s + 1)))
    pl.when(s > 0)(lambda: signal((d, s - 1)))
    pl.semaphore_wait(barrier, len(peers) + 1 - s // last + (s + last - 1) // last)


def remote(src, dst, sent, got, peer):
    return pltpu.make_async_remote_copy(
        src_ref=src,
        dst_ref=dst,
        send_sem=sent,
        recv_sem=got,
        device_id=peer,
        device_id_type=MESH,
    )


def plane_stages(x_ref, out_ref, own_sem, sent, got, place, ordered=False):
    d, s, d_c, d_x, d_y, line = place
    flip, d_d = d_c - d, d_x + d_y - d
    slots = list(range(8))
    if ordered:
        slots = [d, d_c, d_x, d_x + flip, d_y, d_y + flip, d_d, d_d + flip]
    half = x_ref.shape[0] // 2
    halves = (pl.ds(0, half), pl.ds(half, half))
    source = {1: 0, 2: 0, 4: 0, 3: 2, 5: 4, 7: 6}

    def piece(k, h, peer):
        back = source[k] if k in source else (4 if h == 0 else 2)
        src = x_ref.at[halves[h]] if back == 0 else out_ref.at[slots[back], halves[h]]
        dst = out_ref.at[slots[back] if ordered else k, halves[h]]
        return remote(src, dst, sent.at[k, h], got.at[k, h], (peer, s))

    own = pltpu.make_async_copy(x_ref, out_ref.at[slots[0]], own_sem)

    def begin(h):
        for k, peer in ((2, d_x), (4, d_y), (1, d_c)):
            piece(k, h, peer).start()
        if h:
            own.start()

    def first():
        piece(4, 0, d_y).wait_recv()
        piece(6, 0, d_x).start()
        piece(5, 0, d_c).start()
        piece(2, 0, d_x).wait_recv()
        piece(3, 0, d_c).start()

    def second():
        piece(2, 1, d_x).wait_recv()
        piece(6, 1, d_y).start()
        piece(3, 1, d_c).start()
        piece(4, 1, d_y).wait_recv()
        piece(5, 1, d_c).start()

    def end():
        for h in (0, 1):
            piece(6, h, d_x).wait_recv()
            piece(7, h, d_c).start()
        for k in (1, 3, 5, 7):
            for h in (0, 1):
                piece(k, h, d_c).wait_recv()
        for k in range(1, 8):
            for h in (0, 1):
                piece(k, h, d_c).wait_send()
        own.wait()

    return begin, first, second, end


def abreast(block):
    return jnp.concatenate(
        [block[i * HEAD_SIZE : (i + 1) * HEAD_SIZE] for i in range(GROUP)], axis=1
    )


def across(rows):
    return jnp.concatenate([rows[i : i + 1] for i in range(GROUP)], axis=1)


def seen(back, me, start):
    length = start.shape[1]
    key = lax.broadcasted_iota(jnp.int32, (length, length), 0)
    found = key + (me - back) * length >= start
    if back == 0:
        found &= key <= lax.broadcasted_iota(jnp.int32, (length, length), 1)
    bias = jnp.where(found, 0.0, -1e30)
    return jnp.concatenate([bias] * GROUP, axis=1)


def spans(i, length):
    row, head = i // KEY_VALUE_HEADS, i % KEY_VALUE_HEADS
    wide, pair = GROUP * HEAD_SIZE, 2 * HEAD_SIZE
    tokens = pl.ds(pl.multiple_of(row * length, length), length)
    return (
        tokens,
        pl.ds(pl.multiple_of(head * wide, wide), wide),
        pl.ds(pl.multiple_of(head * pair, pair), pair),
        head,
    )


def attend_kernel(n, rows, planes, out_rows, start_ref, q_ref, kv_ref, *refs):
    x_refs, refs = refs[:planes], refs[planes:]
    o_ref, lse_ref, held, *refs = refs
    out_refs, refs = refs[:planes], refs[planes:]
    if planes:
        full_ref, filled, *refs = refs
    o_acc, l_acc, sent, got, *refs = refs
    d, me = lax.axis_index("dp"), lax.axis_index("seq")
    length = q_ref.shape[1] // rows
    if planes:
        place = places()
        d, me, d_c, d_x, d_y, _ = place
        greet([(d_c, me), (d_x, me), (d_y, me)], (d, me))
        each = [
            plane_stages(x_refs[i], out_refs[i], *refs[3 * i : 3 * i + 3], place, i > 0)
            for i in range(planes)
        ]
    else:
        greet([], (d, me))
        each = []

    def climb(step, head):
        lines = pl.ds(head * 2 * HEAD_SIZE, 2 * HEAD_SIZE)
        src = kv_ref.at[lines] if step == 1 else held.at[step - 2, lines]
        dst = held.at[step - 1, lines]
        return remote(src, dst, sent.at[step - 1, head], got.at[step - 1, head], (d, me + 1))

    heads = range(KEY_VALUE_HEADS)

    def climbs(step):
        for head in heads:
            climb(step, head).start()

    def level(back):
        @pl.loop(0, rows * KEY_VALUE_HEADS, unroll=KEY_VALUE_HEADS)
        def _(i):
            tokens, wide, pair, head = spans(i, length)
            block = kv_ref[pair, tokens] if back == 0 else held[back - 1, pair, tokens]
            keys, values = block[:HEAD_SIZE].T, block[HEAD_SIZE:]
            bias = seen(back, me, start_ref[0:1, tokens])
            p = jnp.exp(dot(keys, abreast(q_ref[wide, tokens])) + bias)
            total = jnp.sum(p, axis=0, keepdims=True)
            out = dot(values, p.astype(BF16))
            for g in range(GROUP):
                own = slice(g * length, (g + 1) * length)
                line = slice(g, g + 1)
                part = pl.ds(wide.start + g * HEAD_SIZE, HEAD_SIZE)
                if back == 0:
                    l_acc[head, line, tokens] = total[:, own]
                    o_acc[part, tokens] = out[:, own]
                else:
                    l_acc[head, line, tokens] += total[:, own]
                    o_acc[part, tokens] += out[:, own]

    pl.when(me < n - 1)(lambda: climbs(1))
    for stages in each:
        stages[0](0)
        stages[0](1)
    level(0)
    for back in range(1, n):

        def step(back=back):
            for head in heads:
                climb(back, head).wait_recv()
                if back < n - 1:
                    pl.when(me < n - 1)(lambda head=head: climb(back + 1, head).start())
            level(back)

        pl.when(me >= back)(step)
        if back <= 2:
            for stages in each:
                stages[back]()

    @pl.loop(0, rows * KEY_VALUE_HEADS)
    def _(i):
        tokens, wide, pair, head = spans(i, length)
        for g in range(GROUP):
            line = slice(g, g + 1)
            part = pl.ds(wide.start + g * HEAD_SIZE, HEAD_SIZE)
            out = o_acc[part, tokens] / l_acc[head, line, tokens]
            o_acc[part, tokens] = out
            o_ref[part, tokens] = out.astype(BF16)
            lse_ref[head, line, tokens] = jnp.log(l_acc[head, line, tokens])

    if planes:
        tall = full_ref.shape[0] // 32
        filled[...] = jnp.zeros_like(filled)

        @pl.loop(0, 32)
        def _(i):
            src = pl.ds(pl.multiple_of(i * out_rows, 8), out_rows)
            dst = pl.ds(pl.multiple_of(i * tall, 8), out_rows)
            filled[dst, :] = o_acc[src, :]

        full_ref[...] = filled[...].astype(BF16)

    for back in range(1, n):
        for head in heads:
            pl.when((me >= back - 1) & (me < n - 1))(
                lambda back=back, head=head: climb(back, head).wait_send()
            )
    for stages in each:
        stages[3]()


def attend(start, queries, pairs, rows, n, more, out_rows):
    vmem, dma = pl.BlockSpec(memory_space=pltpu.VMEM), pltpu.SemaphoreType.DMA
    anywhere = pl.BlockSpec(memory_space=pl.ANY)
    count = queries.shape[1]
    lines = (KEY_VALUE_HEADS, 8, count)
    out_shape = [
        jax.ShapeDtypeStruct(queries.shape, BF16),
        jax.ShapeDtypeStruct(lines, F32),
        jax.ShapeDtypeStruct((n - 1, *pairs.shape), BF16),
    ]
    scratch, full = [], []
    if more:
        full = [(QW // out_rows * more[1].shape[1], count)]
        scratch.append(pltpu.VMEM(full[0], F32))
    scratch += [
        pltpu.VMEM(queries.shape, F32),
        pltpu.VMEM(lines, F32),
        dma((n - 1, KEY_VALUE_HEADS)),
        dma((n - 1, KEY_VALUE_HEADS)),
    ]
    for extra in more:
        out_shape.append(jax.ShapeDtypeStruct((8, *extra.shape), BF16))
        scratch += [dma, dma((8, 2)), dma((8, 2))]
    out_shape += [jax.ShapeDtypeStruct(shape, BF16) for shape in full]
    return pl.pallas_call(
        functools.partial(attend_kernel, n, rows, len(more), out_rows),
        in_specs=[vmem] * 3 + [anywhere] * len(more),
        out_specs=[vmem] * 3 + [anywhere] * len(more) + [vmem] * len(full),
        out_shape=out_shape,
        scratch_shapes=scratch,
        compiler_params=pltpu.CompilerParams(
            collective_id=2, has_side_effects=True, vmem_limit_bytes=48 * 2**20
        ),
        name="attend",
    )(start, queries, pairs, *more)


def plus(ref, *others):
    total = ref[...].astype(F32)
    for other in others:
        total += other[...].astype(F32)
    ref[...] = total.astype(BF16)


def attend_back_kernel(n, rows, summed, *refs):
    start_ref, q_ref, do_ref, o_ref, lse_ref, kv_ref, held, *refs = refs
    if summed:
        h_ref, w_ref, m_ref, *refs = refs
    dq_ref, dkv_ref, *refs = refs
    if summed:
        mixed_ref, *refs = refs
    inner, part, rcv, sent, got, *refs = refs
    d, me = lax.axis_index("dp"), lax.axis_index("seq")
    length = q_ref.shape[1] // rows
    if summed:
        place = places()
        d, me, d_c, d_x, d_y, _ = place
        w_v, h_v, m_v, w_sem, h_sem, m_sem, *refs = refs
        kept, leaving = refs[:2]
        m_load = pltpu.make_async_copy(m_ref, m_v, m_sem)
        load, product = block_products(h_ref, h_v, h_sem, lambda h, span: dot(h, w_v[:, span]))
        load(0).start()
        w_load = pltpu.make_async_copy(w_ref, w_v, w_sem)
        w_load.start()
        greet([(d_c, me), (d_x, me), (d_y, me)], (d, me))
        crossing, far, near, pass_on, end = plane_sums(*refs, place)

        def pair(turn, i):
            slot = turn // 2 % 2
            if turn >= 4:
                crossing(3 if slot == 0 else 1, slot).wait_send()
            product(turn, leaving.at[slot])
            crossing(i, slot).start()
            product(turn + 1, kept.at[i])

        def stage(i):
            if i == 0:
                w_load.wait()
                m_load.start()
                pair(0, 3)
                far()
            elif i == 1:
                pair(2, 1)
                near(1)
                pair(4, 2)
                near(2)
                pair(6, 0)
                near(0)
            elif i == 2:
                pass_on()
            else:
                end()
                m_load.wait()
                mixed_ref[...] = (kept[0].astype(F32) + m_v[...]).astype(BF16)
                crossing(2, 0).wait_send()
                crossing(0, 1).wait_send()
    else:
        greet([], (d, me))

        def stage(i):
            pass

    def descend(back):
        return remote(
            part.at[back - 1], rcv.at[back - 1], sent.at[back - 1], got.at[back - 1], (d, me - 1)
        )

    def level(back):
        @pl.loop(0, rows * KEY_VALUE_HEADS, unroll=2)
        def _(i):
            tokens, wide, pair, head = spans(i, length)
            block = kv_ref[pair, tokens] if back == 0 else held[back - 1, pair, tokens]
            keys_t = block[:HEAD_SIZE]
            keys, values = keys_t.T, block[HEAD_SIZE:].T
            q, do = abreast(q_ref[wide, tokens]), abreast(do_ref[wide, tokens])
            bias = seen(back, me, start_ref[0:1, tokens])
            p = jnp.exp(dot(keys, q) + (bias - across(lse_ref[head, :, tokens])))
            ds = (p * (dot(values, do) - across(inner[head, :, tokens]))).astype(BF16)
            dv = back_product(p.astype(BF16), do)
            dk = back_product(ds, q)
            dq = dot(keys_t, ds)
            if back == 0:
                dkv_ref[pair, tokens] = jnp.concatenate([dk.T, dv.T], axis=0)
            else:
                part[back - 1, pair, tokens] = jnp.concatenate([dk.T, dv.T], axis=0).astype(BF16)
            for g in range(GROUP):
                own = slice(g * length, (g + 1) * length)
                line = pl.ds(wide.start + g * HEAD_SIZE, HEAD_SIZE)
                dq_ref[line, tokens] += dq[:, own]

    def finish(back):
        def more():
            descend(back + 1).wait_recv()
            if back == 0:
                dkv_ref[...] += rcv[0].astype(F32)
            else:
                plus(part.at[back - 1], rcv.at[back])

        if back < n - 1:
            pl.when(me < n - 1)(more)
        if back > 0:
            descend(back).start()

    stage(0)
    dq_ref[...] = jnp.zeros_like(dq_ref)

    @pl.loop(0, rows * KEY_VALUE_HEADS)
    def _(i):
        tokens, wide, pair, head = spans(i, length)
        for g in range(GROUP):
            line = slice(g, g + 1)
            own = pl.ds(wide.start + g * HEAD_SIZE, HEAD_SIZE)
            product = do_ref[own, tokens].astype(F32) * o_ref[own, tokens].astype(F32)
            inner[head, line, tokens] = jnp.sum(product, axis=0, keepdims=True)

    for back in range(n - 1, -1, -1):

        def run(back=back):
            level(back)
            pl.when(me == n - 1)(lambda: finish(back))

        if back:
            pl.when(me >= back)(run)
        else:
            level(0)
            pl.when(me == n - 1)(lambda: finish(0))
        if back + 1 < n - 1:
            pl.when((me >= back + 1) & (me < n - 1))(lambda back=back: finish(back + 1))
        if n - 1 - back in (1, 2):
            stage(n - 1 - back)
    pl.when(me < n - 1)(lambda: finish(0))
    stage(3)
    for back in range(1, n):
        pl.when(me >= back)(lambda back=back: descend(back).wait_send())


def attend_back(start, queries, dheads, heads, lse, pairs, held, rows, n, more):
    vmem, dma = pl.BlockSpec(memory_space=pltpu.VMEM), pltpu.SemaphoreType.DMA
    anywhere = pl.BlockSpec(memory_space=pl.ANY)
    count = queries.shape[1]
    out_shape = [
        jax.ShapeDtypeStruct(queries.shape, F32),
        jax.ShapeDtypeStruct(pairs.shape, F32),
    ]
    scratch = [
        pltpu.VMEM((KEY_VALUE_HEADS, 8, count), F32),
        pltpu.VMEM((n - 1, *pairs.shape), BF16),
        pltpu.VMEM((n - 1, *pairs.shape), BF16),
        dma((n - 1,)),
        dma((n - 1,)),
    ]
    if more:
        (tokens, deep), (_, width) = more[0].shape, more[1].shape
        block = tokens // 8
        out_shape.append(jax.ShapeDtypeStruct((block, width), BF16))
        scratch += [
            pltpu.VMEM((deep, width), BF16),
            pltpu.VMEM((2, block, deep), BF16),
            pltpu.VMEM((block, width), F32),
            dma,
            dma((2,)),
            dma,
            *sums_scratch(block, width),
        ]
    return pl.pallas_call(
        functools.partial(attend_back_kernel, n, rows, bool(more)),
        in_specs=[vmem] * 7 + [anywhere] * len(more),
        out_specs=[vmem] * len(out_shape),
        out_shape=out_shape,
        scratch_shapes=scratch,
        compiler_params=pltpu.CompilerParams(
            collective_id=3, has_side_effects=True, vmem_limit_bytes=62 * 2**20
        ),
        name="attend_back",
    )(start, queries, dheads, heads, lse, pairs, held, *more)


def weights_kernel(n, *refs):
    x_refs, (w_ref, *out_refs), refs = refs[:n], refs[n : 2 * n + 1], refs[2 * n + 1 :]
    spread_ref, own_sem, recv, send_z, send_x, send_y, send_d, send_c, own_w, sent_w, got_w = refs
    d, s, d_c, d_x, d_y, line = places()
    d_d = d_x + 4 - 8 * line
    flip = d_c - d
    plane = (d, d_c, d_x, d_x + flip, d_y, d_y + flip, d_d, d_d + flip)
    greet([(other, s) for other in plane[1:]], (d, s))
    part = spread_ref.shape[2] // 2

    def columns(k, half):
        begin = half * 8 * part + plane[k] * part
        src = w_ref.at[:, pl.ds(pl.multiple_of(begin, 128), part)]
        dst = spread_ref.at[d, :, pl.ds(half * part, part)]
        if k == 0:
            return pltpu.make_async_copy(src, dst, own_w.at[half])
        return remote(src, dst, sent_w.at[k, half], got_w.at[k, half], (plane[k], s))

    def copies(slot, sent, got, peer, own=False, many=1):
        return [
            remote(
                x_refs[i] if own else out_refs[i].at[slot if i == 0 else slot % 4],
                out_refs[i].at[slot if i == 0 else slot % 4],
                sent(i),
                got(i),
                peer,
            )
            for i in range(many)
        ]

    def start(group):
        for one in group:
            one.start()

    def sent(group):
        for one in group:
            one.wait_send()

    def each(visit, between=lambda: None):
        visit(s, 0)
        between()
        for far in (1, 2, 3):
            pl.when(s >= far)(lambda far=far: visit(s - far, 1))
            pl.when(s + far <= 3)(lambda far=far: visit(s + far, -1))

    def got(k, b):
        return lambda i: recv.at[i, k, b]

    def arrived(k, b):
        many = 1 if k else n
        for one in copies(d * 4 + b, lambda i: send_x.at[i, b], got(k, b), (d_x, s), many=many):
            one.wait_recv()

    own = [
        pltpu.make_async_copy(x_refs[i], out_refs[i].at[d * 4 + s if i == 0 else s], own_sem.at[i])
        for i in range(n)
    ]
    start(own)

    def up(b, own=False):
        return copies(d * 4 + b, lambda i: send_z.at[i, 0, b], got(0, b), (d, s + 1), own, n)

    def down(b, own=False):
        return copies(d * 4 + b, lambda i: send_z.at[i, 1, b], got(0, b), (d, s - 1), own, n)

    def spread(b, own=False):
        return (
            copies(d * 4 + b, lambda i: send_x.at[i, b], got(2, b), (d_x, s), own)
            + copies(d * 4 + b, lambda i: send_y.at[i, b], got(4, b), (d_y, s), own)
            + copies(d * 4 + b, lambda i: send_c.at[i, 0, b], got(1, b), (d_c, s), own)
        )

    def column_block(b, direction):
        own = direction == 0
        if direction:
            arrived(0, b)
        if direction >= 0:
            pl.when(s < 3)(lambda: start(up(b, own)))
        if direction <= 0:
            pl.when(s > 0)(lambda: start(down(b, own)))
        start(spread(b, own))

    def start_columns():
        for k in range(8):
            for half in (0, 1):
                columns(k, half).start()

    each(column_block, start_columns)

    def over_y(b):
        return copies(d_x * 4 + b, lambda i: send_d.at[i, b], got(6, b), (d_y, s))

    def over_x(b):
        return copies(d_y * 4 + b, lambda i: send_d.at[i, b], got(6, b), (d_x, s))

    def to_core(index, holder, b):
        return copies(
            holder * 4 + b, lambda i: send_c.at[i, index, b], got(2 * index + 1, b), (d_c, s)
        )

    def side_blocks(b, direction):
        arrived(2, b)
        pl.when(b % 2 == 0)(lambda: start(over_y(b)))
        start(to_core(1, d_x, b))
        arrived(4, b)
        pl.when(b % 2 == 1)(lambda: start(over_x(b)))
        start(to_core(2, d_y, b))

    each(side_blocks)

    def far_block(b, direction):
        arrived(6, b)
        start(to_core(3, d_d, b))

    each(far_block)

    def finish(b, direction):
        for k in (1, 3, 5, 7):
            arrived(k, b)
        if direction >= 0:
            pl.when(s < 3)(lambda: sent(up(b)))
        if direction <= 0:
            pl.when(s > 0)(lambda: sent(down(b)))
        sent(spread(b))
        sent(over_y(b))
        sent(to_core(1, d_x, b))
        sent(to_core(2, d_y, b))
        sent(to_core(3, d_d, b))

    each(finish)
    for one in own:
        one.wait()
    for k in range(8):
        for half in (0, 1):
            if k:
                columns(k, half).wait_recv()
                columns(k, half).wait_send()
            else:
                columns(k, half).wait()


def gather_weights(first, others, wide, n_dp, n_seq):
    rows, part = wide.shape[0], wide.shape[1] // (2 * n_dp)
    if (n_dp, n_seq) != (8, 4):
        spread = lax.all_to_all(wide.reshape(rows, 2, n_dp, part), "dp", 2, 0, tiled=False)
        spread = spread.reshape(n_dp, rows, 2 * part)
        return [lax.all_gather(x, BOTH, axis=0, tiled=False) for x in (first, *others)] + [spread]
    arrays = [first, *others]
    n = len(arrays)
    dma = pltpu.SemaphoreType.DMA
    return pl.pallas_call(
        functools.partial(weights_kernel, n),
        out_shape=[
            jax.ShapeDtypeStruct((n_seq if i else n_dp * n_seq, *x.shape), x.dtype)
            for i, x in enumerate(arrays)
        ]
        + [jax.ShapeDtypeStruct((n_dp, rows, 2 * part), wide.dtype)],
        in_specs=[pl.BlockSpec(memory_space=pl.ANY)] * (n + 1),
        out_specs=[pl.BlockSpec(memory_space=pl.ANY)] * (n + 1),
        scratch_shapes=[
            dma((n,)),
            dma((n, 8, 4)),
            dma((n, 2, 4)),
            dma((n, 4)),
            dma((n, 4)),
            dma((n, 4)),
            dma((n, 4, 4)),
            dma((2,)),
            dma((8, 2)),
            dma((8, 2)),
        ],
        compiler_params=pltpu.CompilerParams(collective_id=1, has_side_effects=True),
        name="gather_weights",
    )(*arrays, wide)


def weight_sums(product, refs, place):
    kept, leaving, rcv_c, rcv_d, rcv_x, rcv_y, rcv_z = refs[:7]
    sent_c, got_c, sent_p, got_p, sent_z, got_z = refs[7:]
    d, s, d_c, d_x, d_y, line = place
    holders = (d, d_x, d_y, d_x + d_y - d)
    flip = d_c - d
    low, high = pl.ds(0, 2), pl.ds(2, 2)

    def crossing(i, slot):
        return remote(leaving.at[slot], rcv_c.at[i], sent_c.at[i], got_c.at[i], (d_c, s))

    def pair(i, slot, before=None):
        if before is not None:
            crossing(before, slot).wait_send()
        product(holders[i] + flip, leaving.at[slot])
        crossing(i, slot).start()
        product(holders[i], kept.at[i])

    def merge(i):
        crossing(i, 0).wait_recv()
        plus(kept.at[i], rcv_c.at[i])

    def push(i):
        src, dst, peer = (
            (kept.at[3, low], rcv_d.at[low], d_x),
            (kept.at[3, high], rcv_d.at[high], d_y),
            (kept.at[1, low], rcv_x.at[low], d_x),
            (kept.at[2, high], rcv_y.at[high], d_y),
            (kept.at[2, low], rcv_y.at[low], d_y),
            (kept.at[1, high], rcv_x.at[high], d_x),
        )[i]
        return remote(src, dst, sent_p.at[i], got_p.at[i], (peer, s))

    def straight(b):
        return remote(kept.at[0, b], rcv_z.at[s], sent_z.at[b], got_z.at[s], (d, b))

    def from_line(b):
        return remote(kept.at[0, b], rcv_z.at[b], sent_z.at[b], got_z.at[b], (d, b))

    def far():
        pair(3, 0)
        pair(1, 1)
        merge(3)
        push(0).start()
        push(1).start()

    def near():
        pair(2, 0, 3)
        pair(0, 1, 1)
        merge(1)
        push(2).start()
        merge(2)
        push(3).start()
        merge(0)

    def pass_on():
        push(0).wait_recv()
        plus(kept.at[2, low], rcv_d.at[low])
        push(4).start()
        push(1).wait_recv()
        plus(kept.at[1, high], rcv_d.at[high])
        push(5).start()

    def along():
        for i in (2, 3, 4, 5):
            push(i).wait_recv()
        plus(kept.at[0], rcv_x, rcv_y)
        for b in range(4):
            pl.when(s != b)(lambda b=b: straight(b).start())

    def end(out_ref):
        out_ref[...] = kept[0, s].astype(F32)
        for b in range(4):

            @pl.when(s != b)
            def _(b=b):
                from_line(b).wait_recv()
                out_ref[...] += rcv_z[b].astype(F32)

        for b in range(4):
            pl.when(s != b)(lambda b=b: straight(b).wait_send())
        crossing(2, 0).wait_send()
        crossing(0, 1).wait_send()
        for i in range(6):
            push(i).wait_send()

    return far, near, pass_on, along, end


def weight_sums_scratch(rows, columns):
    dma = pltpu.SemaphoreType.DMA
    buffer = lambda *lead: pltpu.VMEM((*lead, rows, columns), BF16)
    return [
        buffer(4, 4),
        buffer(2, 4),
        buffer(4, 4),
        buffer(4),
        buffer(4),
        buffer(4),
        buffer(4),
        dma((4,)),
        dma((4,)),
        dma((6,)),
        dma((6,)),
        dma((4,)),
        dma((4,)),
    ]


def normed_back(dy, x, gain):
    inverse = lax.rsqrt(jnp.mean(x * x, axis=1, keepdims=True) + epsilon)
    gy = dy * gain
    x = x * inverse
    return inverse * (gy - x * jnp.mean(gy * x, axis=1, keepdims=True))


def sum_weights_kernel(n_ref, p_ref, h_ref, a_ref, few_ref, own_ref, *refs):
    w_ref, x_ref, dm_ref, gain_ref, back_ref, wide_ref, *refs = refs
    qkv_out, few_out, products_out, out_out, dx_ref, wide_out, dg_ref, *refs = refs
    w_v, qkv_sum, back_v, w_sem, own_sem, sent_w, got_w, *refs = refs
    w_load = pltpu.make_async_copy(w_ref, w_v, w_sem)
    w_load.start()
    place = places()
    d, s, d_c, d_x, d_y, line = place
    flip, d_d = d_c - d, d_x + d_y - d
    plane = (d, d_c, d_x, d_x + flip, d_y, d_y + flip, d_d, d_d + flip)
    greet([(other, s) for other in plane[1:]] + [(d, (s + i) % 4) for i in (1, 2, 3)])

    def exchange(k):
        src, dst = back_ref.at[plane[k]], back_v.at[d]
        if k == 0:
            return pltpu.make_async_copy(src, dst, own_sem)
        return remote(src, dst, sent_w.at[k], got_w.at[k], (plane[k], s))

    width, chunk = p_ref.shape[0], 512

    def chunks(make, dst):
        @pl.loop(0, width // chunk)
        def _(c):
            span = pl.ds(pl.multiple_of(c * chunk, chunk), chunk)
            dst[:, :, span] = make(span).astype(BF16).reshape(*dst.shape[:2], chunk)

    def qkv_product(k, dst):
        tall = dst.shape[0] * dst.shape[1]
        rows = n_ref[:, pl.ds(pl.multiple_of(k * tall, tall), tall)].T
        chunks(lambda span: back_product(rows, p_ref[span, :]), dst)
        for b in range(4):
            dst[b, :16, -128:] = few_ref[k * 4 + b]

    def out_product(k, dst):
        tall = dst.shape[0] * dst.shape[1]
        rows = h_ref[pl.ds(pl.multiple_of(k * tall, 16), tall), :]
        chunks(lambda span: dot(rows, a_ref[:, span]), dst)

    far, near, pass_on, along, end = weight_sums(qkv_product, refs[:13], place)
    far_2, near_2, pass_on_2, along_2, end_2 = weight_sums(out_product, refs[13:], place)
    block = 128

    def token_grads(first, count):
        def body(x_tile, dm_tile, dx_tile):
            i = pl.program_id(0) + first
            span = pl.ds(pl.multiple_of(i * block, block), block)
            dy = back_product(p_ref[:, span].T, w_v[...])
            dx_tile[...] = dm_tile[...] + normed_back(dy, x_tile[...].astype(F32), gain_ref[...])

        spec = lambda: pl.BlockSpec((block, x_ref.shape[1]), lambda i: (i + first, 0))
        pltpu.emit_pipeline(body, grid=(count,), in_specs=[spec(), spec()], out_specs=[spec()])(
            x_ref, dm_ref, dx_ref
        )

    blocks = x_ref.shape[0] // block
    far()
    near()
    w_load.wait()
    token_grads(0, 1)
    pass_on()
    far_2()
    near_2()
    token_grads(1, 2)
    along()
    pass_on_2()
    for k in range(8):
        exchange(k).start()
    token_grads(3, blocks - 3)
    along_2()
    end(qkv_sum)
    exchange(0).wait()
    for k in range(1, 8):
        exchange(k).wait_recv()
        exchange(k).wait_send()
    part = back_v.shape[2] // 2
    total = jnp.zeros((dg_ref.shape[0], 1), F32)
    for j in range(16):
        half_j, holder = j // 8, j % 8
        span = slice(j * part, (j + 1) * part)
        grad = back_v[holder, :, half_j * part : (half_j + 1) * part].astype(F32)
        wide_out[:, span] = grad
        total += jnp.sum(grad * wide_ref[:, span].astype(F32), axis=1, keepdims=True)
    dg_ref[...] = jnp.broadcast_to(total, dg_ref.shape)
    inner = QW + 2 * KW
    total = jnp.sum(qkv_sum[:, :inner] * own_ref[:, :inner].astype(F32), axis=1, keepdims=True)
    products_out[...] = jnp.broadcast_to(total, products_out.shape)
    few_out[...] = qkv_sum[:16, inner:]
    qkv_out[...] = qkv_sum[:, :inner]
    end_2(out_out)


def sum_weights(normed, dprojected, heads, dattend, few, own, w, x, dmiddle, gain, back, wide):
    dma, anywhere = pltpu.SemaphoreType.DMA, pl.BlockSpec(memory_space=pl.ANY)
    vmem = pl.BlockSpec(memory_space=pltpu.VMEM)
    rows, width = own.shape
    tall = heads.shape[0] // 32
    scratch = [
        pltpu.VMEM(w.shape, BF16),
        pltpu.VMEM(own.shape, F32),
        pltpu.VMEM(back.shape, BF16),
        dma,
        dma,
        dma((8,)),
        dma((8,)),
    ]
    scratch += weight_sums_scratch(rows, width) + weight_sums_scratch(tall, width)
    return pl.pallas_call(
        sum_weights_kernel,
        out_shape=[
            jax.ShapeDtypeStruct((rows, QW + 2 * KW), F32),
            jax.ShapeDtypeStruct((16, width - QW - 2 * KW), F32),
            jax.ShapeDtypeStruct((rows, 128), F32),
            jax.ShapeDtypeStruct((tall, width), F32),
            jax.ShapeDtypeStruct(dmiddle.shape, F32),
            jax.ShapeDtypeStruct(wide.shape, F32),
            jax.ShapeDtypeStruct((rows, 128), F32),
        ],
        in_specs=[vmem] * 6 + [anywhere] * 3 + [vmem, anywhere, vmem],
        out_specs=[vmem] * 4 + [anywhere, vmem, vmem],
        scratch_shapes=scratch,
        compiler_params=pltpu.CompilerParams(
            collective_id=6, has_side_effects=True, vmem_limit_bytes=63 * 2**20
        ),
        name="sum_weights",
    )(normed, dprojected, heads, dattend, few, own, w, x, dmiddle, gain, back, wide)


def plane_kernel(rows, heads_ref, w_ref, x_ref, gain_ref, g_ref, down_ref, *refs):
    out_ref, dh_ref, mid_ref, w_v, x_v, down_v, mid_v, n_v, load, mid_sem, *refs = refs
    place = places()
    d, s, d_c, d_x, d_y, line = place
    w_load = pltpu.make_async_copy(w_ref, w_v, load.at[0])
    x_load = pltpu.make_async_copy(x_ref, x_v, load.at[1])
    down_load = pltpu.make_async_copy(down_ref, down_v, load.at[2])
    w_load.start()
    x_load.start()
    down_load.start()
    greet([(d_c, s), (d_x, s), (d_y, s)])
    begin, first, second, end = plane_stages(n_v, out_ref, *refs, place)
    w_load.wait()
    x_load.wait()
    width, chunk = mid_v.shape[1], 512

    def stored(row):
        tokens = pl.ds(row * (mid_v.shape[0] // rows), mid_v.shape[0] // rows)
        return pltpu.make_async_copy(mid_v.at[tokens], mid_ref.at[tokens], mid_sem.at[row])

    for row in range(rows):
        tokens = slice(row * (mid_v.shape[0] // rows), (row + 1) * (mid_v.shape[0] // rows))
        heads = heads_ref[:, tokens].T

        @pl.loop(0, width // chunk)
        def _(c):
            span = pl.ds(pl.multiple_of(c * chunk, chunk), chunk)
            weight = w_v[:, :, :, span].reshape(heads.shape[1], chunk)
            mid_v[tokens, span] = x_v[tokens, span].astype(F32) + dot(heads, weight)

        stored(row).start()
        mid = mid_v[tokens, :]
        inverse = lax.rsqrt(jnp.mean(mid * mid, axis=1, keepdims=True) + epsilon)
        n_v[tokens, :] = (mid * inverse * gain_ref[...]).astype(BF16)
        begin(row)
    down_load.wait()

    def body(g_tile, dh_tile):
        dh_tile[...] = back_product(g_tile[...], down_v[...]).astype(BF16)

    pltpu.emit_pipeline(
        body,
        grid=(g_ref.shape[0] // 512,),
        in_specs=[pl.BlockSpec((512, down_v.shape[1]), lambda i: (i, 0))],
        out_specs=[pl.BlockSpec((512, down_v.shape[0]), lambda i: (i, 0))],
    )(g_ref, dh_ref)
    first()
    second()
    end()
    for row in range(rows):
        stored(row).wait()


def plane_gather(heads, w, x, gain, g, down):
    dma, anywhere = pltpu.SemaphoreType.DMA, pl.BlockSpec(memory_space=pl.ANY)
    vmem = pl.BlockSpec(memory_space=pltpu.VMEM)
    everyone, dhidden, middle = pl.pallas_call(
        functools.partial(plane_kernel, 2),
        out_shape=[
            jax.ShapeDtypeStruct((8, *x.shape), BF16),
            jax.ShapeDtypeStruct((g.shape[0], down.shape[0]), BF16),
            jax.ShapeDtypeStruct(x.shape, F32),
        ],
        in_specs=[vmem, anywhere, anywhere, vmem, anywhere, anywhere],
        out_specs=[anywhere] * 3,
        scratch_shapes=[
            pltpu.VMEM(w.shape, BF16),
            pltpu.VMEM(x.shape, BF16),
            pltpu.VMEM(down.shape, BF16),
            pltpu.VMEM(x.shape, F32),
            pltpu.VMEM(x.shape, BF16),
            dma((3,)),
            dma((2,)),
            dma,
            dma((8, 2)),
            dma((8, 2)),
        ],
        compiler_params=pltpu.CompilerParams(
            collective_id=4, has_side_effects=True, vmem_limit_bytes=48 * 2**20
        ),
        name="plane_gather",
    )(heads, w, x, gain, g, down)
    return everyone.reshape(8 * x.shape[0], x.shape[1]), dhidden, middle


def transposed_kernel(x_ref, g_ref, out_ref):
    n_seq, n_dp, rows, _ = out_ref.shape
    total = outer_sum(x_ref[...], g_ref[...])
    for i in range(n_dp * n_seq):
        out_ref[i % n_seq, i // n_seq] = total[i * rows : (i + 1) * rows].astype(BF16)


def transposed_product(x, g, n_dp, n_seq):
    (tokens, width), wide = x.shape, g.shape[1]
    rows, tall = width // (n_dp * n_seq), 512
    return pl.pallas_call(
        transposed_kernel,
        grid=(width // tall,),
        in_specs=[
            pl.BlockSpec((tokens, tall), lambda i: (0, i)),
            pl.BlockSpec((tokens, wide), lambda i: (0, 0)),
        ],
        out_specs=pl.BlockSpec(
            (n_seq, tall // (n_seq * rows), rows, wide), lambda i: (0, i, 0, 0)
        ),
        out_shape=jax.ShapeDtypeStruct((n_seq, n_dp, rows, wide), BF16),
        compiler_params=pltpu.CompilerParams(vmem_limit_bytes=60 * 2**20),
        cost_estimate=pl.CostEstimate(
            flops=2 * tokens * width * wide,
            bytes_accessed=2 * (tokens * width + tokens * wide + width * wide),
            transcendentals=0,
        ),
        name="transposed_product",
    )(x, g)


def plane_sums(kept, leaving, rcv_c, rcv_d, rcv_x, rcv_y, sent_c, got_c, sent_p, got_p, place):
    d, s, d_c, d_x, d_y, line = place
    rows = kept.shape[1]
    low, high = pl.ds(0, rows // 2), pl.ds(rows // 2, rows // 2)

    def crossing(i, slot):
        return remote(leaving.at[slot], rcv_c.at[i], sent_c.at[i], got_c.at[i], (d_c, s))

    def merge(i):
        crossing(i, 0).wait_recv()
        plus(kept.at[i], rcv_c.at[i])

    def push(i):
        src, dst, peer = (
            (kept.at[3, low], rcv_d.at[low], d_x),
            (kept.at[3, high], rcv_d.at[high], d_y),
            (kept.at[1, low], rcv_x.at[low], d_x),
            (kept.at[2, high], rcv_y.at[high], d_y),
            (kept.at[2, low], rcv_y.at[low], d_y),
            (kept.at[1, high], rcv_x.at[high], d_x),
        )[i]
        return remote(src, dst, sent_p.at[i], got_p.at[i], (peer, s))

    def far():
        merge(3)
        push(0).start()
        push(1).start()

    def near(i):
        merge(i)
        if i:
            push(i + 1).start()

    def pass_on():
        push(0).wait_recv()
        plus(kept.at[2, low], rcv_d.at[low])
        push(4).start()
        push(1).wait_recv()
        plus(kept.at[1, high], rcv_d.at[high])
        push(5).start()

    def end():
        for i in (2, 3, 4, 5):
            push(i).wait_recv()
        plus(kept.at[0], rcv_x, rcv_y)
        for i in range(6):
            push(i).wait_send()

    return crossing, far, near, pass_on, end


def sums_scratch(rows, width):
    dma = pltpu.SemaphoreType.DMA
    buffer = lambda *lead: pltpu.VMEM((*lead, rows, width), BF16)
    return [
        buffer(4),
        buffer(2),
        buffer(4),
        buffer(),
        buffer(),
        buffer(),
        dma((4,)),
        dma((4,)),
        dma((6,)),
        dma((6,)),
    ]


ORDER = (7, 6, 3, 2, 5, 4, 1, 0)


def block_products(g_ref, g_v, g_sem, multiply):
    rows = g_v.shape[1]

    def load(turn):
        block = pl.ds(ORDER[turn] * rows, rows)
        return pltpu.make_async_copy(g_ref.at[block], g_v.at[turn % 2], g_sem.at[turn % 2])

    def product(turn, dst):
        if turn + 1 < 8:
            load(turn + 1).start()
        load(turn).wait()
        chunk = 512

        @pl.loop(0, dst.shape[1] // chunk)
        def _(c):
            span = pl.ds(pl.multiple_of(c * chunk, chunk), chunk)
            dst[:, span] = multiply(g_v[turn % 2], span).astype(BF16)

    return load, product


def plane_sum_kernel(g_ref, w_ref, h_ref, t_ref, out_ref, grad_ref, w_v, g_v, h_v, *refs):
    w_sem, g_sem, h_sem, out_sem, *refs = refs
    place = places()
    d, s, d_c, d_x, d_y, line = place
    kept, leaving = refs[:2]
    w_wait = load_rows(w_ref, w_v, w_sem, 8, 4)
    load, product = block_products(
        g_ref, g_v, g_sem, lambda g, span: back_product(g, w_v[span, :])
    )
    load(0).start()
    h_load = pltpu.make_async_copy(h_ref, h_v, h_sem)
    h_load.start()
    greet([(d_c, s), (d_x, s), (d_y, s)])
    crossing, far, near, pass_on, end = plane_sums(*refs, place)
    w_wait()

    def pair(turn, i):
        slot = turn // 2 % 2
        if turn >= 4:
            crossing(3 if slot == 0 else 1, slot).wait_send()
        product(turn, leaving.at[slot])
        crossing(i, slot).start()
        product(turn + 1, kept.at[i])

    pair(0, 3)
    far()
    pair(2, 1)
    pair(4, 2)
    near(1)
    near(2)
    pair(6, 0)
    near(0)
    h_load.wait()

    def grad_body(t_tile, grad_tile):
        grad_tile[...] = outer_sum(h_v[...], t_tile[...]).astype(BF16)

    tokens, deep = h_v.shape
    wide = 256

    def grad_tiles(first, count):
        pltpu.emit_pipeline(
            grad_body,
            grid=(count,),
            in_specs=[pl.BlockSpec((tokens, wide), lambda i: (0, first + i))],
            out_specs=[pl.BlockSpec((deep, wide), lambda i: (0, first + i))],
        )(t_ref, grad_ref)

    grad_tiles(0, 2)
    pass_on()
    grad_tiles(2, t_ref.shape[1] // wide - 2)
    end()
    out = pltpu.make_async_copy(kept.at[0], out_ref, out_sem)
    out.start()
    crossing(2, 0).wait_send()
    crossing(0, 1).wait_send()
    out.wait()


def plane_sum(g, w, h, t, rows):
    dma, anywhere = pltpu.SemaphoreType.DMA, pl.BlockSpec(memory_space=pl.ANY)
    width, deep = w.shape
    return pl.pallas_call(
        plane_sum_kernel,
        out_shape=[
            jax.ShapeDtypeStruct((rows, width), BF16),
            jax.ShapeDtypeStruct((h.shape[1], t.shape[1]), BF16),
        ],
        in_specs=[anywhere] * 4,
        out_specs=[anywhere] * 2,
        scratch_shapes=[
            pltpu.VMEM((width, deep), BF16),
            pltpu.VMEM((2, rows, deep), BF16),
            pltpu.VMEM(h.shape, BF16),
            dma,
            dma((2,)),
            dma,
            dma,
            *sums_scratch(rows, width),
        ],
        compiler_params=pltpu.CompilerParams(
            collective_id=5, has_side_effects=True, vmem_limit_bytes=62 * 2**20
        ),
        name="plane_sum",
    )(g, w, h, t)


def sigmoid(v):
    return 1.0 / (1.0 + jnp.exp(-v))


def load_rows(w_ref, w_v, sem, n_dp, n_seq):
    rows = w_v.shape[0] // (n_dp * n_seq)

    @pl.loop(0, n_dp * n_seq)
    def _(i):
        src = pl.ds(pl.multiple_of(i * rows, rows), rows)
        place = (i % n_dp) * n_seq + i // n_dp
        dst = pl.ds(pl.multiple_of(place * rows, rows), rows)
        pltpu.make_async_copy(w_ref.at[src], w_v.at[dst], sem).start()

    return pltpu.make_async_copy(w_ref, w_v, sem).wait


def gate_up_kernel(n_dp, n_seq, x_ref, dh_ref, w_ref, hidden_ref, dgu_ref, w_v, sem):
    pl.when(pl.program_id(0) == 0)(lambda: load_rows(w_ref, w_v, sem, n_dp, n_seq)())
    part = hidden_ref.shape[1]
    step = 256 if part % 256 == 0 else 128
    for c in range(0, part, step):
        first, second = slice(c, c + step), slice(part + c, part + c + step)
        gate, up = dot(x_ref[...], w_v[:, first]), dot(x_ref[...], w_v[:, second])
        dhidden = dh_ref[:, first].astype(F32)
        sig = sigmoid(gate)
        silu = gate * sig
        hidden_ref[:, first] = (silu * up).astype(BF16)
        dgu_ref[:, first] = (dhidden * up * (sig + silu * (1.0 - sig))).astype(BF16)
        dgu_ref[:, second] = (dhidden * silu).astype(BF16)


def gate_up_product(x, dhidden, w, n_dp, n_seq):
    tokens, width = x.shape
    wide = w.shape[1]
    block = 512
    span = lambda columns: pl.BlockSpec((block, columns), lambda i: (i, 0))
    return pl.pallas_call(
        functools.partial(gate_up_kernel, n_dp, n_seq),
        grid=(tokens // block,),
        in_specs=[span(width), span(wide // 2), pl.BlockSpec(memory_space=pl.ANY)],
        out_specs=[span(wide // 2), span(wide)],
        out_shape=[
            jax.ShapeDtypeStruct((tokens, wide // 2), BF16),
            jax.ShapeDtypeStruct((tokens, wide), BF16),
        ],
        scratch_shapes=[pltpu.VMEM(w.shape, BF16), pltpu.SemaphoreType.DMA],
        compiler_params=pltpu.CompilerParams(vmem_limit_bytes=56 * 2**20),
        cost_estimate=pl.CostEstimate(
            flops=2 * tokens * width * wide,
            bytes_accessed=2 * (tokens * width + width * wide + tokens * wide * 2),
            transcendentals=tokens * wide // 2,
        ),
        name="gate_up",
    )(x, dhidden, w)


def mm(a, b):
    return jnp.dot(a, b, preferred_element_type=F32)


def outer_sum(left, right):
    return lax.dot_general(left, right, (((0,), (0,)), ((), ())), preferred_element_type=F32)


def back_product(rows, weight):
    return lax.dot_general(rows, weight, (((1,), (1,)), ((), ())), preferred_element_type=F32)


def gather(x, axes):
    return lax.all_gather(x, axes, axis=0, tiled=True)


def scatter(x, axes):
    return lax.psum_scatter(x, axes, scatter_dimension=0, tiled=True)


def shards(
    tokens, lengths, w_qkv, w_out, w_gate_up, w_down, attn_gain, ffn_gain, head_gains, out_grad
):
    n_dp, n_seq = lax.axis_size("dp"), lax.axis_size("seq")
    rows, length, width = tokens.shape
    count = rows * length
    ff = w_gate_up.shape[1] // 2
    part = ff // n_dp
    wr = w_gate_up.shape[0]
    offset = lax.axis_index("seq") * length
    local_pos = offset + jnp.arange(length, dtype=jnp.int32)
    cosine, sine = rope_tables(jnp.concatenate([local_pos] * rows))
    ends = jnp.cumsum(lengths, axis=1, dtype=jnp.int32)
    start = jnp.sum(
        jnp.where(local_pos[None, :, None] >= ends[:, None, :], lengths[:, None, :], 0), axis=2
    ).reshape(1, count)
    start = jnp.broadcast_to(start, (8, count))

    full = (n_dp, n_seq) == (8, 4)
    qkv_w = w_qkv.shape[1]
    spare = width - qkv_w
    gains = jnp.concatenate([attn_gain, ffn_gain])
    gains = [jnp.pad(g, (0, spare - g.shape[0]))[None] for g in (gains, head_gains)]
    gains.append(jnp.zeros((wr - 2, spare), BF16))
    own_qkv = jnp.concatenate([w_qkv, jnp.concatenate(gains, axis=0)], axis=1)
    out_rows = w_out.shape[0]
    own_out = jnp.pad(w_out, ((0, -out_rows % 16), (0, 0)))
    all_qkv, some_out, spread = gather_weights(own_qkv, [own_out], w_gate_up, n_dp, n_seq)
    qkv_full = all_qkv.reshape(width, width)
    attn_gain_full = all_qkv[:, 0, qkv_w : qkv_w + wr].reshape(-1).astype(F32)
    ffn_gain_full = all_qkv[:, 0, qkv_w + wr : qkv_w + 2 * wr].reshape(-1).astype(F32)
    head_full = all_qkv[:, 1, qkv_w : qkv_w + head_gains.shape[0]].reshape(-1).astype(F32)

    w_down, qkv_full = lax.optimization_barrier((w_down, qkv_full))
    down_w = gather(w_down, "seq")
    cotangent_low = out_grad.reshape(count, width)

    x_rows = tokens.reshape(count, width).astype(F32)
    normed_low = norm_rows(x_rows, attn_gain_full).astype(BF16)
    projected = lax.dot_general(
        qkv_full, normed_low, (((0,), (1,)), ((), ())), preferred_element_type=F32
    )

    queries, pairs = prepare(projected, head_full[:, None], cosine, sine)
    more = [cotangent_low, some_out] if full else []
    heads_out, lse, held, *planes = attend(start, queries, pairs, rows, n_seq, more, out_rows)
    gate_up_w = gather(spread.reshape(n_dp * wr, 2 * part), "seq")
    if full:
        cotangent_all, all_out, heads_full = planes
        cotangent_all = cotangent_all.reshape(n_dp * count, width)
        out_full = all_out.reshape(-1, width)
        normed2_all, dhidden, middle = plane_gather(
            heads_full, all_out, tokens.reshape(count, width), ffn_gain_full[None],
            cotangent_all, down_w,
        )
    else:
        cotangent_all, all_out = gather(cotangent_low, "dp"), some_out
        out_full = all_out.reshape(-1, width)
        fill = ((0, 0), (0, all_out.shape[1] - out_rows), (0, 0))
        heads_full = jnp.pad(heads_out.reshape(n_dp * n_seq, out_rows, count), fill)
        heads_full = heads_full.reshape(-1, count)
        middle = x_rows + outer_sum(heads_full, out_full)
        normed2_all = gather(norm_rows(middle, ffn_gain_full).astype(BF16), "dp")
        dhidden = back_product(cotangent_all, down_w).astype(BF16)
    hidden, dgate_up = gate_up_product(normed2_all, dhidden, gate_up_w, n_dp, n_seq)
    gate_up_grad = transposed_product(normed2_all, dgate_up, n_dp, n_seq)
    gate_up_grad, dgate_up = lax.optimization_barrier((gate_up_grad, dgate_up))
    gate_up_grad = scatter(gate_up_grad.reshape(width, 2 * part), "seq")
    if full:
        dnormed2, down_grad = plane_sum(dgate_up, gate_up_w, hidden, cotangent_all, count)
    else:
        ordered = gate_up_w.reshape(n_seq, n_dp, wr, 2 * part).transpose(1, 0, 2, 3)
        ordered = ordered.reshape(width, 2 * part)
        dnormed2 = scatter(back_product(dgate_up, ordered).astype(BF16), "dp")
        down_grad = outer_sum(hidden, cotangent_all).astype(BF16)
    dnormed2 = dnormed2.astype(F32)

    dmiddle = cotangent_low.astype(F32) + normed_back(dnormed2, middle, ffn_gain_full)
    dattend = dmiddle.astype(BF16)
    dheads = back_product(out_full, dattend).astype(BF16).reshape(n_dp * n_seq, -1, count)
    dheads = dheads[:, :out_rows].reshape(QW, count)
    if full:
        dqueries, dpairs, mixed = attend_back(
            start, queries, dheads, heads_out, lse, pairs, held, rows, n_seq,
            [hidden, down_w, middle],
        )
    else:
        dqueries, dpairs = attend_back(
            start, queries, dheads, heads_out, lse, pairs, held, rows, n_seq, []
        )
        mixed = middle + scatter(mm(hidden, down_w).astype(BF16), "dp").astype(F32)
    gate_up_grad, dqueries = lax.optimization_barrier((gate_up_grad, dqueries))
    gate_up_grad = gate_up_grad.reshape(n_dp, wr, 2 * part)
    down_grad, dqueries = lax.optimization_barrier((down_grad, dqueries))
    down_grad = scatter(down_grad, "seq")
    dprojected_low, head_grad = prepare_back(
        projected, head_full[:, None], cosine, sine, dqueries, dpairs
    )
    few = head_gains.shape[0]
    if full:
        few_rows = jnp.pad(head_grad.reshape(-1, few, 1), ((0, 0), (0, 16 - few), (0, 0)))
        few_rows = jnp.broadcast_to(few_rows.astype(BF16), (n_dp * n_seq, 16, width - qkv_w))
        qkv_grad, head_rows_out, qkv_products, out_weight_grad, tokens_grad, gate_up_grad, ffn_products = (
            sum_weights(
                normed_low,
                dprojected_low,
                heads_full,
                dattend,
                few_rows,
                own_qkv,
                qkv_full,
                tokens.reshape(count, width),
                dmiddle,
                attn_gain_full[None],
                gate_up_grad,
                w_gate_up,
            )
        )
        head_out, ffn_products, qkv_products = (
            head_rows_out[:few, 0], ffn_products[:, 0], qkv_products[:, 0]
        )
    else:
        qkv_grad = lax.dot_general(
            normed_low, dprojected_low, (((0,), (1,)), ((), ())), preferred_element_type=F32
        ).astype(BF16)
        out_grads = mm(heads_full, dattend).astype(BF16)
        qkv_grad, out_weight_grad = (
            scatter(scatter(g, "dp"), "seq").astype(F32) for g in (qkv_grad, out_grads)
        )
        head_out = jnp.sum(
            lax.all_to_all(head_grad.reshape(-1, few), BOTH, 0, 0, tiled=True), axis=0
        )
        qkv_products = jnp.sum(own_qkv[:, :qkv_w].astype(F32) * qkv_grad[:, :qkv_w], axis=1)
        qkv_grad = qkv_grad[:, :qkv_w]
        gate_up_grad = lax.all_to_all(gate_up_grad, "dp", 0, 0, tiled=True)
        gate_up_grad = gate_up_grad.reshape(n_dp, wr, 2, part).transpose(1, 2, 0, 3)
        gate_up_grad = gate_up_grad.reshape(wr, 2 * ff).astype(F32)
        ffn_products = jnp.sum(w_gate_up.astype(F32) * gate_up_grad, axis=1)
        dnormed = back_product(dprojected_low.T, qkv_full)
        tokens_grad = dmiddle + normed_back(dnormed, x_rows, attn_gain_full)
    attn_gain_out = qkv_products / attn_gain.astype(F32)
    ffn_gain_out = ffn_products / ffn_gain.astype(F32)
    return (
        mixed.astype(BF16).reshape(rows, length, width),
        tokens_grad.reshape(rows, length, width),
        qkv_grad,
        out_weight_grad[:out_rows],
        gate_up_grad,
        down_grad.astype(F32),
        attn_gain_out,
        ffn_gain_out,
        head_out,
    )


def solution(mesh):
    in_specs = (
        P("dp", "seq", None),
        P("dp", None),
        P(("dp", "seq"), None),
        P(("dp", "seq"), None),
        P(("dp", "seq"), None),
        P(("dp", "seq"), None),
        P(("dp", "seq")),
        P(("dp", "seq")),
        P(("dp", "seq")),
        P("dp", "seq", None),
    )
    out_specs = (
        P("dp", "seq", None),
        P("dp", "seq", None),
        P(("dp", "seq"), None),
        P(("dp", "seq"), None),
        P(("dp", "seq"), None),
        P(("dp", "seq"), None),
        P(("dp", "seq")),
        P(("dp", "seq")),
        P(("dp", "seq")),
    )
    return jax.shard_map(shards, mesh=mesh, in_specs=in_specs, out_specs=out_specs, check_vma=False)
```

```python
import functools

import jax
import jax.numpy as jnp
from jax import lax
from jax.experimental import pallas as pl
from jax.experimental.pallas import tpu as pltpu
from jax.sharding import PartitionSpec as P

QUERY_HEADS = 20
KEY_VALUE_HEADS = 5
HEAD_SIZE = 64
GROUP = QUERY_HEADS // KEY_VALUE_HEADS
QW = QUERY_HEADS * HEAD_SIZE
KW = KEY_VALUE_HEADS * HEAD_SIZE
BOTH = ("dp", "seq")

epsilon = 1e-06
F32 = jnp.float32
BF16 = jnp.bfloat16
MESH = pl.DeviceIdType.MESH


def norm_rows(inputs, scales):
    return inputs * lax.rsqrt(jnp.mean(inputs * inputs, axis=-1, keepdims=True) + epsilon) * scales


def rope_tables(positions):
    inverse_freq = 10000.0 ** (-(jnp.arange(HEAD_SIZE // 2, dtype=F32) * 2.0 / HEAD_SIZE))
    angles = inverse_freq[:, None] * positions.astype(F32)[None, :]
    return (jnp.cos(angles), jnp.sin(angles))


def head_rows(i):
    return pl.ds(pl.multiple_of(i * HEAD_SIZE, HEAD_SIZE), HEAD_SIZE)


def key_rows(i):
    return head_rows(2 * i), head_rows(2 * i + 1)


def unit(v):
    inverse = lax.rsqrt(jnp.mean(v * v, axis=0, keepdims=True) + epsilon)
    return v * inverse, inverse


def prepare_kernel(p_ref, gain_ref, cos_ref, sin_ref, q_ref, kv_ref):
    cosine, sine = cos_ref[...], sin_ref[...]

    def turned(v, gain):
        v = unit(v)[0] * gain
        first, second = v[: HEAD_SIZE // 2], v[HEAD_SIZE // 2 :]
        return jnp.concatenate(
            [first * cosine - second * sine, second * cosine + first * sine], axis=0
        )

    @pl.loop(0, KEY_VALUE_HEADS)
    def _(i):
        key, value = key_rows(i)
        keys_in = p_ref[head_rows(QUERY_HEADS + i), :]
        kv_ref[key, :] = turned(keys_in, gain_ref[HEAD_SIZE:, :]).astype(BF16)
        values_in = p_ref[head_rows(QUERY_HEADS + KEY_VALUE_HEADS + i), :]
        kv_ref[value, :] = values_in.astype(BF16)

    @pl.loop(0, QUERY_HEADS)
    def _(i):
        rows = head_rows(i)
        queries = turned(p_ref[rows, :], gain_ref[:HEAD_SIZE, :]) * HEAD_SIZE**-0.5
        q_ref[rows, :] = queries.astype(BF16)


def prepare(projected, gains, cosine, sine):
    tokens = projected.shape[1]
    return pl.pallas_call(
        prepare_kernel,
        out_shape=[
            jax.ShapeDtypeStruct((QW, tokens), BF16),
            jax.ShapeDtypeStruct((2 * KW, tokens), BF16),
        ],
        compiler_params=pltpu.CompilerParams(vmem_limit_bytes=40 * 2**20),
        name="prepare",
    )(projected, gains, cosine, sine)


def prepare_back_kernel(p_ref, gain_ref, cos_ref, sin_ref, dq_ref, dkv_ref, out_ref, dg_ref, acc):
    cosine, sine = cos_ref[...], sin_ref[...]
    acc[...] = jnp.zeros_like(acc)

    def back(v, gain, dy, lines):
        u, inverse = unit(v)
        first, second = dy[: HEAD_SIZE // 2], dy[HEAD_SIZE // 2 :]
        dz = jnp.concatenate(
            [first * cosine + second * sine, second * cosine - first * sine], axis=0
        )
        acc[lines, :] += dz * u
        du = dz * gain
        return inverse * (du - u * jnp.mean(du * u, axis=0, keepdims=True))

    @pl.loop(0, KEY_VALUE_HEADS)
    def _(i):
        key, value = key_rows(i)
        rows = head_rows(QUERY_HEADS + i)
        dv = back(p_ref[rows, :], gain_ref[HEAD_SIZE:, :], dkv_ref[key, :], slice(HEAD_SIZE, None))
        out_ref[rows, :] = dv.astype(BF16)
        out_ref[head_rows(QUERY_HEADS + KEY_VALUE_HEADS + i), :] = dkv_ref[value, :].astype(BF16)

    @pl.loop(0, QUERY_HEADS)
    def _(i):
        rows = head_rows(i)
        dy = dq_ref[rows, :] * HEAD_SIZE**-0.5
        dv = back(p_ref[rows, :], gain_ref[:HEAD_SIZE, :], dy, slice(0, HEAD_SIZE))
        out_ref[rows, :] = dv.astype(BF16)

    rest = out_ref.shape[0] - QW - 2 * KW
    out_ref[QW + 2 * KW :, :] = jnp.zeros((rest, out_ref.shape[1]), BF16)
    total = jnp.sum(acc[...], axis=1, keepdims=True)
    dg_ref[...] = jnp.broadcast_to(total, dg_ref.shape)


def prepare_back(projected, gains, cosine, sine, dqueries, dpairs):
    tokens = projected.shape[1]
    dprojected, dgains = pl.pallas_call(
        prepare_back_kernel,
        out_shape=[
            jax.ShapeDtypeStruct(projected.shape, BF16),
            jax.ShapeDtypeStruct((2 * HEAD_SIZE, 128), F32),
        ],
        scratch_shapes=[pltpu.VMEM((2 * HEAD_SIZE, tokens), F32)],
        compiler_params=pltpu.CompilerParams(vmem_limit_bytes=40 * 2**20),
        name="prepare_back",
    )(projected, gains, cosine, sine, dqueries, dpairs)
    return dprojected, dgains[:, 0]


def dot(a, b):
    return jnp.dot(a, b, preferred_element_type=F32)


def places():
    d, s = lax.axis_index("dp"), lax.axis_index("seq")
    core, column, line = d % 2, (d // 2) % 2, d // 4
    return d, s, d + 1 - 2 * core, d + 2 - 4 * column, d + 4 - 8 * line, line


def greet(peers, line=None):
    barrier = pltpu.get_barrier_semaphore()

    def signal(peer):
        pl.semaphore_signal(barrier, inc=1, device_id=peer, device_id_type=MESH)

    for peer in peers:
        signal(peer)
    if line is None:
        pl.semaphore_wait(barrier, len(peers))
        return
    d, s = line
    last = lax.axis_size("seq") - 1
    pl.when(s < last)(lambda: signal((d, s + 1)))
    pl.when(s > 0)(lambda: signal((d, s - 1)))
    pl.semaphore_wait(barrier, len(peers) + 1 - s // last + (s + last - 1) // last)


def remote(src, dst, sent, got, peer):
    return pltpu.make_async_remote_copy(
        src_ref=src,
        dst_ref=dst,
        send_sem=sent,
        recv_sem=got,
        device_id=peer,
        device_id_type=MESH,
    )


def plane_stages(x_ref, out_ref, own_sem, sent, got, place, ordered=False):
    d, s, d_c, d_x, d_y, line = place
    flip, d_d = d_c - d, d_x + d_y - d
    slots = list(range(8))
    if ordered:
        slots = [d, d_c, d_x, d_x + flip, d_y, d_y + flip, d_d, d_d + flip]
    half = x_ref.shape[0] // 2
    halves = (pl.ds(0, half), pl.ds(half, half))
    source = {1: 0, 2: 0, 4: 0, 3: 2, 5: 4, 7: 6}

    def piece(k, h, peer):
        back = source[k] if k in source else (4 if h == 0 else 2)
        src = x_ref.at[halves[h]] if back == 0 else out_ref.at[slots[back], halves[h]]
        dst = out_ref.at[slots[back] if ordered else k, halves[h]]
        return remote(src, dst, sent.at[k, h], got.at[k, h], (peer, s))

    own = pltpu.make_async_copy(x_ref, out_ref.at[slots[0]], own_sem)

    def begin(h):
        for k, peer in ((2, d_x), (4, d_y), (1, d_c)):
            piece(k, h, peer).start()
        if h:
            own.start()

    def first():
        piece(4, 0, d_y).wait_recv()
        piece(6, 0, d_x).start()
        piece(5, 0, d_c).start()
        piece(2, 0, d_x).wait_recv()
        piece(3, 0, d_c).start()

    def second():
        piece(2, 1, d_x).wait_recv()
        piece(6, 1, d_y).start()
        piece(3, 1, d_c).start()
        piece(4, 1, d_y).wait_recv()
        piece(5, 1, d_c).start()

    def end():
        for h in (0, 1):
            piece(6, h, d_x).wait_recv()
            piece(7, h, d_c).start()
        for k in (1, 3, 5, 7):
            for h in (0, 1):
                piece(k, h, d_c).wait_recv()
        for k in range(1, 8):
            for h in (0, 1):
                piece(k, h, d_c).wait_send()
        own.wait()

    return begin, first, second, end


def abreast(block):
    return jnp.concatenate(
        [block[i * HEAD_SIZE : (i + 1) * HEAD_SIZE] for i in range(GROUP)], axis=1
    )


def across(rows):
    return jnp.concatenate([rows[i : i + 1] for i in range(GROUP)], axis=1)


def seen(back, me, start):
    length = start.shape[1]
    key = lax.broadcasted_iota(jnp.int32, (length, length), 0)
    found = key + (me - back) * length >= start
    if back == 0:
        found &= key <= lax.broadcasted_iota(jnp.int32, (length, length), 1)
    bias = jnp.where(found, 0.0, -1e30)
    return jnp.concatenate([bias] * GROUP, axis=1)


def spans(i, length):
    row, head = i // KEY_VALUE_HEADS, i % KEY_VALUE_HEADS
    wide, pair = GROUP * HEAD_SIZE, 2 * HEAD_SIZE
    tokens = pl.ds(pl.multiple_of(row * length, length), length)
    return (
        tokens,
        pl.ds(pl.multiple_of(head * wide, wide), wide),
        pl.ds(pl.multiple_of(head * pair, pair), pair),
        head,
    )


def attend_kernel(n, rows, planes, out_rows, start_ref, q_ref, kv_ref, *refs):
    x_refs, refs = refs[:planes], refs[planes:]
    o_ref, lse_ref, held, *refs = refs
    out_refs, refs = refs[:planes], refs[planes:]
    if planes:
        full_ref, filled, *refs = refs
    o_acc, l_acc, sent, got, *refs = refs
    d, me = lax.axis_index("dp"), lax.axis_index("seq")
    length = q_ref.shape[1] // rows
    if planes:
        place = places()
        d, me, d_c, d_x, d_y, _ = place
        greet([(d_c, me), (d_x, me), (d_y, me)], (d, me))
        each = [
            plane_stages(x_refs[i], out_refs[i], *refs[3 * i : 3 * i + 3], place, i > 0)
            for i in range(planes)
        ]
    else:
        greet([], (d, me))
        each = []

    def climb(step, head):
        lines = pl.ds(head * 2 * HEAD_SIZE, 2 * HEAD_SIZE)
        src = kv_ref.at[lines] if step == 1 else held.at[step - 2, lines]
        dst = held.at[step - 1, lines]
        return remote(src, dst, sent.at[step - 1, head], got.at[step - 1, head], (d, me + 1))

    heads = range(KEY_VALUE_HEADS)

    def climbs(step):
        for head in heads:
            climb(step, head).start()

    def level(back):
        @pl.loop(0, rows * KEY_VALUE_HEADS, unroll=KEY_VALUE_HEADS)
        def _(i):
            tokens, wide, pair, head = spans(i, length)
            block = kv_ref[pair, tokens] if back == 0 else held[back - 1, pair, tokens]
            keys, values = block[:HEAD_SIZE].T, block[HEAD_SIZE:]
            bias = seen(back, me, start_ref[0:1, tokens])
            p = jnp.exp(dot(keys, abreast(q_ref[wide, tokens])) + bias)
            total = jnp.sum(p, axis=0, keepdims=True)
            out = dot(values, p.astype(BF16))
            for g in range(GROUP):
                own = slice(g * length, (g + 1) * length)
                line = slice(g, g + 1)
                part = pl.ds(wide.start + g * HEAD_SIZE, HEAD_SIZE)
                if back == 0:
                    l_acc[head, line, tokens] = total[:, own]
                    o_acc[part, tokens] = out[:, own]
                else:
                    l_acc[head, line, tokens] += total[:, own]
                    o_acc[part, tokens] += out[:, own]

    pl.when(me < n - 1)(lambda: climbs(1))
    for stages in each:
        stages[0](0)
        stages[0](1)
    level(0)
    for back in range(1, n):

        def step(back=back):
            for head in heads:
                climb(back, head).wait_recv()
                if back < n - 1:
                    pl.when(me < n - 1)(lambda head=head: climb(back + 1, head).start())
            level(back)

        pl.when(me >= back)(step)
        if back <= 2:
            for stages in each:
                stages[back]()

    @pl.loop(0, rows * KEY_VALUE_HEADS)
    def _(i):
        tokens, wide, pair, head = spans(i, length)
        for g in range(GROUP):
            line = slice(g, g + 1)
            part = pl.ds(wide.start + g * HEAD_SIZE, HEAD_SIZE)
            out = o_acc[part, tokens] / l_acc[head, line, tokens]
            o_acc[part, tokens] = out
            o_ref[part, tokens] = out.astype(BF16)
            lse_ref[head, line, tokens] = jnp.log(l_acc[head, line, tokens])

    if planes:
        tall = full_ref.shape[0] // 32
        filled[...] = jnp.zeros_like(filled)

        @pl.loop(0, 32)
        def _(i):
            src = pl.ds(pl.multiple_of(i * out_rows, 8), out_rows)
            dst = pl.ds(pl.multiple_of(i * tall, 8), out_rows)
            filled[dst, :] = o_acc[src, :]

        full_ref[...] = filled[...].astype(BF16)

    for back in range(1, n):
        for head in heads:
            pl.when((me >= back - 1) & (me < n - 1))(
                lambda back=back, head=head: climb(back, head).wait_send()
            )
    for stages in each:
        stages[3]()


def attend(start, queries, pairs, rows, n, more, out_rows):
    vmem, dma = pl.BlockSpec(memory_space=pltpu.VMEM), pltpu.SemaphoreType.DMA
    anywhere = pl.BlockSpec(memory_space=pl.ANY)
    count = queries.shape[1]
    lines = (KEY_VALUE_HEADS, 8, count)
    out_shape = [
        jax.ShapeDtypeStruct(queries.shape, BF16),
        jax.ShapeDtypeStruct(lines, F32),
        jax.ShapeDtypeStruct((n - 1, *pairs.shape), BF16),
    ]
    scratch, full = [], []
    if more:
        full = [(QW // out_rows * more[1].shape[1], count)]
        scratch.append(pltpu.VMEM(full[0], F32))
    scratch += [
        pltpu.VMEM(queries.shape, F32),
        pltpu.VMEM(lines, F32),
        dma((n - 1, KEY_VALUE_HEADS)),
        dma((n - 1, KEY_VALUE_HEADS)),
    ]
    for extra in more:
        out_shape.append(jax.ShapeDtypeStruct((8, *extra.shape), BF16))
        scratch += [dma, dma((8, 2)), dma((8, 2))]
    out_shape += [jax.ShapeDtypeStruct(shape, BF16) for shape in full]
    return pl.pallas_call(
        functools.partial(attend_kernel, n, rows, len(more), out_rows),
        in_specs=[vmem] * 3 + [anywhere] * len(more),
        out_specs=[vmem] * 3 + [anywhere] * len(more) + [vmem] * len(full),
        out_shape=out_shape,
        scratch_shapes=scratch,
        compiler_params=pltpu.CompilerParams(
            collective_id=2, has_side_effects=True, vmem_limit_bytes=48 * 2**20
        ),
        name="attend",
    )(start, queries, pairs, *more)


def plus(ref, *others):
    total = ref[...].astype(F32)
    for other in others:
        total += other[...].astype(F32)
    ref[...] = total.astype(BF16)


def attend_back_kernel(n, rows, summed, *refs):
    start_ref, q_ref, do_ref, o_ref, lse_ref, kv_ref, held, *refs = refs
    if summed:
        h_ref, w_ref, m_ref, *refs = refs
    dq_ref, dkv_ref, *refs = refs
    if summed:
        mixed_ref, *refs = refs
    inner, part, rcv, sent, got, *refs = refs
    d, me = lax.axis_index("dp"), lax.axis_index("seq")
    length = q_ref.shape[1] // rows
    if summed:
        place = places()
        d, me, d_c, d_x, d_y, _ = place
        w_v, h_v, m_v, w_sem, h_sem, m_sem, *refs = refs
        kept, leaving = refs[:2]
        m_load = pltpu.make_async_copy(m_ref, m_v, m_sem)
        load, product = block_products(h_ref, h_v, h_sem, lambda h, span: dot(h, w_v[:, span]))
        load(0).start()
        w_load = pltpu.make_async_copy(w_ref, w_v, w_sem)
        w_load.start()
        greet([(d_c, me), (d_x, me), (d_y, me)], (d, me))
        crossing, far, near, pass_on, end = plane_sums(*refs, place)

        def pair(turn, i):
            slot = turn // 2 % 2
            if turn >= 4:
                crossing(3 if slot == 0 else 1, slot).wait_send()
            product(turn, leaving.at[slot])
            crossing(i, slot).start()
            product(turn + 1, kept.at[i])

        def stage(i):
            if i == 0:
                w_load.wait()
                m_load.start()
                pair(0, 3)
                far()
            elif i == 1:
                pair(2, 1)
                near(1)
                pair(4, 2)
                near(2)
                pair(6, 0)
                near(0)
            elif i == 2:
                pass_on()
            else:
                end()
                m_load.wait()
                mixed_ref[...] = (kept[0].astype(F32) + m_v[...]).astype(BF16)
                crossing(2, 0).wait_send()
                crossing(0, 1).wait_send()
    else:
        greet([], (d, me))

        def stage(i):
            pass

    def descend(back):
        return remote(
            part.at[back - 1], rcv.at[back - 1], sent.at[back - 1], got.at[back - 1], (d, me - 1)
        )

    def level(back):
        @pl.loop(0, rows * KEY_VALUE_HEADS, unroll=2)
        def _(i):
            tokens, wide, pair, head = spans(i, length)
            block = kv_ref[pair, tokens] if back == 0 else held[back - 1, pair, tokens]
            keys_t = block[:HEAD_SIZE]
            keys, values = keys_t.T, block[HEAD_SIZE:].T
            q, do = abreast(q_ref[wide, tokens]), abreast(do_ref[wide, tokens])
            bias = seen(back, me, start_ref[0:1, tokens])
            p = jnp.exp(dot(keys, q) + (bias - across(lse_ref[head, :, tokens])))
            ds = (p * (dot(values, do) - across(inner[head, :, tokens]))).astype(BF16)
            dv = back_product(p.astype(BF16), do)
            dk = back_product(ds, q)
            dq = dot(keys_t, ds)
            if back == 0:
                dkv_ref[pair, tokens] = jnp.concatenate([dk.T, dv.T], axis=0)
            else:
                part[back - 1, pair, tokens] = jnp.concatenate([dk.T, dv.T], axis=0).astype(BF16)
            for g in range(GROUP):
                own = slice(g * length, (g + 1) * length)
                line = pl.ds(wide.start + g * HEAD_SIZE, HEAD_SIZE)
                dq_ref[line, tokens] += dq[:, own]

    def finish(back):
        def more():
            descend(back + 1).wait_recv()
            if back == 0:
                dkv_ref[...] += rcv[0].astype(F32)
            else:
                plus(part.at[back - 1], rcv.at[back])

        if back < n - 1:
            pl.when(me < n - 1)(more)
        if back > 0:
            descend(back).start()

    stage(0)
    dq_ref[...] = jnp.zeros_like(dq_ref)

    @pl.loop(0, rows * KEY_VALUE_HEADS)
    def _(i):
        tokens, wide, pair, head = spans(i, length)
        for g in range(GROUP):
            line = slice(g, g + 1)
            own = pl.ds(wide.start + g * HEAD_SIZE, HEAD_SIZE)
            product = do_ref[own, tokens].astype(F32) * o_ref[own, tokens].astype(F32)
            inner[head, line, tokens] = jnp.sum(product, axis=0, keepdims=True)

    for back in range(n - 1, -1, -1):

        def run(back=back):
            level(back)
            pl.when(me == n - 1)(lambda: finish(back))

        if back:
            pl.when(me >= back)(run)
        else:
            level(0)
            pl.when(me == n - 1)(lambda: finish(0))
        if back + 1 < n - 1:
            pl.when((me >= back + 1) & (me < n - 1))(lambda back=back: finish(back + 1))
        if n - 1 - back in (1, 2):
            stage(n - 1 - back)
    pl.when(me < n - 1)(lambda: finish(0))
    stage(3)
    for back in range(1, n):
        pl.when(me >= back)(lambda back=back: descend(back).wait_send())


def attend_back(start, queries, dheads, heads, lse, pairs, held, rows, n, more):
    vmem, dma = pl.BlockSpec(memory_space=pltpu.VMEM), pltpu.SemaphoreType.DMA
    anywhere = pl.BlockSpec(memory_space=pl.ANY)
    count = queries.shape[1]
    out_shape = [
        jax.ShapeDtypeStruct(queries.shape, F32),
        jax.ShapeDtypeStruct(pairs.shape, F32),
    ]
    scratch = [
        pltpu.VMEM((KEY_VALUE_HEADS, 8, count), F32),
        pltpu.VMEM((n - 1, *pairs.shape), BF16),
        pltpu.VMEM((n - 1, *pairs.shape), BF16),
        dma((n - 1,)),
        dma((n - 1,)),
    ]
    if more:
        (tokens, deep), (_, width) = more[0].shape, more[1].shape
        block = tokens // 8
        out_shape.append(jax.ShapeDtypeStruct((block, width), BF16))
        scratch += [
            pltpu.VMEM((deep, width), BF16),
            pltpu.VMEM((2, block, deep), BF16),
            pltpu.VMEM((block, width), F32),
            dma,
            dma((2,)),
            dma,
            *sums_scratch(block, width),
        ]
    return pl.pallas_call(
        functools.partial(attend_back_kernel, n, rows, bool(more)),
        in_specs=[vmem] * 7 + [anywhere] * len(more),
        out_specs=[vmem] * len(out_shape),
        out_shape=out_shape,
        scratch_shapes=scratch,
        compiler_params=pltpu.CompilerParams(
            collective_id=3, has_side_effects=True, vmem_limit_bytes=62 * 2**20
        ),
        name="attend_back",
    )(start, queries, dheads, heads, lse, pairs, held, *more)


def weights_kernel(n, *refs):
    x_refs, (w_ref, *out_refs), refs = refs[:n], refs[n : 2 * n + 1], refs[2 * n + 1 :]
    spread_ref, own_sem, recv, send_z, send_x, send_y, send_d, send_c, own_w, sent_w, got_w = refs
    d, s, d_c, d_x, d_y, line = places()
    d_d = d_x + 4 - 8 * line
    flip = d_c - d
    plane = (d, d_c, d_x, d_x + flip, d_y, d_y + flip, d_d, d_d + flip)
    greet([(other, s) for other in plane[1:]], (d, s))
    part = spread_ref.shape[2] // 2

    def columns(k, half):
        begin = half * 8 * part + plane[k] * part
        src = w_ref.at[:, pl.ds(pl.multiple_of(begin, 128), part)]
        dst = spread_ref.at[d, :, pl.ds(half * part, part)]
        if k == 0:
            return pltpu.make_async_copy(src, dst, own_w.at[half])
        return remote(src, dst, sent_w.at[k, half], got_w.at[k, half], (plane[k], s))

    def copies(slot, sent, got, peer, own=False, many=1):
        return [
            remote(
                x_refs[i] if own else out_refs[i].at[slot if i == 0 else slot % 4],
                out_refs[i].at[slot if i == 0 else slot % 4],
                sent(i),
                got(i),
                peer,
            )
            for i in range(many)
        ]

    def start(group):
        for one in group:
            one.start()

    def sent(group):
        for one in group:
            one.wait_send()

    def each(visit, between=lambda: None):
        visit(s, 0)
        between()
        for far in (1, 2, 3):
            pl.when(s >= far)(lambda far=far: visit(s - far, 1))
            pl.when(s + far <= 3)(lambda far=far: visit(s + far, -1))

    def got(k, b):
        return lambda i: recv.at[i, k, b]

    def arrived(k, b):
        many = 1 if k else n
        for one in copies(d * 4 + b, lambda i: send_x.at[i, b], got(k, b), (d_x, s), many=many):
            one.wait_recv()

    own = [
        pltpu.make_async_copy(x_refs[i], out_refs[i].at[d * 4 + s if i == 0 else s], own_sem.at[i])
        for i in range(n)
    ]
    start(own)

    def up(b, own=False):
        return copies(d * 4 + b, lambda i: send_z.at[i, 0, b], got(0, b), (d, s + 1), own, n)

    def down(b, own=False):
        return copies(d * 4 + b, lambda i: send_z.at[i, 1, b], got(0, b), (d, s - 1), own, n)

    def spread(b, own=False):
        return (
            copies(d * 4 + b, lambda i: send_x.at[i, b], got(2, b), (d_x, s), own)
            + copies(d * 4 + b, lambda i: send_y.at[i, b], got(4, b), (d_y, s), own)
            + copies(d * 4 + b, lambda i: send_c.at[i, 0, b], got(1, b), (d_c, s), own)
        )

    def column_block(b, direction):
        own = direction == 0
        if direction:
            arrived(0, b)
        if direction >= 0:
            pl.when(s < 3)(lambda: start(up(b, own)))
        if direction <= 0:
            pl.when(s > 0)(lambda: start(down(b, own)))
        start(spread(b, own))

    def start_columns():
        for k in range(8):
            for half in (0, 1):
                columns(k, half).start()

    each(column_block, start_columns)

    def over_y(b):
        return copies(d_x * 4 + b, lambda i: send_d.at[i, b], got(6, b), (d_y, s))

    def over_x(b):
        return copies(d_y * 4 + b, lambda i: send_d.at[i, b], got(6, b), (d_x, s))

    def to_core(index, holder, b):
        return copies(
            holder * 4 + b, lambda i: send_c.at[i, index, b], got(2 * index + 1, b), (d_c, s)
        )

    def side_blocks(b, direction):
        arrived(2, b)
        pl.when(b % 2 == 0)(lambda: start(over_y(b)))
        start(to_core(1, d_x, b))
        arrived(4, b)
        pl.when(b % 2 == 1)(lambda: start(over_x(b)))
        start(to_core(2, d_y, b))

    each(side_blocks)

    def far_block(b, direction):
        arrived(6, b)
        start(to_core(3, d_d, b))

    each(far_block)

    def finish(b, direction):
        for k in (1, 3, 5, 7):
            arrived(k, b)
        if direction >= 0:
            pl.when(s < 3)(lambda: sent(up(b)))
        if direction <= 0:
            pl.when(s > 0)(lambda: sent(down(b)))
        sent(spread(b))
        sent(over_y(b))
        sent(to_core(1, d_x, b))
        sent(to_core(2, d_y, b))
        sent(to_core(3, d_d, b))

    each(finish)
    for one in own:
        one.wait()
    for k in range(8):
        for half in (0, 1):
            if k:
                columns(k, half).wait_recv()
                columns(k, half).wait_send()
            else:
                columns(k, half).wait()


def gather_weights(first, others, wide, n_dp, n_seq):
    rows, part = wide.shape[0], wide.shape[1] // (2 * n_dp)
    if (n_dp, n_seq) != (8, 4):
        spread = lax.all_to_all(wide.reshape(rows, 2, n_dp, part), "dp", 2, 0, tiled=False)
        spread = spread.reshape(n_dp, rows, 2 * part)
        return [lax.all_gather(x, BOTH, axis=0, tiled=False) for x in (first, *others)] + [spread]
    arrays = [first, *others]
    n = len(arrays)
    dma = pltpu.SemaphoreType.DMA
    return pl.pallas_call(
        functools.partial(weights_kernel, n),
        out_shape=[
            jax.ShapeDtypeStruct((n_seq if i else n_dp * n_seq, *x.shape), x.dtype)
            for i, x in enumerate(arrays)
        ]
        + [jax.ShapeDtypeStruct((n_dp, rows, 2 * part), wide.dtype)],
        in_specs=[pl.BlockSpec(memory_space=pl.ANY)] * (n + 1),
        out_specs=[pl.BlockSpec(memory_space=pl.ANY)] * (n + 1),
        scratch_shapes=[
            dma((n,)),
            dma((n, 8, 4)),
            dma((n, 2, 4)),
            dma((n, 4)),
            dma((n, 4)),
            dma((n, 4)),
            dma((n, 4, 4)),
            dma((2,)),
            dma((8, 2)),
            dma((8, 2)),
        ],
        compiler_params=pltpu.CompilerParams(collective_id=1, has_side_effects=True),
        name="gather_weights",
    )(*arrays, wide)


def weight_sums(product, refs, place):
    kept, leaving, rcv_c, rcv_d, rcv_x, rcv_y, rcv_z = refs[:7]
    sent_c, got_c, sent_p, got_p, sent_z, got_z = refs[7:]
    d, s, d_c, d_x, d_y, line = place
    holders = (d, d_x, d_y, d_x + d_y - d)
    flip = d_c - d
    low, high = pl.ds(0, 2), pl.ds(2, 2)

    def crossing(i, slot):
        return remote(leaving.at[slot], rcv_c.at[i], sent_c.at[i], got_c.at[i], (d_c, s))

    def pair(i, slot, before=None):
        if before is not None:
            crossing(before, slot).wait_send()
        product(holders[i] + flip, leaving.at[slot])
        crossing(i, slot).start()
        product(holders[i], kept.at[i])

    def merge(i):
        crossing(i, 0).wait_recv()
        plus(kept.at[i], rcv_c.at[i])

    def push(i):
        src, dst, peer = (
            (kept.at[3, low], rcv_d.at[low], d_x),
            (kept.at[3, high], rcv_d.at[high], d_y),
            (kept.at[1, low], rcv_x.at[low], d_x),
            (kept.at[2, high], rcv_y.at[high], d_y),
            (kept.at[2, low], rcv_y.at[low], d_y),
            (kept.at[1, high], rcv_x.at[high], d_x),
        )[i]
        return remote(src, dst, sent_p.at[i], got_p.at[i], (peer, s))

    def straight(b):
        return remote(kept.at[0, b], rcv_z.at[s], sent_z.at[b], got_z.at[s], (d, b))

    def from_line(b):
        return remote(kept.at[0, b], rcv_z.at[b], sent_z.at[b], got_z.at[b], (d, b))

    def far():
        pair(3, 0)
        pair(1, 1)
        merge(3)
        push(0).start()
        push(1).start()

    def near():
        pair(2, 0, 3)
        pair(0, 1, 1)
        merge(1)
        push(2).start()
        merge(2)
        push(3).start()
        merge(0)

    def pass_on():
        push(0).wait_recv()
        plus(kept.at[2, low], rcv_d.at[low])
        push(4).start()
        push(1).wait_recv()
        plus(kept.at[1, high], rcv_d.at[high])
        push(5).start()

    def along():
        for i in (2, 3, 4, 5):
            push(i).wait_recv()
        plus(kept.at[0], rcv_x, rcv_y)
        for b in range(4):
            pl.when(s != b)(lambda b=b: straight(b).start())

    def end(out_ref):
        out_ref[...] = kept[0, s].astype(F32)
        for b in range(4):

            @pl.when(s != b)
            def _(b=b):
                from_line(b).wait_recv()
                out_ref[...] += rcv_z[b].astype(F32)

        for b in range(4):
            pl.when(s != b)(lambda b=b: straight(b).wait_send())
        crossing(2, 0).wait_send()
        crossing(0, 1).wait_send()
        for i in range(6):
            push(i).wait_send()

    return far, near, pass_on, along, end


def weight_sums_scratch(rows, columns):
    dma = pltpu.SemaphoreType.DMA
    buffer = lambda *lead: pltpu.VMEM((*lead, rows, columns), BF16)
    return [
        buffer(4, 4),
        buffer(2, 4),
        buffer(4, 4),
        buffer(4),
        buffer(4),
        buffer(4),
        buffer(4),
        dma((4,)),
        dma((4,)),
        dma((6,)),
        dma((6,)),
        dma((4,)),
        dma((4,)),
    ]


def normed_back(dy, x, gain):
    inverse = lax.rsqrt(jnp.mean(x * x, axis=1, keepdims=True) + epsilon)
    gy = dy * gain
    x = x * inverse
    return inverse * (gy - x * jnp.mean(gy * x, axis=1, keepdims=True))


def middle_back_kernel(out_rows, dy_ref, mid_ref, g_ref, gain_ref, w_ref, dm_ref, low_ref, dh_ref, acc):
    dm = g_ref[...].astype(F32)
    dm += normed_back(dy_ref[...].astype(F32), mid_ref[...], gain_ref[...])
    dm_ref[...] = dm
    low = dm.astype(BF16)
    low_ref[...] = low
    tall = w_ref.shape[0] // 32
    heads = back_product(w_ref[...], low)
    for i in range(32):
        acc[i * out_rows : (i + 1) * out_rows, :] = heads[i * tall : i * tall + out_rows]
    dh_ref[...] = acc[...].astype(BF16)


def middle_back(dy, middle, g, gain, w, out_rows):
    count, width = middle.shape
    block = 256
    rows = pl.BlockSpec((block, width), lambda i: (i, 0))
    whole = lambda x: pl.BlockSpec(x.shape, lambda i: (0, 0))
    return pl.pallas_call(
        functools.partial(middle_back_kernel, out_rows),
        grid=(count // block,),
        in_specs=[rows] * 3 + [whole(gain), whole(w)],
        out_specs=[rows, rows, pl.BlockSpec((32 * out_rows, block), lambda i: (0, i))],
        out_shape=[
            jax.ShapeDtypeStruct((count, width), F32),
            jax.ShapeDtypeStruct((count, width), BF16),
            jax.ShapeDtypeStruct((32 * out_rows, count), BF16),
        ],
        scratch_shapes=[pltpu.VMEM((32 * out_rows, block), F32)],
        compiler_params=pltpu.CompilerParams(vmem_limit_bytes=56 * 2**20),
        name="middle_back",
    )(dy, middle, g, gain, w)


def sum_weights_kernel(n_ref, p_ref, h_ref, a_ref, few_ref, own_ref, *refs):
    w_ref, x_ref, dm_ref, back_0_ref, back_1_ref, gain_ref, wide_ref, *refs = refs
    qkv_out, few_out, products_out, out_out, dx_ref, wide_out, dg_ref, *refs = refs
    w_v, qkv_sum, back_v, w_sem, own_sem, sent_w, got_w, *refs = refs
    w_load = pltpu.make_async_copy(w_ref, w_v, w_sem)
    w_load.start()
    place = places()
    d, s, d_c, d_x, d_y, line = place
    flip, d_d = d_c - d, d_x + d_y - d
    plane = (d, d_c, d_x, d_x + flip, d_y, d_y + flip, d_d, d_d + flip)
    greet([(other, s) for other in plane[1:]] + [(d, (s + i) % 4) for i in (1, 2, 3)])

    def exchange(k, i):
        src, dst = (back_0_ref, back_1_ref)[i].at[plane[k]], back_v.at[i, d]
        if k == 0:
            return pltpu.make_async_copy(src, dst, own_sem.at[i])
        return remote(src, dst, sent_w.at[k, i], got_w.at[k, i], (plane[k], s))

    width, chunk = p_ref.shape[0], 512

    def chunks(make, dst):
        @pl.loop(0, width // chunk)
        def _(c):
            span = pl.ds(pl.multiple_of(c * chunk, chunk), chunk)
            dst[:, :, span] = make(span).astype(BF16).reshape(*dst.shape[:2], chunk)

    def qkv_product(k, dst):
        tall = dst.shape[0] * dst.shape[1]
        rows = n_ref[:, pl.ds(pl.multiple_of(k * tall, tall), tall)].T
        chunks(lambda span: back_product(rows, p_ref[span, :]), dst)
        for b in range(4):
            dst[b, :16, -128:] = few_ref[k * 4 + b]

    def out_product(k, dst):
        tall = dst.shape[0] * dst.shape[1]
        rows = h_ref[pl.ds(pl.multiple_of(k * tall, 16), tall), :]
        chunks(lambda span: dot(rows, a_ref[:, span]), dst)

    far, near, pass_on, along, end = weight_sums(qkv_product, refs[:13], place)
    far_2, near_2, pass_on_2, along_2, end_2 = weight_sums(out_product, refs[13:], place)
    block = 128

    def token_grads(first, count):
        def body(x_tile, dm_tile, dx_tile):
            i = pl.program_id(0) + first
            span = pl.ds(pl.multiple_of(i * block, block), block)
            dy = back_product(p_ref[:, span].T, w_v[...])
            dx_tile[...] = dm_tile[...] + normed_back(dy, x_tile[...].astype(F32), gain_ref[...])

        spec = lambda: pl.BlockSpec((block, x_ref.shape[1]), lambda i: (i + first, 0))
        pltpu.emit_pipeline(body, grid=(count,), in_specs=[spec(), spec()], out_specs=[spec()])(
            x_ref, dm_ref, dx_ref
        )

    blocks = x_ref.shape[0] // block
    far()
    near()
    w_load.wait()
    token_grads(0, 1)
    pass_on()
    far_2()
    near_2()
    token_grads(1, 2)
    along()
    pass_on_2()
    for k in range(8):
        exchange(k, 0).start()
        exchange(k, 1).start()
    token_grads(3, blocks - 3)
    along_2()
    end(qkv_sum)
    for i in (0, 1):
        exchange(0, i).wait()
        for k in range(1, 8):
            exchange(k, i).wait_recv()
            exchange(k, i).wait_send()
    part = back_v.shape[3]
    total = jnp.zeros((dg_ref.shape[0], 1), F32)
    for j in range(16):
        half_j, holder = j // 8, j % 8
        span = slice(j * part, (j + 1) * part)
        grad = back_v[half_j, holder].astype(F32)
        wide_out[:, span] = grad
        total += jnp.sum(grad * wide_ref[:, span].astype(F32), axis=1, keepdims=True)
    dg_ref[...] = jnp.broadcast_to(total, dg_ref.shape)
    inner = QW + 2 * KW
    total = jnp.sum(qkv_sum[:, :inner] * own_ref[:, :inner].astype(F32), axis=1, keepdims=True)
    products_out[...] = jnp.broadcast_to(total, products_out.shape)
    few_out[...] = qkv_sum[:16, inner:]
    qkv_out[...] = qkv_sum[:, :inner]
    end_2(out_out)


def sum_weights(normed, dprojected, heads, dattend, few, own, w, x, dmiddle, gain, back, back_1, wide):
    dma, anywhere = pltpu.SemaphoreType.DMA, pl.BlockSpec(memory_space=pl.ANY)
    vmem = pl.BlockSpec(memory_space=pltpu.VMEM)
    rows, width = own.shape
    tall = heads.shape[0] // 32
    scratch = [
        pltpu.VMEM(w.shape, BF16),
        pltpu.VMEM(own.shape, F32),
        pltpu.VMEM((2, *back.shape), BF16),
        dma,
        dma((2,)),
        dma((8, 2)),
        dma((8, 2)),
    ]
    scratch += weight_sums_scratch(rows, width) + weight_sums_scratch(tall, width)
    return pl.pallas_call(
        sum_weights_kernel,
        out_shape=[
            jax.ShapeDtypeStruct((rows, QW + 2 * KW), F32),
            jax.ShapeDtypeStruct((16, width - QW - 2 * KW), F32),
            jax.ShapeDtypeStruct((rows, 128), F32),
            jax.ShapeDtypeStruct((tall, width), F32),
            jax.ShapeDtypeStruct(dmiddle.shape, F32),
            jax.ShapeDtypeStruct(wide.shape, F32),
            jax.ShapeDtypeStruct((rows, 128), F32),
        ],
        in_specs=[vmem] * 6 + [anywhere] * 5 + [vmem] * 2,
        out_specs=[vmem] * 4 + [anywhere, vmem, vmem],
        scratch_shapes=scratch,
        compiler_params=pltpu.CompilerParams(
            collective_id=6, has_side_effects=True, vmem_limit_bytes=63 * 2**20
        ),
        name="sum_weights",
    )(normed, dprojected, heads, dattend, few, own, w, x, dmiddle, back, back_1, gain, wide)


def plane_kernel(rows, heads_ref, w_ref, x_ref, gain_ref, g_ref, down_ref, *refs):
    out_ref, dh_ref, mid_ref, w_v, x_v, down_v, mid_v, n_v, load, mid_sem, *refs = refs
    place = places()
    d, s, d_c, d_x, d_y, line = place
    w_load = pltpu.make_async_copy(w_ref, w_v, load.at[0])
    x_load = pltpu.make_async_copy(x_ref, x_v, load.at[1])
    down_load = pltpu.make_async_copy(down_ref, down_v, load.at[2])
    w_load.start()
    x_load.start()
    down_load.start()
    greet([(d_c, s), (d_x, s), (d_y, s)])
    begin, first, second, end = plane_stages(n_v, out_ref, *refs, place)
    w_load.wait()
    x_load.wait()
    width, chunk = mid_v.shape[1], 512

    def stored(row):
        tokens = pl.ds(row * (mid_v.shape[0] // rows), mid_v.shape[0] // rows)
        return pltpu.make_async_copy(mid_v.at[tokens], mid_ref.at[tokens], mid_sem.at[row])

    for row in range(rows):
        tokens = slice(row * (mid_v.shape[0] // rows), (row + 1) * (mid_v.shape[0] // rows))
        heads = heads_ref[:, tokens].T

        @pl.loop(0, width // chunk)
        def _(c):
            span = pl.ds(pl.multiple_of(c * chunk, chunk), chunk)
            weight = w_v[:, :, :, span].reshape(heads.shape[1], chunk)
            mid_v[tokens, span] = x_v[tokens, span].astype(F32) + dot(heads, weight)

        stored(row).start()
        mid = mid_v[tokens, :]
        inverse = lax.rsqrt(jnp.mean(mid * mid, axis=1, keepdims=True) + epsilon)
        n_v[tokens, :] = (mid * inverse * gain_ref[...]).astype(BF16)
        begin(row)
    down_load.wait()

    def body(g_tile, dh_tile):
        dh_tile[...] = back_product(g_tile[...], down_v[...]).astype(BF16)

    pltpu.emit_pipeline(
        body,
        grid=(g_ref.shape[0] // 512,),
        in_specs=[pl.BlockSpec((512, down_v.shape[1]), lambda i: (i, 0))],
        out_specs=[pl.BlockSpec((512, down_v.shape[0]), lambda i: (i, 0))],
    )(g_ref, dh_ref)
    first()
    second()
    end()
    for row in range(rows):
        stored(row).wait()


def plane_gather(heads, w, x, gain, g, down):
    dma, anywhere = pltpu.SemaphoreType.DMA, pl.BlockSpec(memory_space=pl.ANY)
    vmem = pl.BlockSpec(memory_space=pltpu.VMEM)
    everyone, dhidden, middle = pl.pallas_call(
        functools.partial(plane_kernel, 2),
        out_shape=[
            jax.ShapeDtypeStruct((8, *x.shape), BF16),
            jax.ShapeDtypeStruct((g.shape[0], down.shape[0]), BF16),
            jax.ShapeDtypeStruct(x.shape, F32),
        ],
        in_specs=[vmem, anywhere, anywhere, vmem, anywhere, anywhere],
        out_specs=[anywhere] * 3,
        scratch_shapes=[
            pltpu.VMEM(w.shape, BF16),
            pltpu.VMEM(x.shape, BF16),
            pltpu.VMEM(down.shape, BF16),
            pltpu.VMEM(x.shape, F32),
            pltpu.VMEM(x.shape, BF16),
            dma((3,)),
            dma((2,)),
            dma,
            dma((8, 2)),
            dma((8, 2)),
        ],
        compiler_params=pltpu.CompilerParams(
            collective_id=4, has_side_effects=True, vmem_limit_bytes=48 * 2**20
        ),
        name="plane_gather",
    )(heads, w, x, gain, g, down)
    return everyone.reshape(8 * x.shape[0], x.shape[1]), dhidden, middle


def transposed_kernel(x_ref, g_ref, out_ref):
    n_seq, n_dp, rows, _ = out_ref.shape
    total = outer_sum(x_ref[...], g_ref[...])
    for i in range(n_dp * n_seq):
        out_ref[i % n_seq, i // n_seq] = total[i * rows : (i + 1) * rows].astype(BF16)


def transposed_product(x, g, n_dp, n_seq, parts):
    (tokens, width), wide = x.shape, g.shape[1] // parts
    rows, tall = width // (n_dp * n_seq), 512
    return pl.pallas_call(
        transposed_kernel,
        grid=(width // tall,),
        in_specs=[
            pl.BlockSpec((tokens, tall), lambda i: (0, i)),
            pl.BlockSpec((tokens, wide), lambda i: (0, 0)),
        ],
        out_specs=pl.BlockSpec(
            (n_seq, tall // (n_seq * rows), rows, wide), lambda i: (0, i, 0, 0)
        ),
        out_shape=jax.ShapeDtypeStruct((n_seq, n_dp, rows, wide), BF16),
        compiler_params=pltpu.CompilerParams(vmem_limit_bytes=60 * 2**20),
        cost_estimate=pl.CostEstimate(
            flops=2 * tokens * width * wide,
            bytes_accessed=2 * (tokens * width + tokens * wide + width * wide),
            transcendentals=0,
        ),
        name="transposed_product",
    )(x, g)


def plane_sums(kept, leaving, rcv_c, rcv_d, rcv_x, rcv_y, sent_c, got_c, sent_p, got_p, place):
    d, s, d_c, d_x, d_y, line = place
    rows = kept.shape[1]
    low, high = pl.ds(0, rows // 2), pl.ds(rows // 2, rows // 2)

    def crossing(i, slot):
        return remote(leaving.at[slot], rcv_c.at[i], sent_c.at[i], got_c.at[i], (d_c, s))

    def merge(i):
        crossing(i, 0).wait_recv()
        plus(kept.at[i], rcv_c.at[i])

    def push(i):
        src, dst, peer = (
            (kept.at[3, low], rcv_d.at[low], d_x),
            (kept.at[3, high], rcv_d.at[high], d_y),
            (kept.at[1, low], rcv_x.at[low], d_x),
            (kept.at[2, high], rcv_y.at[high], d_y),
            (kept.at[2, low], rcv_y.at[low], d_y),
            (kept.at[1, high], rcv_x.at[high], d_x),
        )[i]
        return remote(src, dst, sent_p.at[i], got_p.at[i], (peer, s))

    def far():
        merge(3)
        push(0).start()
        push(1).start()

    def near(i):
        merge(i)
        if i:
            push(i + 1).start()

    def pass_on():
        push(0).wait_recv()
        plus(kept.at[2, low], rcv_d.at[low])
        push(4).start()
        push(1).wait_recv()
        plus(kept.at[1, high], rcv_d.at[high])
        push(5).start()

    def end():
        for i in (2, 3, 4, 5):
            push(i).wait_recv()
        plus(kept.at[0], rcv_x, rcv_y)
        for i in range(6):
            push(i).wait_send()

    return crossing, far, near, pass_on, end


def sums_scratch(rows, width):
    dma = pltpu.SemaphoreType.DMA
    buffer = lambda *lead: pltpu.VMEM((*lead, rows, width), BF16)
    return [
        buffer(4),
        buffer(2),
        buffer(4),
        buffer(),
        buffer(),
        buffer(),
        dma((4,)),
        dma((4,)),
        dma((6,)),
        dma((6,)),
    ]


ORDER = (7, 6, 3, 2, 5, 4, 1, 0)


def block_products(g_ref, g_v, g_sem, multiply):
    rows = g_v.shape[1]

    def load(turn):
        block = pl.ds(ORDER[turn] * rows, rows)
        return pltpu.make_async_copy(g_ref.at[block], g_v.at[turn % 2], g_sem.at[turn % 2])

    def product(turn, dst):
        if turn + 1 < 8:
            load(turn + 1).start()
        load(turn).wait()
        chunk = 512

        @pl.loop(0, dst.shape[1] // chunk)
        def _(c):
            span = pl.ds(pl.multiple_of(c * chunk, chunk), chunk)
            dst[:, span] = multiply(g_v[turn % 2], span).astype(BF16)

    return load, product


def plane_sum_kernel(
    g_ref, w_ref, h_ref, t_ref, x_ref, out_ref, grad_ref, wide_ref, w_v, g_v, h_v, *refs
):
    w_sem, g_sem, h_sem, out_sem, *refs = refs
    place = places()
    d, s, d_c, d_x, d_y, line = place
    kept, leaving = refs[:2]
    w_wait = load_rows(w_ref, w_v, w_sem, 8, 4)
    load, product = block_products(
        g_ref, g_v, g_sem, lambda g, span: back_product(g, w_v[span, :])
    )
    load(0).start()
    h_load = pltpu.make_async_copy(h_ref, h_v, h_sem)
    h_load.start()
    greet([(d_c, s), (d_x, s), (d_y, s)])
    crossing, far, near, pass_on, end = plane_sums(*refs, place)
    w_wait()

    def pair(turn, i):
        slot = turn // 2 % 2
        if turn >= 4:
            crossing(3 if slot == 0 else 1, slot).wait_send()
        product(turn, leaving.at[slot])
        crossing(i, slot).start()
        product(turn + 1, kept.at[i])

    pair(0, 3)
    far()
    pair(2, 1)
    pair(4, 2)
    near(1)
    near(2)
    pair(6, 0)
    near(0)
    h_load.wait()

    def grad_body(t_tile, grad_tile):
        grad_tile[...] = outer_sum(h_v[...], t_tile[...]).astype(BF16)

    tokens, deep = h_v.shape
    wide = 256

    def grad_tiles(first, count):
        pltpu.emit_pipeline(
            grad_body,
            grid=(count,),
            in_specs=[pl.BlockSpec((tokens, wide), lambda i: (0, first + i))],
            out_specs=[pl.BlockSpec((deep, wide), lambda i: (0, first + i))],
        )(t_ref, grad_ref)

    def wide_body(x_tile, wide_tile):
        total = outer_sum(x_tile[...], h_v[...])
        high = wide_tile.shape[2]
        for j in range(4):
            wide_tile[j, 0] = total[j * high : (j + 1) * high].astype(BF16)

    grad_tiles(0, 2)
    pass_on()
    grad_tiles(2, t_ref.shape[1] // wide - 2)
    h_load = pltpu.make_async_copy(g_ref.at[:, pl.ds(deep, deep)], h_v, h_sem)
    h_load.start()
    h_load.wait()
    pltpu.emit_pipeline(
        wide_body,
        grid=(8,),
        in_specs=[pl.BlockSpec((tokens, x_ref.shape[1] // 8), lambda i: (0, i))],
        out_specs=[
            pl.BlockSpec((4, 1, x_ref.shape[1] // 32, deep), lambda i: (0, i, 0, 0))
        ],
    )(x_ref, wide_ref)
    end()
    out = pltpu.make_async_copy(kept.at[0], out_ref, out_sem)
    out.start()
    crossing(2, 0).wait_send()
    crossing(0, 1).wait_send()
    out.wait()


def plane_sum(g, w, h, t, x, rows):
    dma, anywhere = pltpu.SemaphoreType.DMA, pl.BlockSpec(memory_space=pl.ANY)
    width, deep = w.shape
    return pl.pallas_call(
        plane_sum_kernel,
        out_shape=[
            jax.ShapeDtypeStruct((rows, width), BF16),
            jax.ShapeDtypeStruct((h.shape[1], t.shape[1]), BF16),
            jax.ShapeDtypeStruct((4, 8, width // 32, h.shape[1]), BF16),
        ],
        in_specs=[anywhere] * 5,
        out_specs=[anywhere] * 3,
        scratch_shapes=[
            pltpu.VMEM((width, deep), BF16),
            pltpu.VMEM((2, rows, deep), BF16),
            pltpu.VMEM(h.shape, BF16),
            dma,
            dma((2,)),
            dma,
            dma,
            *sums_scratch(rows, width),
        ],
        compiler_params=pltpu.CompilerParams(
            collective_id=5, has_side_effects=True, vmem_limit_bytes=62 * 2**20
        ),
        name="plane_sum",
    )(g, w, h, t, x)


def sigmoid(v):
    return 1.0 / (1.0 + jnp.exp(-v))


def load_rows(w_ref, w_v, sem, n_dp, n_seq):
    rows = w_v.shape[0] // (n_dp * n_seq)

    @pl.loop(0, n_dp * n_seq)
    def _(i):
        src = pl.ds(pl.multiple_of(i * rows, rows), rows)
        place = (i % n_dp) * n_seq + i // n_dp
        dst = pl.ds(pl.multiple_of(place * rows, rows), rows)
        pltpu.make_async_copy(w_ref.at[src], w_v.at[dst], sem).start()

    return pltpu.make_async_copy(w_ref, w_v, sem).wait


def gate_up_kernel(n_dp, n_seq, x_ref, dh_ref, w_ref, hidden_ref, dgu_ref, w_v, sem):
    pl.when(pl.program_id(0) == 0)(lambda: load_rows(w_ref, w_v, sem, n_dp, n_seq)())
    part = hidden_ref.shape[1]
    step = 256 if part % 256 == 0 else 128
    for c in range(0, part, step):
        first, second = slice(c, c + step), slice(part + c, part + c + step)
        gate, up = dot(x_ref[...], w_v[:, first]), dot(x_ref[...], w_v[:, second])
        dhidden = dh_ref[:, first].astype(F32)
        sig = sigmoid(gate)
        silu = gate * sig
        hidden_ref[:, first] = (silu * up).astype(BF16)
        dgu_ref[:, first] = (dhidden * up * (sig + silu * (1.0 - sig))).astype(BF16)
        dgu_ref[:, second] = (dhidden * silu).astype(BF16)


def gate_up_product(x, dhidden, w, n_dp, n_seq):
    tokens, width = x.shape
    wide = w.shape[1]
    block = 512
    span = lambda columns: pl.BlockSpec((block, columns), lambda i: (i, 0))
    return pl.pallas_call(
        functools.partial(gate_up_kernel, n_dp, n_seq),
        grid=(tokens // block,),
        in_specs=[span(width), span(wide // 2), pl.BlockSpec(memory_space=pl.ANY)],
        out_specs=[span(wide // 2), span(wide)],
        out_shape=[
            jax.ShapeDtypeStruct((tokens, wide // 2), BF16),
            jax.ShapeDtypeStruct((tokens, wide), BF16),
        ],
        scratch_shapes=[pltpu.VMEM(w.shape, BF16), pltpu.SemaphoreType.DMA],
        compiler_params=pltpu.CompilerParams(vmem_limit_bytes=56 * 2**20),
        cost_estimate=pl.CostEstimate(
            flops=2 * tokens * width * wide,
            bytes_accessed=2 * (tokens * width + width * wide + tokens * wide * 2),
            transcendentals=tokens * wide // 2,
        ),
        name="gate_up",
    )(x, dhidden, w)


def mm(a, b):
    return jnp.dot(a, b, preferred_element_type=F32)


def outer_sum(left, right):
    return lax.dot_general(left, right, (((0,), (0,)), ((), ())), preferred_element_type=F32)


def back_product(rows, weight):
    return lax.dot_general(rows, weight, (((1,), (1,)), ((), ())), preferred_element_type=F32)


def gather(x, axes):
    return lax.all_gather(x, axes, axis=0, tiled=True)


def scatter(x, axes):
    return lax.psum_scatter(x, axes, scatter_dimension=0, tiled=True)


def shards(
    tokens, lengths, w_qkv, w_out, w_gate_up, w_down, attn_gain, ffn_gain, head_gains, out_grad
):
    n_dp, n_seq = lax.axis_size("dp"), lax.axis_size("seq")
    rows, length, width = tokens.shape
    count = rows * length
    ff = w_gate_up.shape[1] // 2
    part = ff // n_dp
    wr = w_gate_up.shape[0]
    offset = lax.axis_index("seq") * length
    local_pos = offset + jnp.arange(length, dtype=jnp.int32)
    cosine, sine = rope_tables(jnp.concatenate([local_pos] * rows))
    ends = jnp.cumsum(lengths, axis=1, dtype=jnp.int32)
    start = jnp.sum(
        jnp.where(local_pos[None, :, None] >= ends[:, None, :], lengths[:, None, :], 0), axis=2
    ).reshape(1, count)
    start = jnp.broadcast_to(start, (8, count))

    full = (n_dp, n_seq) == (8, 4)
    qkv_w = w_qkv.shape[1]
    spare = width - qkv_w
    gains = jnp.concatenate([attn_gain, ffn_gain])
    gains = [jnp.pad(g, (0, spare - g.shape[0]))[None] for g in (gains, head_gains)]
    gains.append(jnp.zeros((wr - 2, spare), BF16))
    own_qkv = jnp.concatenate([w_qkv, jnp.concatenate(gains, axis=0)], axis=1)
    out_rows = w_out.shape[0]
    own_out = jnp.pad(w_out, ((0, -out_rows % 16), (0, 0)))
    all_qkv, some_out, spread = gather_weights(own_qkv, [own_out], w_gate_up, n_dp, n_seq)
    qkv_full = all_qkv.reshape(width, width)
    attn_gain_full = all_qkv[:, 0, qkv_w : qkv_w + wr].reshape(-1).astype(F32)
    ffn_gain_full = all_qkv[:, 0, qkv_w + wr : qkv_w + 2 * wr].reshape(-1).astype(F32)
    head_full = all_qkv[:, 1, qkv_w : qkv_w + head_gains.shape[0]].reshape(-1).astype(F32)

    w_down, qkv_full = lax.optimization_barrier((w_down, qkv_full))
    down_w = gather(w_down, "seq")
    cotangent_low = out_grad.reshape(count, width)

    x_rows = tokens.reshape(count, width).astype(F32)
    normed_low = norm_rows(x_rows, attn_gain_full).astype(BF16)
    projected = lax.dot_general(
        qkv_full, normed_low, (((0,), (1,)), ((), ())), preferred_element_type=F32
    )

    queries, pairs = prepare(projected, head_full[:, None], cosine, sine)
    more = [cotangent_low, some_out] if full else []
    heads_out, lse, held, *planes = attend(start, queries, pairs, rows, n_seq, more, out_rows)
    gate_up_w = gather(spread.reshape(n_dp * wr, 2 * part), "seq")
    if full:
        cotangent_all, all_out, heads_full = planes
        cotangent_all = cotangent_all.reshape(n_dp * count, width)
        out_full = all_out.reshape(-1, width)
        normed2_all, dhidden, middle = plane_gather(
            heads_full, all_out, tokens.reshape(count, width), ffn_gain_full[None],
            cotangent_all, down_w,
        )
    else:
        cotangent_all, all_out = gather(cotangent_low, "dp"), some_out
        out_full = all_out.reshape(-1, width)
        fill = ((0, 0), (0, all_out.shape[1] - out_rows), (0, 0))
        heads_full = jnp.pad(heads_out.reshape(n_dp * n_seq, out_rows, count), fill)
        heads_full = heads_full.reshape(-1, count)
        middle = x_rows + outer_sum(heads_full, out_full)
        normed2_all = gather(norm_rows(middle, ffn_gain_full).astype(BF16), "dp")
        dhidden = back_product(cotangent_all, down_w).astype(BF16)
    hidden, dgate_up = gate_up_product(normed2_all, dhidden, gate_up_w, n_dp, n_seq)
    gate_grad = transposed_product(normed2_all, dgate_up, n_dp, n_seq, 2 if full else 1)
    gate_grad, dgate_up = lax.optimization_barrier((gate_grad, dgate_up))
    gate_grad = scatter(gate_grad.reshape(width, -1), "seq")
    if full:
        dnormed2, down_grad, up_grad = plane_sum(
            dgate_up, gate_up_w, hidden, cotangent_all, normed2_all, count
        )
        gate_grad, up_grad, dnormed2 = lax.optimization_barrier((gate_grad, up_grad, dnormed2))
        up_grad = scatter(up_grad.reshape(width, part), "seq")
    else:
        ordered = gate_up_w.reshape(n_seq, n_dp, wr, 2 * part).transpose(1, 0, 2, 3)
        ordered = ordered.reshape(width, 2 * part)
        dnormed2 = scatter(back_product(dgate_up, ordered).astype(BF16), "dp")
        down_grad = outer_sum(hidden, cotangent_all).astype(BF16)
    if full:
        dmiddle, dattend, dheads = middle_back(
            dnormed2, middle, cotangent_low, ffn_gain_full[None], out_full, out_rows
        )
    else:
        dmiddle = cotangent_low.astype(F32)
        dmiddle += normed_back(dnormed2.astype(F32), middle, ffn_gain_full)
        dattend = dmiddle.astype(BF16)
        dheads = back_product(out_full, dattend).astype(BF16).reshape(n_dp * n_seq, -1, count)
        dheads = dheads[:, :out_rows].reshape(QW, count)
    if full:
        dqueries, dpairs, mixed = attend_back(
            start, queries, dheads, heads_out, lse, pairs, held, rows, n_seq,
            [hidden, down_w, middle],
        )
    else:
        dqueries, dpairs = attend_back(
            start, queries, dheads, heads_out, lse, pairs, held, rows, n_seq, []
        )
        mixed = middle + scatter(mm(hidden, down_w).astype(BF16), "dp").astype(F32)
    if full:
        gate_grad, up_grad, dqueries = lax.optimization_barrier((gate_grad, up_grad, dqueries))
        up_grad = up_grad.reshape(n_dp, wr, part)
    gate_grad = gate_grad.reshape(n_dp, wr, -1)
    down_grad, dqueries = lax.optimization_barrier((down_grad, dqueries))
    down_grad = scatter(down_grad, "seq")
    dprojected_low, head_grad = prepare_back(
        projected, head_full[:, None], cosine, sine, dqueries, dpairs
    )
    few = head_gains.shape[0]
    if full:
        few_rows = jnp.pad(head_grad.reshape(-1, few, 1), ((0, 0), (0, 16 - few), (0, 0)))
        few_rows = jnp.broadcast_to(few_rows.astype(BF16), (n_dp * n_seq, 16, width - qkv_w))
        qkv_grad, head_rows_out, qkv_products, out_weight_grad, tokens_grad, gate_up_grad, ffn_products = (
            sum_weights(
                normed_low,
                dprojected_low,
                heads_full,
                dattend,
                few_rows,
                own_qkv,
                qkv_full,
                tokens.reshape(count, width),
                dmiddle,
                attn_gain_full[None],
                gate_grad,
                up_grad,
                w_gate_up,
            )
        )
        head_out, ffn_products, qkv_products = (
            head_rows_out[:few, 0], ffn_products[:, 0], qkv_products[:, 0]
        )
    else:
        qkv_grad = lax.dot_general(
            normed_low, dprojected_low, (((0,), (1,)), ((), ())), preferred_element_type=F32
        ).astype(BF16)
        out_grads = mm(heads_full, dattend).astype(BF16)
        qkv_grad, out_weight_grad = (
            scatter(scatter(g, "dp"), "seq").astype(F32) for g in (qkv_grad, out_grads)
        )
        head_out = jnp.sum(
            lax.all_to_all(head_grad.reshape(-1, few), BOTH, 0, 0, tiled=True), axis=0
        )
        qkv_products = jnp.sum(own_qkv[:, :qkv_w].astype(F32) * qkv_grad[:, :qkv_w], axis=1)
        qkv_grad = qkv_grad[:, :qkv_w]
        gate_up_grad = lax.all_to_all(gate_grad, "dp", 0, 0, tiled=True)
        gate_up_grad = gate_up_grad.reshape(n_dp, wr, 2, part).transpose(1, 2, 0, 3)
        gate_up_grad = gate_up_grad.reshape(wr, 2 * ff).astype(F32)
        ffn_products = jnp.sum(w_gate_up.astype(F32) * gate_up_grad, axis=1)
        dnormed = back_product(dprojected_low.T, qkv_full)
        tokens_grad = dmiddle + normed_back(dnormed, x_rows, attn_gain_full)
    attn_gain_out = qkv_products / attn_gain.astype(F32)
    ffn_gain_out = ffn_products / ffn_gain.astype(F32)
    return (
        mixed.astype(BF16).reshape(rows, length, width),
        tokens_grad.reshape(rows, length, width),
        qkv_grad,
        out_weight_grad[:out_rows],
        gate_up_grad,
        down_grad.astype(F32),
        attn_gain_out,
        ffn_gain_out,
        head_out,
    )


def solution(mesh):
    in_specs = (
        P("dp", "seq", None),
        P("dp", None),
        P(("dp", "seq"), None),
        P(("dp", "seq"), None),
        P(("dp", "seq"), None),
        P(("dp", "seq"), None),
        P(("dp", "seq")),
        P(("dp", "seq")),
        P(("dp", "seq")),
        P("dp", "seq", None),
    )
    out_specs = (
        P("dp", "seq", None),
        P("dp", "seq", None),
        P(("dp", "seq"), None),
        P(("dp", "seq"), None),
        P(("dp", "seq"), None),
        P(("dp", "seq"), None),
        P(("dp", "seq")),
        P(("dp", "seq")),
        P(("dp", "seq")),
    )
    return jax.shard_map(shards, mesh=mesh, in_specs=in_specs, out_specs=out_specs, check_vma=False)
```

```python
import functools

import jax
import jax.numpy as jnp
from jax import lax
from jax.experimental import pallas as pl
from jax.experimental.pallas import tpu as pltpu
from jax.sharding import PartitionSpec as P

QUERY_HEADS = 20
KEY_VALUE_HEADS = 5
HEAD_SIZE = 64
GROUP = QUERY_HEADS // KEY_VALUE_HEADS
QW = QUERY_HEADS * HEAD_SIZE
KW = KEY_VALUE_HEADS * HEAD_SIZE
BOTH = ("dp", "seq")

epsilon = 1e-06
F32 = jnp.float32
BF16 = jnp.bfloat16
MESH = pl.DeviceIdType.MESH


def norm_rows(inputs, scales):
    return inputs * lax.rsqrt(jnp.mean(inputs * inputs, axis=-1, keepdims=True) + epsilon) * scales


def rope_tables(positions):
    inverse_freq = 10000.0 ** (-(jnp.arange(HEAD_SIZE // 2, dtype=F32) * 2.0 / HEAD_SIZE))
    angles = inverse_freq[:, None] * positions.astype(F32)[None, :]
    return (jnp.cos(angles), jnp.sin(angles))


def head_rows(i):
    return pl.ds(pl.multiple_of(i * HEAD_SIZE, HEAD_SIZE), HEAD_SIZE)


def key_rows(i):
    return head_rows(2 * i), head_rows(2 * i + 1)


def unit(v):
    inverse = lax.rsqrt(jnp.mean(v * v, axis=0, keepdims=True) + epsilon)
    return v * inverse, inverse


def prepare_kernel(p_ref, gain_ref, cos_ref, sin_ref, q_ref, kv_ref):
    cosine, sine = cos_ref[...], sin_ref[...]

    def turned(v, gain):
        v = unit(v)[0] * gain
        first, second = v[: HEAD_SIZE // 2], v[HEAD_SIZE // 2 :]
        return jnp.concatenate(
            [first * cosine - second * sine, second * cosine + first * sine], axis=0
        )

    @pl.loop(0, KEY_VALUE_HEADS, unroll=KEY_VALUE_HEADS)
    def _(i):
        key, value = key_rows(i)
        keys_in = p_ref[head_rows(QUERY_HEADS + i), :]
        kv_ref[key, :] = turned(keys_in, gain_ref[HEAD_SIZE:, :]).astype(BF16)
        values_in = p_ref[head_rows(QUERY_HEADS + KEY_VALUE_HEADS + i), :]
        kv_ref[value, :] = values_in.astype(BF16)

    @pl.loop(0, QUERY_HEADS, unroll=KEY_VALUE_HEADS)
    def _(i):
        rows = head_rows(i)
        queries = turned(p_ref[rows, :], gain_ref[:HEAD_SIZE, :]) * HEAD_SIZE**-0.5
        q_ref[rows, :] = queries.astype(BF16)


def prepare(projected, gains, cosine, sine):
    tokens = projected.shape[1]
    return pl.pallas_call(
        prepare_kernel,
        out_shape=[
            jax.ShapeDtypeStruct((QW, tokens), BF16),
            jax.ShapeDtypeStruct((2 * KW, tokens), BF16),
        ],
        compiler_params=pltpu.CompilerParams(vmem_limit_bytes=40 * 2**20),
        name="prepare",
    )(projected, gains, cosine, sine)


def prepare_back_kernel(
    p_ref, gain_ref, cos_ref, sin_ref, dq_ref, dkv_ref, out_ref, dg_ref, acc_q, acc_k
):
    cosine, sine = cos_ref[...], sin_ref[...]
    step = pl.program_id(0)

    @pl.when(step == 0)
    def _():
        acc_q[...] = jnp.zeros_like(acc_q)
        acc_k[...] = jnp.zeros_like(acc_k)

    def back(v, gain, dy, acc):
        u, inverse = unit(v)
        first, second = dy[: HEAD_SIZE // 2], dy[HEAD_SIZE // 2 :]
        dz = jnp.concatenate(
            [first * cosine + second * sine, second * cosine - first * sine], axis=0
        )
        acc[...] += dz * u
        du = dz * gain
        return inverse * (du - u * jnp.mean(du * u, axis=0, keepdims=True))

    @pl.loop(0, KEY_VALUE_HEADS, unroll=KEY_VALUE_HEADS)
    def _(i):
        key, value = key_rows(i)
        rows = head_rows(QUERY_HEADS + i)
        dv = back(p_ref[rows, :], gain_ref[HEAD_SIZE:, :], dkv_ref[key, :], acc_k)
        out_ref[rows, :] = dv.astype(BF16)
        out_ref[head_rows(QUERY_HEADS + KEY_VALUE_HEADS + i), :] = dkv_ref[value, :].astype(BF16)

    @pl.loop(0, QUERY_HEADS, unroll=KEY_VALUE_HEADS)
    def _(i):
        rows = head_rows(i)
        dy = dq_ref[rows, :] * HEAD_SIZE**-0.5
        dv = back(p_ref[rows, :], gain_ref[:HEAD_SIZE, :], dy, acc_q)
        out_ref[rows, :] = dv.astype(BF16)

    rest = out_ref.shape[0] - QW - 2 * KW
    out_ref[QW + 2 * KW :, :] = jnp.zeros((rest, out_ref.shape[1]), BF16)

    @pl.when(step == pl.num_programs(0) - 1)
    def _():
        few = 2 * HEAD_SIZE // dg_ref.shape[0]
        dg_ref[...] = jnp.zeros_like(dg_ref)
        for half, acc in enumerate((acc_q, acc_k)):
            total = jnp.sum(acc[...], axis=1, keepdims=True)
            total = jnp.broadcast_to(total, (HEAD_SIZE, dg_ref.shape[2]))
            for i in range(HEAD_SIZE // few):
                dg_ref[half * (HEAD_SIZE // few) + i, :few, :] = total[i * few : (i + 1) * few]


def prepare_back(projected, gains, cosine, sine, dqueries, dpairs, width, devices):
    tokens = projected.shape[1]
    block = min(256, tokens)
    some = lambda x, rows=None: pl.BlockSpec((rows or x.shape[0], block), lambda i: (0, i))
    return pl.pallas_call(
        prepare_back_kernel,
        grid=(tokens // block,),
        in_specs=[
            some(projected, QW + 2 * KW),
            pl.BlockSpec(gains.shape, lambda i: (0, 0)),
            *[some(x) for x in (cosine, sine, dqueries, dpairs)],
        ],
        out_specs=[
            pl.BlockSpec((width, block), lambda i: (0, i)),
            pl.BlockSpec((devices, 16, 128), lambda i: (0, 0, 0)),
        ],
        out_shape=[
            jax.ShapeDtypeStruct((width, tokens), BF16),
            jax.ShapeDtypeStruct((devices, 16, 128), F32),
        ],
        scratch_shapes=[pltpu.VMEM((HEAD_SIZE, block), F32)] * 2,
        compiler_params=pltpu.CompilerParams(vmem_limit_bytes=62 * 2**20),
        name="prepare_back",
    )(projected, gains, cosine, sine, dqueries, dpairs)


def dot(a, b):
    return jnp.dot(a, b, preferred_element_type=F32)


def places():
    d, s = lax.axis_index("dp"), lax.axis_index("seq")
    core, column, line = d % 2, (d // 2) % 2, d // 4
    return d, s, d + 1 - 2 * core, d + 2 - 4 * column, d + 4 - 8 * line, line


def greet(peers, line=None):
    barrier = pltpu.get_barrier_semaphore()

    def signal(peer):
        pl.semaphore_signal(barrier, inc=1, device_id=peer, device_id_type=MESH)

    for peer in peers:
        signal(peer)
    if line is None:
        pl.semaphore_wait(barrier, len(peers))
        return
    d, s = line
    last = lax.axis_size("seq") - 1
    pl.when(s < last)(lambda: signal((d, s + 1)))
    pl.when(s > 0)(lambda: signal((d, s - 1)))
    pl.semaphore_wait(barrier, len(peers) + 1 - s // last + (s + last - 1) // last)


def remote(src, dst, sent, got, peer):
    return pltpu.make_async_remote_copy(
        src_ref=src,
        dst_ref=dst,
        send_sem=sent,
        recv_sem=got,
        device_id=peer,
        device_id_type=MESH,
    )


def plane_stages(x_ref, out_ref, own_sem, sent, got, place, ordered=False):
    d, s, d_c, d_x, d_y, line = place
    flip, d_d = d_c - d, d_x + d_y - d
    slots = list(range(8))
    if ordered:
        slots = [d, d_c, d_x, d_x + flip, d_y, d_y + flip, d_d, d_d + flip]
    half = x_ref.shape[0] // 2
    halves = (pl.ds(0, half), pl.ds(half, half))
    source = {1: 0, 2: 0, 4: 0, 3: 2, 5: 4, 7: 6}

    def piece(k, h, peer):
        back = source[k] if k in source else (4 if h == 0 else 2)
        src = x_ref.at[halves[h]] if back == 0 else out_ref.at[slots[back], halves[h]]
        dst = out_ref.at[slots[back] if ordered else k, halves[h]]
        return remote(src, dst, sent.at[k, h], got.at[k, h], (peer, s))

    own = pltpu.make_async_copy(x_ref, out_ref.at[slots[0]], own_sem)

    def begin(h):
        for k, peer in ((2, d_x), (4, d_y), (1, d_c)):
            piece(k, h, peer).start()
        if h:
            own.start()

    def first():
        piece(4, 0, d_y).wait_recv()
        piece(6, 0, d_x).start()
        piece(5, 0, d_c).start()
        piece(2, 0, d_x).wait_recv()
        piece(3, 0, d_c).start()

    def second():
        piece(2, 1, d_x).wait_recv()
        piece(6, 1, d_y).start()
        piece(3, 1, d_c).start()
        piece(4, 1, d_y).wait_recv()
        piece(5, 1, d_c).start()

    def end():
        for h in (0, 1):
            piece(6, h, d_x).wait_recv()
            piece(7, h, d_c).start()
        for k in (1, 3, 5, 7):
            for h in (0, 1):
                piece(k, h, d_c).wait_recv()
        for k in range(1, 8):
            for h in (0, 1):
                piece(k, h, d_c).wait_send()
        own.wait()

    return begin, first, second, end


def abreast(block):
    return jnp.concatenate(
        [block[i * HEAD_SIZE : (i + 1) * HEAD_SIZE] for i in range(GROUP)], axis=1
    )


def across(rows):
    return jnp.concatenate([rows[i : i + 1] for i in range(GROUP)], axis=1)


def seen(back, me, start):
    length = start.shape[1]
    key = lax.broadcasted_iota(jnp.int32, (length, length), 0)
    found = key + (me - back) * length >= start
    if back == 0:
        found &= key <= lax.broadcasted_iota(jnp.int32, (length, length), 1)
    bias = jnp.where(found, 0.0, -1e30)
    return jnp.concatenate([bias] * GROUP, axis=1)


def spans(i, length):
    row, head = i // KEY_VALUE_HEADS, i % KEY_VALUE_HEADS
    wide, pair = GROUP * HEAD_SIZE, 2 * HEAD_SIZE
    tokens = pl.ds(pl.multiple_of(row * length, length), length)
    return (
        tokens,
        pl.ds(pl.multiple_of(head * wide, wide), wide),
        pl.ds(pl.multiple_of(head * pair, pair), pair),
        head,
    )


def attend_kernel(n, rows, planes, out_rows, start_ref, q_ref, kv_ref, *refs):
    x_refs, refs = refs[:planes], refs[planes:]
    o_ref, lse_ref, held, *refs = refs
    out_refs, refs = refs[:planes], refs[planes:]
    if planes:
        full_ref, filled, *refs = refs
    o_acc, l_acc, sent, got, *refs = refs
    d, me = lax.axis_index("dp"), lax.axis_index("seq")
    length = q_ref.shape[1] // rows
    if planes:
        place = places()
        d, me, d_c, d_x, d_y, _ = place
        greet([(d_c, me), (d_x, me), (d_y, me)], (d, me))
        each = [
            plane_stages(x_refs[i], out_refs[i], *refs[3 * i : 3 * i + 3], place, i > 0)
            for i in range(planes)
        ]
    else:
        greet([], (d, me))
        each = []

    def climb(step, head):
        lines = pl.ds(head * 2 * HEAD_SIZE, 2 * HEAD_SIZE)
        src = kv_ref.at[lines] if step == 1 else held.at[step - 2, lines]
        dst = held.at[step - 1, lines]
        return remote(src, dst, sent.at[step - 1, head], got.at[step - 1, head], (d, me + 1))

    heads = range(KEY_VALUE_HEADS)

    def climbs(step):
        for head in heads:
            climb(step, head).start()

    def level(back):
        @pl.loop(0, rows * KEY_VALUE_HEADS, unroll=KEY_VALUE_HEADS)
        def _(i):
            tokens, wide, pair, head = spans(i, length)
            block = kv_ref[pair, tokens] if back == 0 else held[back - 1, pair, tokens]
            keys, values = block[:HEAD_SIZE].T, block[HEAD_SIZE:]
            bias = seen(back, me, start_ref[0:1, tokens])
            p = jnp.exp(dot(keys, abreast(q_ref[wide, tokens])) + bias)
            total = jnp.sum(p, axis=0, keepdims=True)
            out = dot(values, p.astype(BF16))
            for g in range(GROUP):
                own = slice(g * length, (g + 1) * length)
                line = slice(g, g + 1)
                part = pl.ds(wide.start + g * HEAD_SIZE, HEAD_SIZE)
                if back == 0:
                    l_acc[head, line, tokens] = total[:, own]
                    o_acc[part, tokens] = out[:, own]
                else:
                    l_acc[head, line, tokens] += total[:, own]
                    o_acc[part, tokens] += out[:, own]

    pl.when(me < n - 1)(lambda: climbs(1))
    for stages in each:
        stages[0](0)
        stages[0](1)
    level(0)
    for back in range(1, n):

        def step(back=back):
            for head in heads:
                climb(back, head).wait_recv()
                if back < n - 1:
                    pl.when(me < n - 1)(lambda head=head: climb(back + 1, head).start())
            level(back)

        pl.when(me >= back)(step)
        if back <= 2:
            for stages in each:
                stages[back]()

    @pl.loop(0, rows * KEY_VALUE_HEADS)
    def _(i):
        tokens, wide, pair, head = spans(i, length)
        for g in range(GROUP):
            line = slice(g, g + 1)
            part = pl.ds(wide.start + g * HEAD_SIZE, HEAD_SIZE)
            out = o_acc[part, tokens] / l_acc[head, line, tokens]
            o_acc[part, tokens] = out
            o_ref[part, tokens] = out.astype(BF16)
            lse_ref[head, line, tokens] = jnp.log(l_acc[head, line, tokens])

    if planes:
        tall = full_ref.shape[0] // 32
        filled[...] = jnp.zeros_like(filled)

        @pl.loop(0, 32)
        def _(i):
            src = pl.ds(pl.multiple_of(i * out_rows, 8), out_rows)
            dst = pl.ds(pl.multiple_of(i * tall, 8), out_rows)
            filled[dst, :] = o_acc[src, :]

        full_ref[...] = filled[...].astype(BF16)

    for back in range(1, n):
        for head in heads:
            pl.when((me >= back - 1) & (me < n - 1))(
                lambda back=back, head=head: climb(back, head).wait_send()
            )
    for stages in each:
        stages[3]()


def attend(start, queries, pairs, rows, n, more, out_rows):
    vmem, dma = pl.BlockSpec(memory_space=pltpu.VMEM), pltpu.SemaphoreType.DMA
    anywhere = pl.BlockSpec(memory_space=pl.ANY)
    count = queries.shape[1]
    lines = (KEY_VALUE_HEADS, 8, count)
    out_shape = [
        jax.ShapeDtypeStruct(queries.shape, BF16),
        jax.ShapeDtypeStruct(lines, F32),
        jax.ShapeDtypeStruct((n - 1, *pairs.shape), BF16),
    ]
    scratch, full = [], []
    if more:
        full = [(QW // out_rows * more[1].shape[1], count)]
        scratch.append(pltpu.VMEM(full[0], F32))
    scratch += [
        pltpu.VMEM(queries.shape, F32),
        pltpu.VMEM(lines, F32),
        dma((n - 1, KEY_VALUE_HEADS)),
        dma((n - 1, KEY_VALUE_HEADS)),
    ]
    for extra in more:
        out_shape.append(jax.ShapeDtypeStruct((8, *extra.shape), BF16))
        scratch += [dma, dma((8, 2)), dma((8, 2))]
    out_shape += [jax.ShapeDtypeStruct(shape, BF16) for shape in full]
    return pl.pallas_call(
        functools.partial(attend_kernel, n, rows, len(more), out_rows),
        in_specs=[vmem] * 3 + [anywhere] * len(more),
        out_specs=[vmem] * 3 + [anywhere] * len(more) + [vmem] * len(full),
        out_shape=out_shape,
        scratch_shapes=scratch,
        compiler_params=pltpu.CompilerParams(
            collective_id=2, has_side_effects=True, vmem_limit_bytes=48 * 2**20
        ),
        name="attend",
    )(start, queries, pairs, *more)


def plus(ref, *others):
    total = ref[...].astype(F32)
    for other in others:
        total += other[...].astype(F32)
    ref[...] = total.astype(BF16)


def attend_back_kernel(n, rows, summed, *refs):
    start_ref, q_ref, do_ref, o_ref, lse_ref, kv_ref, held, *refs = refs
    if summed:
        h_ref, w_ref, m_ref, *refs = refs
    dq_ref, dkv_ref, *refs = refs
    if summed:
        mixed_ref, *refs = refs
    inner, part, rcv, sent, got, *refs = refs
    d, me = lax.axis_index("dp"), lax.axis_index("seq")
    length = q_ref.shape[1] // rows
    if summed:
        place = places()
        d, me, d_c, d_x, d_y, _ = place
        w_v, h_v, m_v, w_sem, h_sem, m_sem, *refs = refs
        kept, leaving = refs[:2]
        m_load = pltpu.make_async_copy(m_ref, m_v, m_sem)
        load, product = block_products(h_ref, h_v, h_sem, lambda h, span: dot(h, w_v[:, span]))
        load(0).start()
        w_load = pltpu.make_async_copy(w_ref, w_v, w_sem)
        w_load.start()
        greet([(d_c, me), (d_x, me), (d_y, me)], (d, me))
        crossing, far, near, pass_on, end = plane_sums(*refs, place)

        def pair(turn, i):
            slot = turn // 2 % 2
            if turn >= 4:
                crossing(3 if slot == 0 else 1, slot).wait_send()
            product(turn, leaving.at[slot])
            crossing(i, slot).start()
            product(turn + 1, kept.at[i])

        def stage(i):
            if i == 0:
                w_load.wait()
                m_load.start()
                pair(0, 3)
                far()
            elif i == 1:
                pair(2, 1)
                near(1)
                pair(4, 2)
                near(2)
                pair(6, 0)
                near(0)
            elif i == 2:
                pass_on()
            else:
                end()
                m_load.wait()
                mixed_ref[...] = (kept[0].astype(F32) + m_v[...]).astype(BF16)
                crossing(2, 0).wait_send()
                crossing(0, 1).wait_send()
    else:
        greet([], (d, me))

        def stage(i):
            pass

    def descend(back):
        return remote(
            part.at[back - 1], rcv.at[back - 1], sent.at[back - 1], got.at[back - 1], (d, me - 1)
        )

    def level(back):
        @pl.loop(0, rows * KEY_VALUE_HEADS, unroll=2)
        def _(i):
            tokens, wide, pair, head = spans(i, length)
            block = kv_ref[pair, tokens] if back == 0 else held[back - 1, pair, tokens]
            keys_t = block[:HEAD_SIZE]
            keys, values = keys_t.T, block[HEAD_SIZE:].T
            q, do = abreast(q_ref[wide, tokens]), abreast(do_ref[wide, tokens])
            bias = seen(back, me, start_ref[0:1, tokens])
            p = jnp.exp(dot(keys, q) + (bias - across(lse_ref[head, :, tokens])))
            ds = (p * (dot(values, do) - across(inner[head, :, tokens]))).astype(BF16)
            dv = back_product(p.astype(BF16), do)
            dk = back_product(ds, q)
            dq = dot(keys_t, ds)
            if back == 0:
                dkv_ref[pair, tokens] = jnp.concatenate([dk.T, dv.T], axis=0)
            else:
                part[back - 1, pair, tokens] = jnp.concatenate([dk.T, dv.T], axis=0).astype(BF16)
            for g in range(GROUP):
                own = slice(g * length, (g + 1) * length)
                line = pl.ds(wide.start + g * HEAD_SIZE, HEAD_SIZE)
                dq_ref[line, tokens] += dq[:, own]

    def finish(back):
        def more():
            descend(back + 1).wait_recv()
            if back == 0:
                dkv_ref[...] += rcv[0].astype(F32)
            else:
                plus(part.at[back - 1], rcv.at[back])

        if back < n - 1:
            pl.when(me < n - 1)(more)
        if back > 0:
            descend(back).start()

    stage(0)
    dq_ref[...] = jnp.zeros_like(dq_ref)

    @pl.loop(0, rows * KEY_VALUE_HEADS)
    def _(i):
        tokens, wide, pair, head = spans(i, length)
        for g in range(GROUP):
            line = slice(g, g + 1)
            own = pl.ds(wide.start + g * HEAD_SIZE, HEAD_SIZE)
            product = do_ref[own, tokens].astype(F32) * o_ref[own, tokens].astype(F32)
            inner[head, line, tokens] = jnp.sum(product, axis=0, keepdims=True)

    for back in range(n - 1, -1, -1):

        def run(back=back):
            level(back)
            pl.when(me == n - 1)(lambda: finish(back))

        if back:
            pl.when(me >= back)(run)
        else:
            level(0)
            pl.when(me == n - 1)(lambda: finish(0))
        if back + 1 < n - 1:
            pl.when((me >= back + 1) & (me < n - 1))(lambda back=back: finish(back + 1))
        if n - 1 - back in (1, 2):
            stage(n - 1 - back)
    pl.when(me < n - 1)(lambda: finish(0))
    stage(3)
    for back in range(1, n):
        pl.when(me >= back)(lambda back=back: descend(back).wait_send())


def attend_back(start, queries, dheads, heads, lse, pairs, held, rows, n, more):
    vmem, dma = pl.BlockSpec(memory_space=pltpu.VMEM), pltpu.SemaphoreType.DMA
    anywhere = pl.BlockSpec(memory_space=pl.ANY)
    count = queries.shape[1]
    out_shape = [
        jax.ShapeDtypeStruct(queries.shape, F32),
        jax.ShapeDtypeStruct(pairs.shape, F32),
    ]
    scratch = [
        pltpu.VMEM((KEY_VALUE_HEADS, 8, count), F32),
        pltpu.VMEM((n - 1, *pairs.shape), BF16),
        pltpu.VMEM((n - 1, *pairs.shape), BF16),
        dma((n - 1,)),
        dma((n - 1,)),
    ]
    if more:
        (tokens, deep), (_, width) = more[0].shape, more[1].shape
        block = tokens // 8
        out_shape.append(jax.ShapeDtypeStruct((block, width), BF16))
        scratch += [
            pltpu.VMEM((deep, width), BF16),
            pltpu.VMEM((2, block, deep), BF16),
            pltpu.VMEM((block, width), F32),
            dma,
            dma((2,)),
            dma,
            *sums_scratch(block, width),
        ]
    return pl.pallas_call(
        functools.partial(attend_back_kernel, n, rows, bool(more)),
        in_specs=[vmem] * 7 + [anywhere] * len(more),
        out_specs=[vmem] * len(out_shape),
        out_shape=out_shape,
        scratch_shapes=scratch,
        compiler_params=pltpu.CompilerParams(
            collective_id=3, has_side_effects=True, vmem_limit_bytes=62 * 2**20
        ),
        name="attend_back",
    )(start, queries, dheads, heads, lse, pairs, held, *more)


def weights_kernel(n, *refs):
    x_refs, (w_ref, *out_refs), refs = refs[:n], refs[n : 2 * n + 1], refs[2 * n + 1 :]
    spread_ref, own_sem, recv, send_z, send_x, send_y, send_d, send_c, own_w, sent_w, got_w = refs
    d, s, d_c, d_x, d_y, line = places()
    d_d = d_x + 4 - 8 * line
    flip = d_c - d
    plane = (d, d_c, d_x, d_x + flip, d_y, d_y + flip, d_d, d_d + flip)
    greet([(other, s) for other in plane[1:]], (d, s))
    part = spread_ref.shape[2] // 2

    def columns(k, half):
        begin = half * 8 * part + plane[k] * part
        src = w_ref.at[:, pl.ds(pl.multiple_of(begin, 128), part)]
        dst = spread_ref.at[d, :, pl.ds(half * part, part)]
        if k == 0:
            return pltpu.make_async_copy(src, dst, own_w.at[half])
        return remote(src, dst, sent_w.at[k, half], got_w.at[k, half], (plane[k], s))

    def copies(slot, sent, got, peer, own=False, arrays=(0,)):
        return [
            remote(
                x_refs[i] if own else out_refs[i].at[slot if i == 0 else slot % 4],
                out_refs[i].at[slot if i == 0 else slot % 4],
                sent(i),
                got(i),
                peer,
            )
            for i in arrays
        ]

    def start(group):
        for one in group:
            one.start()

    def sent(group):
        for one in group:
            one.wait_send()

    def each(visit, between=lambda: None):
        visit(s, 0)
        between()
        for far in (1, 2, 3):
            pl.when(s >= far)(lambda far=far: visit(s - far, 1))
            pl.when(s + far <= 3)(lambda far=far: visit(s + far, -1))

    def got(k, b):
        return lambda i: recv.at[i, k, b]

    def arrived(k, b, arrays=(0,)):
        group = copies(d * 4 + b, lambda i: send_x.at[i, b], got(k, b), (d_x, s), arrays=arrays)
        for one in group:
            one.wait_recv()

    own = [
        pltpu.make_async_copy(x_refs[i], out_refs[i].at[d * 4 + s if i == 0 else s], own_sem.at[i])
        for i in range(n)
    ]
    start(own)

    def up(b, own=False, arrays=(0,)):
        return copies(d * 4 + b, lambda i: send_z.at[i, 0, b], got(0, b), (d, s + 1), own, arrays)

    def down(b, own=False, arrays=(0,)):
        return copies(d * 4 + b, lambda i: send_z.at[i, 1, b], got(0, b), (d, s - 1), own, arrays)

    def spread(b, own=False):
        return (
            copies(d * 4 + b, lambda i: send_x.at[i, b], got(2, b), (d_x, s), own)
            + copies(d * 4 + b, lambda i: send_y.at[i, b], got(4, b), (d_y, s), own)
            + copies(d * 4 + b, lambda i: send_c.at[i, 0, b], got(1, b), (d_c, s), own)
        )

    others = tuple(range(1, n))

    def line_block(b, direction, arrays):
        own = direction == 0
        if direction:
            arrived(0, b, arrays)
        if direction >= 0:
            pl.when(s < 3)(lambda: start(up(b, own, arrays)))
        if direction <= 0:
            pl.when(s > 0)(lambda: start(down(b, own, arrays)))

    def column_block(b, direction):
        line_block(b, direction, (0,))
        start(spread(b, direction == 0))

    def other_block(b, direction):
        if direction:
            line_block(b, direction, others)

    def start_columns():
        for k in range(8):
            for half in (0, 1):
                columns(k, half).start()

    each(column_block, start_columns)
    line_block(s, 0, others)

    def over_y(b):
        return copies(d_x * 4 + b, lambda i: send_d.at[i, b], got(6, b), (d_y, s))

    def over_x(b):
        return copies(d_y * 4 + b, lambda i: send_d.at[i, b], got(6, b), (d_x, s))

    def to_core(index, holder, b):
        return copies(
            holder * 4 + b, lambda i: send_c.at[i, index, b], got(2 * index + 1, b), (d_c, s)
        )

    def side_blocks(b, direction):
        arrived(2, b)
        pl.when(b % 2 == 0)(lambda: start(over_y(b)))
        start(to_core(1, d_x, b))
        arrived(4, b)
        pl.when(b % 2 == 1)(lambda: start(over_x(b)))
        start(to_core(2, d_y, b))

    each(side_blocks)

    def far_block(b, direction):
        arrived(6, b)
        start(to_core(3, d_d, b))

    each(other_block)
    each(far_block)

    def finish(b, direction):
        for k in (1, 3, 5, 7):
            arrived(k, b)
        if direction >= 0:
            pl.when(s < 3)(lambda: sent(up(b, arrays=range(n))))
        if direction <= 0:
            pl.when(s > 0)(lambda: sent(down(b, arrays=range(n))))
        sent(spread(b))
        sent(over_y(b))
        sent(to_core(1, d_x, b))
        sent(to_core(2, d_y, b))
        sent(to_core(3, d_d, b))

    each(finish)
    for one in own:
        one.wait()
    for k in range(8):
        for half in (0, 1):
            if k:
                columns(k, half).wait_recv()
                columns(k, half).wait_send()
            else:
                columns(k, half).wait()


def gather_weights(first, others, wide, n_dp, n_seq):
    rows, part = wide.shape[0], wide.shape[1] // (2 * n_dp)
    if (n_dp, n_seq) != (8, 4):
        spread = lax.all_to_all(wide.reshape(rows, 2, n_dp, part), "dp", 2, 0, tiled=False)
        spread = spread.reshape(n_dp, rows, 2 * part)
        return [lax.all_gather(x, BOTH, axis=0, tiled=False) for x in (first, *others)] + [spread]
    arrays = [first, *others]
    n = len(arrays)
    dma = pltpu.SemaphoreType.DMA
    return pl.pallas_call(
        functools.partial(weights_kernel, n),
        out_shape=[
            jax.ShapeDtypeStruct((n_seq if i else n_dp * n_seq, *x.shape), x.dtype)
            for i, x in enumerate(arrays)
        ]
        + [jax.ShapeDtypeStruct((n_dp, rows, 2 * part), wide.dtype)],
        in_specs=[pl.BlockSpec(memory_space=pl.ANY)] * (n + 1),
        out_specs=[pl.BlockSpec(memory_space=pl.ANY)] * (n + 1),
        scratch_shapes=[
            dma((n,)),
            dma((n, 8, 4)),
            dma((n, 2, 4)),
            dma((n, 4)),
            dma((n, 4)),
            dma((n, 4)),
            dma((n, 4, 4)),
            dma((2,)),
            dma((8, 2)),
            dma((8, 2)),
        ],
        compiler_params=pltpu.CompilerParams(collective_id=1, has_side_effects=True),
        name="gather_weights",
    )(*arrays, wide)


def weight_sums(product, refs, place):
    kept, leaving, rcv_c, rcv_d, rcv_x, rcv_y, rcv_z = refs[:7]
    sent_c, got_c, sent_p, got_p, sent_z, got_z = refs[7:]
    d, s, d_c, d_x, d_y, line = place
    holders = (d, d_x, d_y, d_x + d_y - d)
    flip = d_c - d
    low, high = pl.ds(0, 2), pl.ds(2, 2)

    def crossing(i, slot):
        return remote(leaving.at[slot], rcv_c.at[i], sent_c.at[i], got_c.at[i], (d_c, s))

    def pair(i, slot, before=None):
        if before is not None:
            crossing(before, slot).wait_send()
        product(holders[i] + flip, leaving.at[slot])
        crossing(i, slot).start()
        product(holders[i], kept.at[i])

    def merge(i):
        crossing(i, 0).wait_recv()
        plus(kept.at[i], rcv_c.at[i])

    def push(i):
        src, dst, peer = (
            (kept.at[3, low], rcv_d.at[low], d_x),
            (kept.at[3, high], rcv_d.at[high], d_y),
            (kept.at[1, low], rcv_x.at[low], d_x),
            (kept.at[2, high], rcv_y.at[high], d_y),
            (kept.at[2, low], rcv_y.at[low], d_y),
            (kept.at[1, high], rcv_x.at[high], d_x),
        )[i]
        return remote(src, dst, sent_p.at[i], got_p.at[i], (peer, s))

    def straight(b):
        return remote(kept.at[0, b], rcv_z.at[s], sent_z.at[b], got_z.at[s], (d, b))

    def from_line(b):
        return remote(kept.at[0, b], rcv_z.at[b], sent_z.at[b], got_z.at[b], (d, b))

    def far():
        pair(3, 0)
        pair(1, 1)
        merge(3)
        push(0).start()
        push(1).start()

    def near():
        pair(2, 0, 3)
        pair(0, 1, 1)
        merge(1)
        push(2).start()
        merge(2)
        push(3).start()
        merge(0)

    def pass_on():
        push(0).wait_recv()
        plus(kept.at[2, low], rcv_d.at[low])
        push(4).start()
        push(1).wait_recv()
        plus(kept.at[1, high], rcv_d.at[high])
        push(5).start()

    def along():
        for i in (2, 3, 4, 5):
            push(i).wait_recv()
        plus(kept.at[0], rcv_x, rcv_y)
        for b in range(4):
            pl.when(s != b)(lambda b=b: straight(b).start())

    def end(out_ref):
        out_ref[...] = kept[0, s].astype(F32)
        for b in range(4):

            @pl.when(s != b)
            def _(b=b):
                from_line(b).wait_recv()
                out_ref[...] += rcv_z[b].astype(F32)

        for b in range(4):
            pl.when(s != b)(lambda b=b: straight(b).wait_send())
        crossing(2, 0).wait_send()
        crossing(0, 1).wait_send()
        for i in range(6):
            push(i).wait_send()

    return far, near, pass_on, along, end


def weight_sums_scratch(rows, columns):
    dma = pltpu.SemaphoreType.DMA
    buffer = lambda *lead: pltpu.VMEM((*lead, rows, columns), BF16)
    return [
        buffer(4, 4),
        buffer(2, 4),
        buffer(4, 4),
        buffer(4),
        buffer(4),
        buffer(4),
        buffer(4),
        dma((4,)),
        dma((4,)),
        dma((6,)),
        dma((6,)),
        dma((4,)),
        dma((4,)),
    ]


def normed_back(dy, x, gain):
    inverse = lax.rsqrt(jnp.mean(x * x, axis=1, keepdims=True) + epsilon)
    gy = dy * gain
    x = x * inverse
    return inverse * (gy - x * jnp.mean(gy * x, axis=1, keepdims=True))


def middle_back_kernel(out_rows, dy_ref, mid_ref, g_ref, gain_ref, w_ref, dm_ref, low_ref, dh_ref, acc):
    dm = g_ref[...].astype(F32)
    dm += normed_back(dy_ref[...].astype(F32), mid_ref[...], gain_ref[...])
    dm_ref[...] = dm
    low = dm.astype(BF16)
    low_ref[...] = low
    tall = w_ref.shape[0] // 32
    heads = back_product(w_ref[...], low)
    for i in range(32):
        acc[i * out_rows : (i + 1) * out_rows, :] = heads[i * tall : i * tall + out_rows]
    dh_ref[...] = acc[...].astype(BF16)


def middle_back(dy, middle, g, gain, w, out_rows):
    count, width = middle.shape
    block = 256
    rows = pl.BlockSpec((block, width), lambda i: (i, 0))
    whole = lambda x: pl.BlockSpec(x.shape, lambda i: (0, 0))
    return pl.pallas_call(
        functools.partial(middle_back_kernel, out_rows),
        grid=(count // block,),
        in_specs=[rows] * 3 + [whole(gain), whole(w)],
        out_specs=[rows, rows, pl.BlockSpec((32 * out_rows, block), lambda i: (0, i))],
        out_shape=[
            jax.ShapeDtypeStruct((count, width), F32),
            jax.ShapeDtypeStruct((count, width), BF16),
            jax.ShapeDtypeStruct((32 * out_rows, count), BF16),
        ],
        scratch_shapes=[pltpu.VMEM((32 * out_rows, block), F32)],
        compiler_params=pltpu.CompilerParams(vmem_limit_bytes=56 * 2**20),
        name="middle_back",
    )(dy, middle, g, gain, w)


def sum_weights_kernel(n_ref, p_ref, h_ref, a_ref, few_ref, own_ref, *refs):
    w_ref, x_ref, dm_ref, back_0_ref, back_1_ref, gain_ref, wide_ref, *refs = refs
    qkv_out, small_out, out_out, dx_ref, wide_out, *refs = refs
    w_v, qkv_sum, out_sum, back_v, w_sem, own_sem, sent_w, got_w, *refs = refs
    w_load = pltpu.make_async_copy(w_ref, w_v, w_sem)
    w_load.start()
    place = places()
    d, s, d_c, d_x, d_y, line = place
    flip, d_d = d_c - d, d_x + d_y - d
    plane = (d, d_c, d_x, d_x + flip, d_y, d_y + flip, d_d, d_d + flip)
    greet([(other, s) for other in plane[1:]] + [(d, (s + i) % 4) for i in (1, 2, 3)])

    def exchange(k, i):
        src, dst = (back_0_ref, back_1_ref)[i].at[plane[k]], back_v.at[i, d]
        if k == 0:
            return pltpu.make_async_copy(src, dst, own_sem.at[i])
        return remote(src, dst, sent_w.at[k, i], got_w.at[k, i], (plane[k], s))

    width, chunk = p_ref.shape[0], 512

    def chunks(make, dst):
        @pl.loop(0, width // chunk)
        def _(c):
            span = pl.ds(pl.multiple_of(c * chunk, chunk), chunk)
            dst[:, :, span] = make(span).astype(BF16).reshape(*dst.shape[:2], chunk)

    def qkv_product(k, dst):
        tall = dst.shape[0] * dst.shape[1]
        rows = n_ref[:, pl.ds(pl.multiple_of(k * tall, tall), tall)].T
        chunks(lambda span: back_product(rows, p_ref[span, :]), dst)
        for b in range(4):
            dst[b, :16, -128:] = few_ref[k * 4 + b].astype(BF16)

    def out_product(k, dst):
        tall = dst.shape[0] * dst.shape[1]
        rows = h_ref[pl.ds(pl.multiple_of(k * tall, 16), tall), :]
        chunks(lambda span: dot(rows, a_ref[:, span]), dst)

    far, near, pass_on, along, end = weight_sums(qkv_product, refs[:13], place)
    far_2, near_2, pass_on_2, along_2, end_2 = weight_sums(out_product, refs[13:], place)
    block = 128

    def token_grads(first, count):
        def body(x_tile, dm_tile, dx_tile):
            i = pl.program_id(0) + first
            span = pl.ds(pl.multiple_of(i * block, block), block)
            dy = back_product(p_ref[:, span].T, w_v[...])
            dx_tile[...] = dm_tile[...] + normed_back(dy, x_tile[...].astype(F32), gain_ref[...])

        spec = lambda: pl.BlockSpec((block, x_ref.shape[1]), lambda i: (i + first, 0))
        pltpu.emit_pipeline(body, grid=(count,), in_specs=[spec(), spec()], out_specs=[spec()])(
            x_ref, dm_ref, dx_ref
        )

    blocks = x_ref.shape[0] // block
    far()
    near()
    w_load.wait()
    token_grads(0, 1)
    pass_on()
    far_2()
    near_2()
    token_grads(1, 2)
    along()
    pass_on_2()
    for k in range(8):
        exchange(k, 0).start()
        exchange(k, 1).start()
    token_grads(3, blocks - 3)
    along_2()
    end(qkv_sum)
    for i in (0, 1):
        exchange(0, i).wait()
        for k in range(1, 8):
            exchange(k, i).wait_recv()
            exchange(k, i).wait_send()
    part = back_v.shape[3]
    total = jnp.zeros((wide_out.shape[0], 1), F32)
    for j in range(16):
        half_j, holder = j // 8, j % 8
        span = slice(j * part, (j + 1) * part)
        grad = back_v[half_j, holder].astype(F32)
        wide_out[:, span] = grad
        total += jnp.sum(grad * wide_ref[:, span].astype(F32), axis=1, keepdims=True)
    tall = wide_out.shape[0]

    def as_row(column):
        return jnp.broadcast_to(column, (column.shape[0], 128)).T[0:1]

    small_out[...] = jnp.zeros_like(small_out)
    small_out[1:2, :tall] = as_row(total)
    inner = QW + 2 * KW
    total = jnp.sum(qkv_sum[:, :inner] * own_ref[:, :inner].astype(F32), axis=1, keepdims=True)
    small_out[0:1, :tall] = as_row(total)
    small_out[2:3, :16] = as_row(qkv_sum[:16, inner : inner + 1])
    qkv_out[...] = qkv_sum[:, :inner]
    end_2(out_sum)
    out_out[...] = out_sum[: out_out.shape[0]]


def sum_weights(normed, dprojected, heads, dattend, few, own, w, x, dmiddle, gain, back, back_1, wide, out_rows):
    dma, anywhere = pltpu.SemaphoreType.DMA, pl.BlockSpec(memory_space=pl.ANY)
    vmem = pl.BlockSpec(memory_space=pltpu.VMEM)
    rows, width = own.shape
    tall = heads.shape[0] // 32
    scratch = [
        pltpu.VMEM(w.shape, BF16),
        pltpu.VMEM(own.shape, F32),
        pltpu.VMEM((tall, width), F32),
        pltpu.VMEM((2, *back.shape), BF16),
        dma,
        dma((2,)),
        dma((8, 2)),
        dma((8, 2)),
    ]
    scratch += weight_sums_scratch(rows, width) + weight_sums_scratch(tall, width)
    return pl.pallas_call(
        sum_weights_kernel,
        out_shape=[
            jax.ShapeDtypeStruct((rows, QW + 2 * KW), F32),
            jax.ShapeDtypeStruct((8, 128), F32),
            jax.ShapeDtypeStruct((out_rows, width), F32),
            jax.ShapeDtypeStruct(dmiddle.shape, F32),
            jax.ShapeDtypeStruct(wide.shape, F32),
        ],
        in_specs=[vmem] * 6 + [anywhere] * 5 + [vmem] * 2,
        out_specs=[vmem] * 3 + [anywhere, vmem],
        scratch_shapes=scratch,
        compiler_params=pltpu.CompilerParams(
            collective_id=6, has_side_effects=True, vmem_limit_bytes=63 * 2**20
        ),
        name="sum_weights",
    )(normed, dprojected, heads, dattend, few, own, w, x, dmiddle, back, back_1, gain, wide)


def plane_kernel(rows, heads_ref, w_ref, x_ref, gain_ref, g_ref, down_ref, *refs):
    out_ref, dh_ref, mid_ref, w_v, x_v, down_v, mid_v, n_v, load, mid_sem, *refs = refs
    place = places()
    d, s, d_c, d_x, d_y, line = place
    w_load = pltpu.make_async_copy(w_ref, w_v, load.at[0])
    x_load = pltpu.make_async_copy(x_ref, x_v, load.at[1])
    down_load = pltpu.make_async_copy(down_ref, down_v, load.at[2])
    w_load.start()
    x_load.start()
    down_load.start()
    greet([(d_c, s), (d_x, s), (d_y, s)])
    begin, first, second, end = plane_stages(n_v, out_ref, *refs, place)
    w_load.wait()
    x_load.wait()
    width, chunk = mid_v.shape[1], 512

    def stored(row):
        tokens = pl.ds(row * (mid_v.shape[0] // rows), mid_v.shape[0] // rows)
        return pltpu.make_async_copy(mid_v.at[tokens], mid_ref.at[tokens], mid_sem.at[row])

    for row in range(rows):
        tokens = slice(row * (mid_v.shape[0] // rows), (row + 1) * (mid_v.shape[0] // rows))
        heads = heads_ref[:, tokens].T

        @pl.loop(0, width // chunk)
        def _(c):
            span = pl.ds(pl.multiple_of(c * chunk, chunk), chunk)
            weight = w_v[:, :, :, span].reshape(heads.shape[1], chunk)
            mid_v[tokens, span] = x_v[tokens, span].astype(F32) + dot(heads, weight)

        stored(row).start()
        mid = mid_v[tokens, :]
        inverse = lax.rsqrt(jnp.mean(mid * mid, axis=1, keepdims=True) + epsilon)
        n_v[tokens, :] = (mid * inverse * gain_ref[...]).astype(BF16)
        begin(row)
    down_load.wait()

    def body(g_tile, dh_tile):
        dh_tile[...] = back_product(g_tile[...], down_v[...]).astype(BF16)

    pltpu.emit_pipeline(
        body,
        grid=(g_ref.shape[0] // 512,),
        in_specs=[pl.BlockSpec((512, down_v.shape[1]), lambda i: (i, 0))],
        out_specs=[pl.BlockSpec((512, down_v.shape[0]), lambda i: (i, 0))],
    )(g_ref, dh_ref)
    first()
    second()
    end()
    for row in range(rows):
        stored(row).wait()


def plane_gather(heads, w, x, gain, g, down):
    dma, anywhere = pltpu.SemaphoreType.DMA, pl.BlockSpec(memory_space=pl.ANY)
    vmem = pl.BlockSpec(memory_space=pltpu.VMEM)
    everyone, dhidden, middle = pl.pallas_call(
        functools.partial(plane_kernel, 2),
        out_shape=[
            jax.ShapeDtypeStruct((8, *x.shape), BF16),
            jax.ShapeDtypeStruct((g.shape[0], down.shape[0]), BF16),
            jax.ShapeDtypeStruct(x.shape, F32),
        ],
        in_specs=[vmem, anywhere, anywhere, vmem, anywhere, anywhere],
        out_specs=[anywhere] * 3,
        scratch_shapes=[
            pltpu.VMEM(w.shape, BF16),
            pltpu.VMEM(x.shape, BF16),
            pltpu.VMEM(down.shape, BF16),
            pltpu.VMEM(x.shape, F32),
            pltpu.VMEM(x.shape, BF16),
            dma((3,)),
            dma((2,)),
            dma,
            dma((8, 2)),
            dma((8, 2)),
        ],
        compiler_params=pltpu.CompilerParams(
            collective_id=4, has_side_effects=True, vmem_limit_bytes=48 * 2**20
        ),
        name="plane_gather",
    )(heads, w, x, gain, g, down)
    return everyone.reshape(8 * x.shape[0], x.shape[1]), dhidden, middle


def transposed_kernel(x_ref, g_ref, out_ref):
    n_seq, n_dp, rows, _ = out_ref.shape
    total = outer_sum(x_ref[...], g_ref[...])
    for i in range(n_dp * n_seq):
        out_ref[i % n_seq, i // n_seq] = total[i * rows : (i + 1) * rows].astype(BF16)


def transposed_product(x, g, n_dp, n_seq, parts):
    (tokens, width), wide = x.shape, g.shape[1] // parts
    rows, tall = width // (n_dp * n_seq), 512
    return pl.pallas_call(
        transposed_kernel,
        grid=(width // tall,),
        in_specs=[
            pl.BlockSpec((tokens, tall), lambda i: (0, i)),
            pl.BlockSpec((tokens, wide), lambda i: (0, 0)),
        ],
        out_specs=pl.BlockSpec(
            (n_seq, tall // (n_seq * rows), rows, wide), lambda i: (0, i, 0, 0)
        ),
        out_shape=jax.ShapeDtypeStruct((n_seq, n_dp, rows, wide), BF16),
        compiler_params=pltpu.CompilerParams(vmem_limit_bytes=60 * 2**20),
        cost_estimate=pl.CostEstimate(
            flops=2 * tokens * width * wide,
            bytes_accessed=2 * (tokens * width + tokens * wide + width * wide),
            transcendentals=0,
        ),
        name="transposed_product",
    )(x, g)


def plane_sums(kept, leaving, rcv_c, rcv_d, rcv_x, rcv_y, sent_c, got_c, sent_p, got_p, place):
    d, s, d_c, d_x, d_y, line = place
    rows = kept.shape[1]
    low, high = pl.ds(0, rows // 2), pl.ds(rows // 2, rows // 2)

    def crossing(i, slot):
        return remote(leaving.at[slot], rcv_c.at[i], sent_c.at[i], got_c.at[i], (d_c, s))

    def merge(i):
        crossing(i, 0).wait_recv()
        plus(kept.at[i], rcv_c.at[i])

    def push(i):
        src, dst, peer = (
            (kept.at[3, low], rcv_d.at[low], d_x),
            (kept.at[3, high], rcv_d.at[high], d_y),
            (kept.at[1, low], rcv_x.at[low], d_x),
            (kept.at[2, high], rcv_y.at[high], d_y),
            (kept.at[2, low], rcv_y.at[low], d_y),
            (kept.at[1, high], rcv_x.at[high], d_x),
        )[i]
        return remote(src, dst, sent_p.at[i], got_p.at[i], (peer, s))

    def far():
        merge(3)
        push(0).start()
        push(1).start()

    def near(i):
        merge(i)
        if i:
            push(i + 1).start()

    def pass_on():
        push(0).wait_recv()
        plus(kept.at[2, low], rcv_d.at[low])
        push(4).start()
        push(1).wait_recv()
        plus(kept.at[1, high], rcv_d.at[high])
        push(5).start()

    def end():
        for i in (2, 3, 4, 5):
            push(i).wait_recv()
        plus(kept.at[0], rcv_x, rcv_y)
        for i in range(6):
            push(i).wait_send()

    return crossing, far, near, pass_on, end


def sums_scratch(rows, width):
    dma = pltpu.SemaphoreType.DMA
    buffer = lambda *lead: pltpu.VMEM((*lead, rows, width), BF16)
    return [
        buffer(4),
        buffer(2),
        buffer(4),
        buffer(),
        buffer(),
        buffer(),
        dma((4,)),
        dma((4,)),
        dma((6,)),
        dma((6,)),
    ]


ORDER = (7, 6, 3, 2, 5, 4, 1, 0)


def block_products(g_ref, g_v, g_sem, multiply):
    rows = g_v.shape[1]

    def load(turn):
        block = pl.ds(ORDER[turn] * rows, rows)
        return pltpu.make_async_copy(g_ref.at[block], g_v.at[turn % 2], g_sem.at[turn % 2])

    def product(turn, dst):
        if turn + 1 < 8:
            load(turn + 1).start()
        load(turn).wait()
        chunk = 512

        @pl.loop(0, dst.shape[1] // chunk)
        def _(c):
            span = pl.ds(pl.multiple_of(c * chunk, chunk), chunk)
            dst[:, span] = multiply(g_v[turn % 2], span).astype(BF16)

    return load, product


def plane_sum_kernel(
    g_ref, w_ref, h_ref, t_ref, x_ref, out_ref, grad_ref, wide_ref, w_v, g_v, h_v, *refs
):
    w_sem, g_sem, h_sem, out_sem, *refs = refs
    place = places()
    d, s, d_c, d_x, d_y, line = place
    kept, leaving = refs[:2]
    w_wait = load_rows(w_ref, w_v, w_sem, 8, 4)
    load, product = block_products(
        g_ref, g_v, g_sem, lambda g, span: back_product(g, w_v[span, :])
    )
    load(0).start()
    h_load = pltpu.make_async_copy(h_ref, h_v, h_sem)
    h_load.start()
    greet([(d_c, s), (d_x, s), (d_y, s)])
    crossing, far, near, pass_on, end = plane_sums(*refs, place)
    w_wait()

    def pair(turn, i):
        slot = turn // 2 % 2
        if turn >= 4:
            crossing(3 if slot == 0 else 1, slot).wait_send()
        product(turn, leaving.at[slot])
        crossing(i, slot).start()
        product(turn + 1, kept.at[i])

    pair(0, 3)
    far()
    pair(2, 1)
    pair(4, 2)
    near(1)
    near(2)
    pair(6, 0)
    near(0)
    h_load.wait()

    def grad_body(t_tile, grad_tile):
        grad_tile[...] = outer_sum(h_v[...], t_tile[...]).astype(BF16)

    tokens, deep = h_v.shape
    wide = 256

    def grad_tiles(first, count):
        pltpu.emit_pipeline(
            grad_body,
            grid=(count,),
            in_specs=[pl.BlockSpec((tokens, wide), lambda i: (0, first + i))],
            out_specs=[pl.BlockSpec((deep, wide), lambda i: (0, first + i))],
        )(t_ref, grad_ref)

    def wide_body(x_tile, wide_tile):
        total = outer_sum(x_tile[...], h_v[...])
        high = wide_tile.shape[2]
        for j in range(4):
            wide_tile[j, 0] = total[j * high : (j + 1) * high].astype(BF16)

    grad_tiles(0, 2)
    pass_on()
    grad_tiles(2, t_ref.shape[1] // wide - 2)
    h_load = pltpu.make_async_copy(g_ref.at[:, pl.ds(deep, deep)], h_v, h_sem)
    h_load.start()
    h_load.wait()
    pltpu.emit_pipeline(
        wide_body,
        grid=(8,),
        in_specs=[pl.BlockSpec((tokens, x_ref.shape[1] // 8), lambda i: (0, i))],
        out_specs=[
            pl.BlockSpec((4, 1, x_ref.shape[1] // 32, deep), lambda i: (0, i, 0, 0))
        ],
    )(x_ref, wide_ref)
    end()
    out = pltpu.make_async_copy(kept.at[0], out_ref, out_sem)
    out.start()
    crossing(2, 0).wait_send()
    crossing(0, 1).wait_send()
    out.wait()


def plane_sum(g, w, h, t, x, rows):
    dma, anywhere = pltpu.SemaphoreType.DMA, pl.BlockSpec(memory_space=pl.ANY)
    width, deep = w.shape
    return pl.pallas_call(
        plane_sum_kernel,
        out_shape=[
            jax.ShapeDtypeStruct((rows, width), BF16),
            jax.ShapeDtypeStruct((h.shape[1], t.shape[1]), BF16),
            jax.ShapeDtypeStruct((4, 8, width // 32, h.shape[1]), BF16),
        ],
        in_specs=[anywhere] * 5,
        out_specs=[anywhere] * 3,
        scratch_shapes=[
            pltpu.VMEM((width, deep), BF16),
            pltpu.VMEM((2, rows, deep), BF16),
            pltpu.VMEM(h.shape, BF16),
            dma,
            dma((2,)),
            dma,
            dma,
            *sums_scratch(rows, width),
        ],
        compiler_params=pltpu.CompilerParams(
            collective_id=5, has_side_effects=True, vmem_limit_bytes=62 * 2**20
        ),
        name="plane_sum",
    )(g, w, h, t, x)


def sigmoid(v):
    return 1.0 / (1.0 + jnp.exp(-v))


def load_rows(w_ref, w_v, sem, n_dp, n_seq):
    rows = w_v.shape[0] // (n_dp * n_seq)

    @pl.loop(0, n_dp * n_seq)
    def _(i):
        src = pl.ds(pl.multiple_of(i * rows, rows), rows)
        place = (i % n_dp) * n_seq + i // n_dp
        dst = pl.ds(pl.multiple_of(place * rows, rows), rows)
        pltpu.make_async_copy(w_ref.at[src], w_v.at[dst], sem).start()

    return pltpu.make_async_copy(w_ref, w_v, sem).wait


def gate_up_kernel(n_dp, n_seq, x_ref, dh_ref, w_ref, hidden_ref, dgu_ref, w_v, sem):
    pl.when(pl.program_id(0) == 0)(lambda: load_rows(w_ref, w_v, sem, n_dp, n_seq)())
    part = hidden_ref.shape[1]
    step = 256 if part % 256 == 0 else 128
    for c in range(0, part, step):
        first, second = slice(c, c + step), slice(part + c, part + c + step)
        gate, up = dot(x_ref[...], w_v[:, first]), dot(x_ref[...], w_v[:, second])
        dhidden = dh_ref[:, first].astype(F32)
        sig = sigmoid(gate)
        silu = gate * sig
        hidden_ref[:, first] = (silu * up).astype(BF16)
        dgu_ref[:, first] = (dhidden * up * (sig + silu * (1.0 - sig))).astype(BF16)
        dgu_ref[:, second] = (dhidden * silu).astype(BF16)


def gate_up_product(x, dhidden, w, n_dp, n_seq):
    tokens, width = x.shape
    wide = w.shape[1]
    block = 512
    span = lambda columns: pl.BlockSpec((block, columns), lambda i: (i, 0))
    return pl.pallas_call(
        functools.partial(gate_up_kernel, n_dp, n_seq),
        grid=(tokens // block,),
        in_specs=[span(width), span(wide // 2), pl.BlockSpec(memory_space=pl.ANY)],
        out_specs=[span(wide // 2), span(wide)],
        out_shape=[
            jax.ShapeDtypeStruct((tokens, wide // 2), BF16),
            jax.ShapeDtypeStruct((tokens, wide), BF16),
        ],
        scratch_shapes=[pltpu.VMEM(w.shape, BF16), pltpu.SemaphoreType.DMA],
        compiler_params=pltpu.CompilerParams(vmem_limit_bytes=56 * 2**20),
        cost_estimate=pl.CostEstimate(
            flops=2 * tokens * width * wide,
            bytes_accessed=2 * (tokens * width + width * wide + tokens * wide * 2),
            transcendentals=tokens * wide // 2,
        ),
        name="gate_up",
    )(x, dhidden, w)


def mm(a, b):
    return jnp.dot(a, b, preferred_element_type=F32)


def outer_sum(left, right):
    return lax.dot_general(left, right, (((0,), (0,)), ((), ())), preferred_element_type=F32)


def back_product(rows, weight):
    return lax.dot_general(rows, weight, (((1,), (1,)), ((), ())), preferred_element_type=F32)


def gather(x, axes):
    return lax.all_gather(x, axes, axis=0, tiled=True)


def scatter(x, axes):
    return lax.psum_scatter(x, axes, scatter_dimension=0, tiled=True)


def shards(
    tokens, lengths, w_qkv, w_out, w_gate_up, w_down, attn_gain, ffn_gain, head_gains, out_grad
):
    n_dp, n_seq = lax.axis_size("dp"), lax.axis_size("seq")
    rows, length, width = tokens.shape
    count = rows * length
    ff = w_gate_up.shape[1] // 2
    part = ff // n_dp
    wr = w_gate_up.shape[0]
    offset = lax.axis_index("seq") * length
    local_pos = offset + jnp.arange(length, dtype=jnp.int32)
    cosine, sine = rope_tables(jnp.concatenate([local_pos] * rows))
    ends = jnp.cumsum(lengths, axis=1, dtype=jnp.int32)
    start = jnp.sum(
        jnp.where(local_pos[None, :, None] >= ends[:, None, :], lengths[:, None, :], 0), axis=2
    ).reshape(1, count)
    start = jnp.broadcast_to(start, (8, count))

    full = (n_dp, n_seq) == (8, 4)
    qkv_w = w_qkv.shape[1]
    spare = width - qkv_w
    gains = jnp.concatenate([attn_gain, ffn_gain])
    gains = [jnp.pad(g, (0, spare - g.shape[0]))[None] for g in (gains, head_gains)]
    gains.append(jnp.zeros((wr - 2, spare), BF16))
    own_qkv = jnp.concatenate([w_qkv, jnp.concatenate(gains, axis=0)], axis=1)
    out_rows = w_out.shape[0]
    own_out = jnp.pad(w_out, ((0, -out_rows % 16), (0, 0)))
    all_qkv, some_out, spread = gather_weights(own_qkv, [own_out], w_gate_up, n_dp, n_seq)
    qkv_full = all_qkv.reshape(width, width)
    attn_gain_full = all_qkv[:, 0, qkv_w : qkv_w + wr].reshape(-1).astype(F32)
    ffn_gain_full = all_qkv[:, 0, qkv_w + wr : qkv_w + 2 * wr].reshape(-1).astype(F32)
    head_full = all_qkv[:, 1, qkv_w : qkv_w + head_gains.shape[0]].reshape(-1).astype(F32)

    attn_gain_full, ffn_gain_full, head_full = lax.optimization_barrier(
        (attn_gain_full[None], ffn_gain_full[None], head_full)
    )

    w_down, qkv_full = lax.optimization_barrier((w_down, qkv_full))
    down_w = gather(w_down, "seq")
    cotangent_low = out_grad.reshape(count, width)

    x_rows = tokens.reshape(count, width).astype(F32)
    normed_low = norm_rows(x_rows, attn_gain_full).astype(BF16)
    projected = lax.dot_general(
        qkv_full, normed_low, (((0,), (1,)), ((), ())), preferred_element_type=F32
    )

    queries, pairs = prepare(projected, head_full[:, None], cosine, sine)
    more = [cotangent_low, some_out] if full else []
    heads_out, lse, held, *planes = attend(start, queries, pairs, rows, n_seq, more, out_rows)
    gate_up_w = gather(spread.reshape(n_dp * wr, 2 * part), "seq")
    if full:
        cotangent_all, all_out, heads_full = planes
        cotangent_all = cotangent_all.reshape(n_dp * count, width)
        out_full = all_out.reshape(-1, width)
        normed2_all, dhidden, middle = plane_gather(
            heads_full, all_out, tokens.reshape(count, width), ffn_gain_full,
            cotangent_all, down_w,
        )
    else:
        cotangent_all, all_out = gather(cotangent_low, "dp"), some_out
        out_full = all_out.reshape(-1, width)
        fill = ((0, 0), (0, all_out.shape[1] - out_rows), (0, 0))
        heads_full = jnp.pad(heads_out.reshape(n_dp * n_seq, out_rows, count), fill)
        heads_full = heads_full.reshape(-1, count)
        middle = x_rows + outer_sum(heads_full, out_full)
        normed2_all = gather(norm_rows(middle, ffn_gain_full).astype(BF16), "dp")
        dhidden = back_product(cotangent_all, down_w).astype(BF16)
    hidden, dgate_up = gate_up_product(normed2_all, dhidden, gate_up_w, n_dp, n_seq)
    gate_grad = transposed_product(normed2_all, dgate_up, n_dp, n_seq, 2 if full else 1)
    gate_grad, dgate_up = lax.optimization_barrier((gate_grad, dgate_up))
    gate_grad = scatter(gate_grad.reshape(width, -1), "seq")
    if full:
        dnormed2, down_grad, up_grad = plane_sum(
            dgate_up, gate_up_w, hidden, cotangent_all, normed2_all, count
        )
        gate_grad, up_grad, dnormed2 = lax.optimization_barrier((gate_grad, up_grad, dnormed2))
        up_grad = scatter(up_grad.reshape(width, part), "seq")
    else:
        ordered = gate_up_w.reshape(n_seq, n_dp, wr, 2 * part).transpose(1, 0, 2, 3)
        ordered = ordered.reshape(width, 2 * part)
        dnormed2 = scatter(back_product(dgate_up, ordered).astype(BF16), "dp")
        down_grad = outer_sum(hidden, cotangent_all).astype(BF16)
    if full:
        dmiddle, dattend, dheads = middle_back(
            dnormed2, middle, cotangent_low, ffn_gain_full, out_full, out_rows
        )
    else:
        dmiddle = cotangent_low.astype(F32)
        dmiddle += normed_back(dnormed2.astype(F32), middle, ffn_gain_full)
        dattend = dmiddle.astype(BF16)
        dheads = back_product(out_full, dattend).astype(BF16).reshape(n_dp * n_seq, -1, count)
        dheads = dheads[:, :out_rows].reshape(QW, count)
    if full:
        dqueries, dpairs, mixed = attend_back(
            start, queries, dheads, heads_out, lse, pairs, held, rows, n_seq,
            [hidden, down_w, middle],
        )
    else:
        dqueries, dpairs = attend_back(
            start, queries, dheads, heads_out, lse, pairs, held, rows, n_seq, []
        )
        mixed = middle + scatter(mm(hidden, down_w).astype(BF16), "dp").astype(F32)
    if full:
        gate_grad, up_grad, dqueries = lax.optimization_barrier((gate_grad, up_grad, dqueries))
        up_grad = up_grad.reshape(n_dp, wr, part)
    gate_grad = gate_grad.reshape(n_dp, wr, -1)
    down_grad, dqueries = lax.optimization_barrier((down_grad, dqueries))
    down_grad = scatter(down_grad, "seq")
    dprojected_low, head_grad = prepare_back(
        projected, head_full[:, None], cosine, sine, dqueries, dpairs, width, n_dp * n_seq
    )
    few = head_gains.shape[0]
    if full:
        qkv_grad, small, out_weight_grad, tokens_grad, gate_up_grad = (
            sum_weights(
                normed_low,
                dprojected_low,
                heads_full,
                dattend,
                head_grad,
                own_qkv,
                qkv_full,
                tokens.reshape(count, width),
                dmiddle,
                attn_gain_full,
                gate_grad,
                up_grad,
                w_gate_up,
                out_rows,
            )
        )
        qkv_products, ffn_products, head_out = small[0, :wr], small[1, :wr], small[2, :few]
    else:
        qkv_grad = lax.dot_general(
            normed_low, dprojected_low, (((0,), (1,)), ((), ())), preferred_element_type=F32
        ).astype(BF16)
        out_grads = mm(heads_full, dattend).astype(BF16)
        qkv_grad, out_weight_grad = (
            scatter(scatter(g, "dp"), "seq").astype(F32) for g in (qkv_grad, out_grads)
        )
        head_out = jnp.sum(
            lax.all_to_all(head_grad[:, :few, 0], BOTH, 0, 0, tiled=True), axis=0
        )
        qkv_products = jnp.sum(own_qkv[:, :qkv_w].astype(F32) * qkv_grad[:, :qkv_w], axis=1)
        qkv_grad = qkv_grad[:, :qkv_w]
        gate_up_grad = lax.all_to_all(gate_grad, "dp", 0, 0, tiled=True)
        gate_up_grad = gate_up_grad.reshape(n_dp, wr, 2, part).transpose(1, 2, 0, 3)
        gate_up_grad = gate_up_grad.reshape(wr, 2 * ff).astype(F32)
        ffn_products = jnp.sum(w_gate_up.astype(F32) * gate_up_grad, axis=1)
        dnormed = back_product(dprojected_low.T, qkv_full)
        tokens_grad = dmiddle + normed_back(dnormed, x_rows, attn_gain_full)
    attn_gain_out = qkv_products / attn_gain.astype(F32)
    ffn_gain_out = ffn_products / ffn_gain.astype(F32)
    return (
        mixed.astype(BF16).reshape(rows, length, width),
        tokens_grad.reshape(rows, length, width),
        qkv_grad,
        out_weight_grad[:out_rows],
        gate_up_grad,
        down_grad.astype(F32),
        attn_gain_out,
        ffn_gain_out,
        head_out,
    )


def solution(mesh):
    in_specs = (
        P("dp", "seq", None),
        P("dp", None),
        P(("dp", "seq"), None),
        P(("dp", "seq"), None),
        P(("dp", "seq"), None),
        P(("dp", "seq"), None),
        P(("dp", "seq")),
        P(("dp", "seq")),
        P(("dp", "seq")),
        P("dp", "seq", None),
    )
    out_specs = (
        P("dp", "seq", None),
        P("dp", "seq", None),
        P(("dp", "seq"), None),
        P(("dp", "seq"), None),
        P(("dp", "seq"), None),
        P(("dp", "seq"), None),
        P(("dp", "seq")),
        P(("dp", "seq")),
        P(("dp", "seq")),
    )
    return jax.shard_map(shards, mesh=mesh, in_specs=in_specs, out_specs=out_specs, check_vma=False)
```

```python
import functools

import jax
import jax.numpy as jnp
from jax import lax
from jax.experimental import pallas as pl
from jax.experimental.pallas import tpu as pltpu
from jax.sharding import PartitionSpec as P

QUERY_HEADS = 20
KEY_VALUE_HEADS = 5
HEAD_SIZE = 64
GROUP = QUERY_HEADS // KEY_VALUE_HEADS
QW = QUERY_HEADS * HEAD_SIZE
KW = KEY_VALUE_HEADS * HEAD_SIZE
BOTH = ("dp", "seq")

epsilon = 1e-06
F32 = jnp.float32
BF16 = jnp.bfloat16
MESH = pl.DeviceIdType.MESH


def norm_rows(inputs, scales):
    return inputs * lax.rsqrt(jnp.mean(inputs * inputs, axis=-1, keepdims=True) + epsilon) * scales


def rope_tables(positions):
    inverse_freq = 10000.0 ** (-(jnp.arange(HEAD_SIZE // 2, dtype=F32) * 2.0 / HEAD_SIZE))
    angles = inverse_freq[:, None] * positions.astype(F32)[None, :]
    return (jnp.cos(angles), jnp.sin(angles))


def head_rows(i):
    return pl.ds(pl.multiple_of(i * HEAD_SIZE, HEAD_SIZE), HEAD_SIZE)


def key_rows(i):
    return head_rows(2 * i), head_rows(2 * i + 1)


def unit(v):
    inverse = lax.rsqrt(jnp.mean(v * v, axis=0, keepdims=True) + epsilon)
    return v * inverse, inverse


def prepare_kernel(p_ref, gain_ref, cos_ref, sin_ref, q_ref, kv_ref):
    cosine, sine = cos_ref[...], sin_ref[...]

    def turned(v, gain):
        v = unit(v)[0] * gain
        first, second = v[: HEAD_SIZE // 2], v[HEAD_SIZE // 2 :]
        return jnp.concatenate(
            [first * cosine - second * sine, second * cosine + first * sine], axis=0
        )

    @pl.loop(0, KEY_VALUE_HEADS, unroll=KEY_VALUE_HEADS)
    def _(i):
        key, value = key_rows(i)
        keys_in = p_ref[head_rows(QUERY_HEADS + i), :]
        kv_ref[key, :] = turned(keys_in, gain_ref[HEAD_SIZE:, :]).astype(BF16)
        values_in = p_ref[head_rows(QUERY_HEADS + KEY_VALUE_HEADS + i), :]
        kv_ref[value, :] = values_in.astype(BF16)

    @pl.loop(0, QUERY_HEADS, unroll=KEY_VALUE_HEADS)
    def _(i):
        rows = head_rows(i)
        queries = turned(p_ref[rows, :], gain_ref[:HEAD_SIZE, :]) * HEAD_SIZE**-0.5
        q_ref[rows, :] = queries.astype(BF16)


def prepare(projected, gains, cosine, sine):
    tokens = projected.shape[1]
    return pl.pallas_call(
        prepare_kernel,
        out_shape=[
            jax.ShapeDtypeStruct((QW, tokens), BF16),
            jax.ShapeDtypeStruct((2 * KW, tokens), BF16),
        ],
        compiler_params=pltpu.CompilerParams(vmem_limit_bytes=40 * 2**20),
        name="prepare",
    )(projected, gains, cosine, sine)


def prepare_back_kernel(
    p_ref, gain_ref, cos_ref, sin_ref, dq_ref, dkv_ref, out_ref, dg_ref, acc_q, acc_k
):
    cosine, sine = cos_ref[...], sin_ref[...]
    step = pl.program_id(0)

    @pl.when(step == 0)
    def _():
        acc_q[...] = jnp.zeros_like(acc_q)
        acc_k[...] = jnp.zeros_like(acc_k)

    def back(v, gain, dy, acc):
        u, inverse = unit(v)
        first, second = dy[: HEAD_SIZE // 2], dy[HEAD_SIZE // 2 :]
        dz = jnp.concatenate(
            [first * cosine + second * sine, second * cosine - first * sine], axis=0
        )
        acc[...] += dz * u
        du = dz * gain
        return inverse * (du - u * jnp.mean(du * u, axis=0, keepdims=True))

    @pl.loop(0, KEY_VALUE_HEADS, unroll=KEY_VALUE_HEADS)
    def _(i):
        key, value = key_rows(i)
        rows = head_rows(QUERY_HEADS + i)
        dv = back(p_ref[rows, :], gain_ref[HEAD_SIZE:, :], dkv_ref[key, :], acc_k)
        out_ref[rows, :] = dv.astype(BF16)
        out_ref[head_rows(QUERY_HEADS + KEY_VALUE_HEADS + i), :] = dkv_ref[value, :].astype(BF16)

    @pl.loop(0, QUERY_HEADS, unroll=KEY_VALUE_HEADS)
    def _(i):
        rows = head_rows(i)
        dy = dq_ref[rows, :] * HEAD_SIZE**-0.5
        dv = back(p_ref[rows, :], gain_ref[:HEAD_SIZE, :], dy, acc_q)
        out_ref[rows, :] = dv.astype(BF16)

    rest = out_ref.shape[0] - QW - 2 * KW
    out_ref[QW + 2 * KW :, :] = jnp.zeros((rest, out_ref.shape[1]), BF16)

    @pl.when(step == pl.num_programs(0) - 1)
    def _():
        few = 2 * HEAD_SIZE // dg_ref.shape[0]
        dg_ref[...] = jnp.zeros_like(dg_ref)
        for half, acc in enumerate((acc_q, acc_k)):
            total = jnp.sum(acc[...], axis=1, keepdims=True)
            total = jnp.broadcast_to(total, (HEAD_SIZE, dg_ref.shape[2]))
            for i in range(HEAD_SIZE // few):
                dg_ref[half * (HEAD_SIZE // few) + i, :few, :] = total[i * few : (i + 1) * few]


def prepare_back(projected, gains, cosine, sine, dqueries, dpairs, width, devices):
    tokens = projected.shape[1]
    block = min(256, tokens)
    some = lambda x, rows=None: pl.BlockSpec((rows or x.shape[0], block), lambda i: (0, i))
    return pl.pallas_call(
        prepare_back_kernel,
        grid=(tokens // block,),
        in_specs=[
            some(projected, QW + 2 * KW),
            pl.BlockSpec(gains.shape, lambda i: (0, 0)),
            *[some(x) for x in (cosine, sine, dqueries, dpairs)],
        ],
        out_specs=[
            pl.BlockSpec((width, block), lambda i: (0, i)),
            pl.BlockSpec((devices, 16, 128), lambda i: (0, 0, 0)),
        ],
        out_shape=[
            jax.ShapeDtypeStruct((width, tokens), BF16),
            jax.ShapeDtypeStruct((devices, 16, 128), F32),
        ],
        scratch_shapes=[pltpu.VMEM((HEAD_SIZE, block), F32)] * 2,
        compiler_params=pltpu.CompilerParams(vmem_limit_bytes=62 * 2**20),
        name="prepare_back",
    )(projected, gains, cosine, sine, dqueries, dpairs)


def dot(a, b):
    return jnp.dot(a, b, preferred_element_type=F32)


def places():
    d, s = lax.axis_index("dp"), lax.axis_index("seq")
    core, column, line = d % 2, (d // 2) % 2, d // 4
    return d, s, d + 1 - 2 * core, d + 2 - 4 * column, d + 4 - 8 * line, line


def greet(peers, line=None):
    barrier = pltpu.get_barrier_semaphore()

    def signal(peer):
        pl.semaphore_signal(barrier, inc=1, device_id=peer, device_id_type=MESH)

    for peer in peers:
        signal(peer)
    if line is None:
        pl.semaphore_wait(barrier, len(peers))
        return
    d, s = line
    last = lax.axis_size("seq") - 1
    pl.when(s < last)(lambda: signal((d, s + 1)))
    pl.when(s > 0)(lambda: signal((d, s - 1)))
    pl.semaphore_wait(barrier, len(peers) + 1 - s // last + (s + last - 1) // last)


def remote(src, dst, sent, got, peer):
    return pltpu.make_async_remote_copy(
        src_ref=src,
        dst_ref=dst,
        send_sem=sent,
        recv_sem=got,
        device_id=peer,
        device_id_type=MESH,
    )


def plane_stages(x_ref, out_ref, own_sem, sent, got, place, ordered=False):
    d, s, d_c, d_x, d_y, line = place
    flip, d_d = d_c - d, d_x + d_y - d
    slots = list(range(8))
    if ordered:
        slots = [d, d_c, d_x, d_x + flip, d_y, d_y + flip, d_d, d_d + flip]
    half = x_ref.shape[0] // 2
    halves = (pl.ds(0, half), pl.ds(half, half))
    source = {1: 0, 2: 0, 4: 0, 3: 2, 5: 4, 7: 6}

    def piece(k, h, peer):
        back = source[k] if k in source else (4 if h == 0 else 2)
        src = x_ref.at[halves[h]] if back == 0 else out_ref.at[slots[back], halves[h]]
        dst = out_ref.at[slots[back] if ordered else k, halves[h]]
        return remote(src, dst, sent.at[k, h], got.at[k, h], (peer, s))

    own = pltpu.make_async_copy(x_ref, out_ref.at[slots[0]], own_sem)

    def begin(h):
        for k, peer in ((2, d_x), (4, d_y), (1, d_c)):
            piece(k, h, peer).start()
        if h:
            own.start()

    def first():
        piece(4, 0, d_y).wait_recv()
        piece(6, 0, d_x).start()
        piece(5, 0, d_c).start()
        piece(2, 0, d_x).wait_recv()
        piece(3, 0, d_c).start()

    def second():
        piece(2, 1, d_x).wait_recv()
        piece(6, 1, d_y).start()
        piece(3, 1, d_c).start()
        piece(4, 1, d_y).wait_recv()
        piece(5, 1, d_c).start()

    def end():
        for h in (0, 1):
            piece(6, h, d_x).wait_recv()
            piece(7, h, d_c).start()
        for k in (1, 3, 5, 7):
            for h in (0, 1):
                piece(k, h, d_c).wait_recv()
        for k in range(1, 8):
            for h in (0, 1):
                piece(k, h, d_c).wait_send()
        own.wait()

    return begin, first, second, end


def abreast(block):
    return jnp.concatenate(
        [block[i * HEAD_SIZE : (i + 1) * HEAD_SIZE] for i in range(GROUP)], axis=1
    )


def across(rows):
    return jnp.concatenate([rows[i : i + 1] for i in range(GROUP)], axis=1)


def seen(back, me, start):
    length = start.shape[1]
    key = lax.broadcasted_iota(jnp.int32, (length, length), 0)
    found = key + (me - back) * length >= start
    if back == 0:
        found &= key <= lax.broadcasted_iota(jnp.int32, (length, length), 1)
    bias = jnp.where(found, 0.0, -1e30)
    return jnp.concatenate([bias] * GROUP, axis=1)


def spans(i, length):
    row, head = i // KEY_VALUE_HEADS, i % KEY_VALUE_HEADS
    wide, pair = GROUP * HEAD_SIZE, 2 * HEAD_SIZE
    tokens = pl.ds(pl.multiple_of(row * length, length), length)
    return (
        tokens,
        pl.ds(pl.multiple_of(head * wide, wide), wide),
        pl.ds(pl.multiple_of(head * pair, pair), pair),
        head,
    )


def attend_kernel(n, rows, planes, out_rows, start_ref, q_ref, kv_ref, *refs):
    x_refs, refs = refs[:planes], refs[planes:]
    o_ref, lse_ref, held, *refs = refs
    out_refs, refs = refs[:planes], refs[planes:]
    if planes:
        full_ref, filled, *refs = refs
    o_acc, l_acc, sent, got, *refs = refs
    d, me = lax.axis_index("dp"), lax.axis_index("seq")
    length = q_ref.shape[1] // rows
    if planes:
        place = places()
        d, me, d_c, d_x, d_y, _ = place
        greet([(d_c, me), (d_x, me), (d_y, me)], (d, me))
        each = [
            plane_stages(x_refs[i], out_refs[i], *refs[3 * i : 3 * i + 3], place, i > 0)
            for i in range(planes)
        ]
    else:
        greet([], (d, me))
        each = []

    def climb(step, head):
        lines = pl.ds(head * 2 * HEAD_SIZE, 2 * HEAD_SIZE)
        src = kv_ref.at[lines] if step == 1 else held.at[step - 2, lines]
        dst = held.at[step - 1, lines]
        return remote(src, dst, sent.at[step - 1, head], got.at[step - 1, head], (d, me + 1))

    heads = range(KEY_VALUE_HEADS)

    def climbs(step):
        for head in heads:
            climb(step, head).start()

    def level(back):
        @pl.loop(0, rows * KEY_VALUE_HEADS, unroll=KEY_VALUE_HEADS)
        def _(i):
            tokens, wide, pair, head = spans(i, length)
            block = kv_ref[pair, tokens] if back == 0 else held[back - 1, pair, tokens]
            keys, values = block[:HEAD_SIZE].T, block[HEAD_SIZE:]
            bias = seen(back, me, start_ref[0:1, tokens])
            p = jnp.exp(dot(keys, abreast(q_ref[wide, tokens])) + bias)
            total = jnp.sum(p, axis=0, keepdims=True)
            out = dot(values, p.astype(BF16))
            for g in range(GROUP):
                own = slice(g * length, (g + 1) * length)
                line = slice(g, g + 1)
                part = pl.ds(wide.start + g * HEAD_SIZE, HEAD_SIZE)
                if back == 0:
                    l_acc[head, line, tokens] = total[:, own]
                    o_acc[part, tokens] = out[:, own]
                else:
                    l_acc[head, line, tokens] += total[:, own]
                    o_acc[part, tokens] += out[:, own]

    pl.when(me < n - 1)(lambda: climbs(1))
    for stages in each:
        stages[0](0)
        stages[0](1)
    level(0)
    for back in range(1, n):

        def step(back=back):
            for head in heads:
                climb(back, head).wait_recv()
                if back < n - 1:
                    pl.when(me < n - 1)(lambda head=head: climb(back + 1, head).start())
            level(back)

        pl.when(me >= back)(step)
        if back <= 2:
            for stages in each:
                stages[back]()

    @pl.loop(0, rows * KEY_VALUE_HEADS, unroll=KEY_VALUE_HEADS)
    def _(i):
        tokens, wide, pair, head = spans(i, length)
        for g in range(GROUP):
            line = slice(g, g + 1)
            part = pl.ds(wide.start + g * HEAD_SIZE, HEAD_SIZE)
            out = o_acc[part, tokens] / l_acc[head, line, tokens]
            o_acc[part, tokens] = out
            o_ref[part, tokens] = out.astype(BF16)
            lse_ref[head, line, tokens] = jnp.log(l_acc[head, line, tokens])

    if planes:
        tall = full_ref.shape[0] // 32
        filled[...] = jnp.zeros_like(filled)

        @pl.loop(0, 32, unroll=8)
        def _(i):
            src = pl.ds(pl.multiple_of(i * out_rows, 8), out_rows)
            dst = pl.ds(pl.multiple_of(i * tall, 8), out_rows)
            filled[dst, :] = o_acc[src, :]

        full_ref[...] = filled[...].astype(BF16)

    for back in range(1, n):
        for head in heads:
            pl.when((me >= back - 1) & (me < n - 1))(
                lambda back=back, head=head: climb(back, head).wait_send()
            )
    for stages in each:
        stages[3]()


def attend(start, queries, pairs, rows, n, more, out_rows):
    vmem, dma = pl.BlockSpec(memory_space=pltpu.VMEM), pltpu.SemaphoreType.DMA
    anywhere = pl.BlockSpec(memory_space=pl.ANY)
    count = queries.shape[1]
    lines = (KEY_VALUE_HEADS, 8, count)
    out_shape = [
        jax.ShapeDtypeStruct(queries.shape, BF16),
        jax.ShapeDtypeStruct(lines, F32),
        jax.ShapeDtypeStruct((n - 1, *pairs.shape), BF16),
    ]
    scratch, full = [], []
    if more:
        full = [(QW // out_rows * more[1].shape[1], count)]
        scratch.append(pltpu.VMEM(full[0], F32))
    scratch += [
        pltpu.VMEM(queries.shape, F32),
        pltpu.VMEM(lines, F32),
        dma((n - 1, KEY_VALUE_HEADS)),
        dma((n - 1, KEY_VALUE_HEADS)),
    ]
    for extra in more:
        out_shape.append(jax.ShapeDtypeStruct((8, *extra.shape), BF16))
        scratch += [dma, dma((8, 2)), dma((8, 2))]
    out_shape += [jax.ShapeDtypeStruct(shape, BF16) for shape in full]
    return pl.pallas_call(
        functools.partial(attend_kernel, n, rows, len(more), out_rows),
        in_specs=[vmem] * 3 + [anywhere] * len(more),
        out_specs=[vmem] * 3 + [anywhere] * len(more) + [vmem] * len(full),
        out_shape=out_shape,
        scratch_shapes=scratch,
        compiler_params=pltpu.CompilerParams(
            collective_id=2, has_side_effects=True, vmem_limit_bytes=48 * 2**20
        ),
        name="attend",
    )(start, queries, pairs, *more)


def plus(ref, *others):
    total = ref[...].astype(F32)
    for other in others:
        total += other[...].astype(F32)
    ref[...] = total.astype(BF16)


def attend_back_kernel(n, rows, summed, *refs):
    start_ref, q_ref, do_ref, o_ref, lse_ref, kv_ref, held, *refs = refs
    if summed:
        h_ref, w_ref, m_ref, *refs = refs
    dq_ref, dkv_ref, *refs = refs
    if summed:
        mixed_ref, *refs = refs
    inner, part, rcv, sent, got, *refs = refs
    d, me = lax.axis_index("dp"), lax.axis_index("seq")
    length = q_ref.shape[1] // rows
    if summed:
        place = places()
        d, me, d_c, d_x, d_y, _ = place
        w_v, h_v, m_v, w_sem, h_sem, m_sem, *refs = refs
        kept, leaving = refs[:2]
        m_load = pltpu.make_async_copy(m_ref, m_v, m_sem)
        load, product = block_products(h_ref, h_v, h_sem, lambda h, span: dot(h, w_v[:, span]))
        load(0).start()
        w_load = pltpu.make_async_copy(w_ref, w_v, w_sem)
        w_load.start()
        greet([(d_c, me), (d_x, me), (d_y, me)], (d, me))
        crossing, far, near, pass_on, end = plane_sums(*refs, place)

        def pair(turn, i):
            slot = turn // 2 % 2
            if turn >= 4:
                crossing(3 if slot == 0 else 1, slot).wait_send()
            product(turn, leaving.at[slot])
            crossing(i, slot).start()
            product(turn + 1, kept.at[i])

        def stage(i):
            if i == 0:
                w_load.wait()
                m_load.start()
                pair(0, 3)
                far()
            elif i == 1:
                pair(2, 1)
                near(1)
                pair(4, 2)
                near(2)
                pair(6, 0)
                near(0)
            elif i == 2:
                pass_on()
            else:
                end()
                m_load.wait()
                mixed_ref[...] = (kept[0].astype(F32) + m_v[...]).astype(BF16)
                crossing(2, 0).wait_send()
                crossing(0, 1).wait_send()
    else:
        greet([], (d, me))

        def stage(i):
            pass

    def descend(back):
        return remote(
            part.at[back - 1], rcv.at[back - 1], sent.at[back - 1], got.at[back - 1], (d, me - 1)
        )

    def level(back):
        @pl.loop(0, rows * KEY_VALUE_HEADS, unroll=2)
        def _(i):
            tokens, wide, pair, head = spans(i, length)
            block = kv_ref[pair, tokens] if back == 0 else held[back - 1, pair, tokens]
            keys_t = block[:HEAD_SIZE]
            keys, values = keys_t.T, block[HEAD_SIZE:].T
            q, do = abreast(q_ref[wide, tokens]), abreast(do_ref[wide, tokens])
            bias = seen(back, me, start_ref[0:1, tokens])
            p = jnp.exp(dot(keys, q) + (bias - across(lse_ref[head, :, tokens])))
            ds = (p * (dot(values, do) - across(inner[head, :, tokens]))).astype(BF16)
            dv = back_product(p.astype(BF16), do)
            dk = back_product(ds, q)
            dq = dot(keys_t, ds)
            if back == 0:
                dkv_ref[pair, tokens] = jnp.concatenate([dk.T, dv.T], axis=0)
            else:
                part[back - 1, pair, tokens] = jnp.concatenate([dk.T, dv.T], axis=0).astype(BF16)
            for g in range(GROUP):
                own = slice(g * length, (g + 1) * length)
                line = pl.ds(wide.start + g * HEAD_SIZE, HEAD_SIZE)
                dq_ref[line, tokens] += dq[:, own]

    def finish(back):
        def more():
            descend(back + 1).wait_recv()
            if back == 0:
                dkv_ref[...] += rcv[0].astype(F32)
            else:
                plus(part.at[back - 1], rcv.at[back])

        if back < n - 1:
            pl.when(me < n - 1)(more)
        if back > 0:
            descend(back).start()

    stage(0)
    dq_ref[...] = jnp.zeros_like(dq_ref)

    @pl.loop(0, rows * KEY_VALUE_HEADS, unroll=KEY_VALUE_HEADS)
    def _(i):
        tokens, wide, pair, head = spans(i, length)
        for g in range(GROUP):
            line = slice(g, g + 1)
            own = pl.ds(wide.start + g * HEAD_SIZE, HEAD_SIZE)
            product = do_ref[own, tokens].astype(F32) * o_ref[own, tokens].astype(F32)
            inner[head, line, tokens] = jnp.sum(product, axis=0, keepdims=True)

    for back in range(n - 1, -1, -1):

        def run(back=back):
            level(back)
            pl.when(me == n - 1)(lambda: finish(back))

        if back:
            pl.when(me >= back)(run)
        else:
            level(0)
            pl.when(me == n - 1)(lambda: finish(0))
        if back + 1 < n - 1:
            pl.when((me >= back + 1) & (me < n - 1))(lambda back=back: finish(back + 1))
        if n - 1 - back in (1, 2):
            stage(n - 1 - back)
    pl.when(me < n - 1)(lambda: finish(0))
    stage(3)
    for back in range(1, n):
        pl.when(me >= back)(lambda back=back: descend(back).wait_send())


def attend_back(start, queries, dheads, heads, lse, pairs, held, rows, n, more):
    vmem, dma = pl.BlockSpec(memory_space=pltpu.VMEM), pltpu.SemaphoreType.DMA
    anywhere = pl.BlockSpec(memory_space=pl.ANY)
    count = queries.shape[1]
    out_shape = [
        jax.ShapeDtypeStruct(queries.shape, F32),
        jax.ShapeDtypeStruct(pairs.shape, F32),
    ]
    scratch = [
        pltpu.VMEM((KEY_VALUE_HEADS, 8, count), F32),
        pltpu.VMEM((n - 1, *pairs.shape), BF16),
        pltpu.VMEM((n - 1, *pairs.shape), BF16),
        dma((n - 1,)),
        dma((n - 1,)),
    ]
    if more:
        (tokens, deep), (_, width) = more[0].shape, more[1].shape
        block = tokens // 8
        out_shape.append(jax.ShapeDtypeStruct((block, width), BF16))
        scratch += [
            pltpu.VMEM((deep, width), BF16),
            pltpu.VMEM((2, block, deep), BF16),
            pltpu.VMEM((block, width), F32),
            dma,
            dma((2,)),
            dma,
            *sums_scratch(block, width),
        ]
    return pl.pallas_call(
        functools.partial(attend_back_kernel, n, rows, bool(more)),
        in_specs=[vmem] * 7 + [anywhere] * len(more),
        out_specs=[vmem] * len(out_shape),
        out_shape=out_shape,
        scratch_shapes=scratch,
        compiler_params=pltpu.CompilerParams(
            collective_id=3, has_side_effects=True, vmem_limit_bytes=62 * 2**20
        ),
        name="attend_back",
    )(start, queries, dheads, heads, lse, pairs, held, *more)


def weights_kernel(n, *refs):
    x_refs, (w_ref, *out_refs), refs = refs[:n], refs[n : 2 * n + 1], refs[2 * n + 1 :]
    spread_ref, own_sem, recv, send_z, send_x, send_y, send_d, send_c, own_w, sent_w, got_w = refs
    d, s, d_c, d_x, d_y, line = places()
    d_d = d_x + 4 - 8 * line
    flip = d_c - d
    plane = (d, d_c, d_x, d_x + flip, d_y, d_y + flip, d_d, d_d + flip)
    greet([(other, s) for other in plane[1:]], (d, s))
    part = spread_ref.shape[2] // 2

    def columns(k, half):
        begin = half * 8 * part + plane[k] * part
        src = w_ref.at[:, pl.ds(pl.multiple_of(begin, 128), part)]
        dst = spread_ref.at[d, :, pl.ds(half * part, part)]
        if k == 0:
            return pltpu.make_async_copy(src, dst, own_w.at[half])
        return remote(src, dst, sent_w.at[k, half], got_w.at[k, half], (plane[k], s))

    def copies(slot, sent, got, peer, own=False, arrays=(0,)):
        return [
            remote(
                x_refs[i] if own else out_refs[i].at[slot if i == 0 else slot % 4],
                out_refs[i].at[slot if i == 0 else slot % 4],
                sent(i),
                got(i),
                peer,
            )
            for i in arrays
        ]

    def start(group):
        for one in group:
            one.start()

    def sent(group):
        for one in group:
            one.wait_send()

    def each(visit, between=lambda: None):
        visit(s, 0)
        between()
        for far in (1, 2, 3):
            pl.when(s >= far)(lambda far=far: visit(s - far, 1))
            pl.when(s + far <= 3)(lambda far=far: visit(s + far, -1))

    def got(k, b):
        return lambda i: recv.at[i, k, b]

    def arrived(k, b, arrays=(0,)):
        group = copies(d * 4 + b, lambda i: send_x.at[i, b], got(k, b), (d_x, s), arrays=arrays)
        for one in group:
            one.wait_recv()

    own = [
        pltpu.make_async_copy(x_refs[i], out_refs[i].at[d * 4 + s if i == 0 else s], own_sem.at[i])
        for i in range(n)
    ]
    start(own)

    def up(b, own=False, arrays=(0,)):
        return copies(d * 4 + b, lambda i: send_z.at[i, 0, b], got(0, b), (d, s + 1), own, arrays)

    def down(b, own=False, arrays=(0,)):
        return copies(d * 4 + b, lambda i: send_z.at[i, 1, b], got(0, b), (d, s - 1), own, arrays)

    def spread(b, own=False):
        return (
            copies(d * 4 + b, lambda i: send_x.at[i, b], got(2, b), (d_x, s), own)
            + copies(d * 4 + b, lambda i: send_y.at[i, b], got(4, b), (d_y, s), own)
            + copies(d * 4 + b, lambda i: send_c.at[i, 0, b], got(1, b), (d_c, s), own)
        )

    others = tuple(range(1, n))

    def line_block(b, direction, arrays):
        own = direction == 0
        if direction:
            arrived(0, b, arrays)
        if direction >= 0:
            pl.when(s < 3)(lambda: start(up(b, own, arrays)))
        if direction <= 0:
            pl.when(s > 0)(lambda: start(down(b, own, arrays)))

    def column_block(b, direction):
        line_block(b, direction, (0,))
        start(spread(b, direction == 0))

    def other_block(b, direction):
        if direction:
            line_block(b, direction, others)

    def start_columns():
        for k in range(8):
            for half in (0, 1):
                columns(k, half).start()

    each(column_block, start_columns)
    line_block(s, 0, others)

    def over_y(b):
        return copies(d_x * 4 + b, lambda i: send_d.at[i, b], got(6, b), (d_y, s))

    def over_x(b):
        return copies(d_y * 4 + b, lambda i: send_d.at[i, b], got(6, b), (d_x, s))

    def to_core(index, holder, b):
        return copies(
            holder * 4 + b, lambda i: send_c.at[i, index, b], got(2 * index + 1, b), (d_c, s)
        )

    def side_blocks(b, direction):
        arrived(2, b)
        pl.when(b % 2 == 0)(lambda: start(over_y(b)))
        start(to_core(1, d_x, b))
        arrived(4, b)
        pl.when(b % 2 == 1)(lambda: start(over_x(b)))
        start(to_core(2, d_y, b))

    each(side_blocks)

    def far_block(b, direction):
        arrived(6, b)
        start(to_core(3, d_d, b))

    each(other_block)
    each(far_block)

    def finish(b, direction):
        for k in (1, 3, 5, 7):
            arrived(k, b)
        if direction >= 0:
            pl.when(s < 3)(lambda: sent(up(b, arrays=range(n))))
        if direction <= 0:
            pl.when(s > 0)(lambda: sent(down(b, arrays=range(n))))
        sent(spread(b))
        sent(over_y(b))
        sent(to_core(1, d_x, b))
        sent(to_core(2, d_y, b))
        sent(to_core(3, d_d, b))

    each(finish)
    for one in own:
        one.wait()
    for k in range(8):
        for half in (0, 1):
            if k:
                columns(k, half).wait_recv()
                columns(k, half).wait_send()
            else:
                columns(k, half).wait()


def gather_weights(first, others, wide, n_dp, n_seq):
    rows, part = wide.shape[0], wide.shape[1] // (2 * n_dp)
    if (n_dp, n_seq) != (8, 4):
        spread = lax.all_to_all(wide.reshape(rows, 2, n_dp, part), "dp", 2, 0, tiled=False)
        spread = spread.reshape(n_dp, rows, 2 * part)
        return [lax.all_gather(x, BOTH, axis=0, tiled=False) for x in (first, *others)] + [spread]
    arrays = [first, *others]
    n = len(arrays)
    dma = pltpu.SemaphoreType.DMA
    return pl.pallas_call(
        functools.partial(weights_kernel, n),
        out_shape=[
            jax.ShapeDtypeStruct((n_seq if i else n_dp * n_seq, *x.shape), x.dtype)
            for i, x in enumerate(arrays)
        ]
        + [jax.ShapeDtypeStruct((n_dp, rows, 2 * part), wide.dtype)],
        in_specs=[pl.BlockSpec(memory_space=pl.ANY)] * (n + 1),
        out_specs=[pl.BlockSpec(memory_space=pl.ANY)] * (n + 1),
        scratch_shapes=[
            dma((n,)),
            dma((n, 8, 4)),
            dma((n, 2, 4)),
            dma((n, 4)),
            dma((n, 4)),
            dma((n, 4)),
            dma((n, 4, 4)),
            dma((2,)),
            dma((8, 2)),
            dma((8, 2)),
        ],
        compiler_params=pltpu.CompilerParams(collective_id=1, has_side_effects=True),
        name="gather_weights",
    )(*arrays, wide)


def weight_sums(product, refs, place):
    kept, leaving, rcv_c, rcv_d, rcv_x, rcv_y, rcv_z = refs[:7]
    sent_c, got_c, sent_p, got_p, sent_z, got_z = refs[7:]
    d, s, d_c, d_x, d_y, line = place
    holders = (d, d_x, d_y, d_x + d_y - d)
    flip = d_c - d
    low, high = pl.ds(0, 2), pl.ds(2, 2)

    def crossing(i, slot):
        return remote(leaving.at[slot], rcv_c.at[i], sent_c.at[i], got_c.at[i], (d_c, s))

    def pair(i, slot, before=None):
        if before is not None:
            crossing(before, slot).wait_send()
        product(holders[i] + flip, leaving.at[slot])
        crossing(i, slot).start()
        product(holders[i], kept.at[i])

    def merge(i):
        crossing(i, 0).wait_recv()
        plus(kept.at[i], rcv_c.at[i])

    def push(i):
        src, dst, peer = (
            (kept.at[3, low], rcv_d.at[low], d_x),
            (kept.at[3, high], rcv_d.at[high], d_y),
            (kept.at[1, low], rcv_x.at[low], d_x),
            (kept.at[2, high], rcv_y.at[high], d_y),
            (kept.at[2, low], rcv_y.at[low], d_y),
            (kept.at[1, high], rcv_x.at[high], d_x),
        )[i]
        return remote(src, dst, sent_p.at[i], got_p.at[i], (peer, s))

    def straight(b):
        return remote(kept.at[0, b], rcv_z.at[s], sent_z.at[b], got_z.at[s], (d, b))

    def from_line(b):
        return remote(kept.at[0, b], rcv_z.at[b], sent_z.at[b], got_z.at[b], (d, b))

    def far():
        pair(3, 0)
        pair(1, 1)
        merge(3)
        push(0).start()
        push(1).start()

    def near():
        pair(2, 0, 3)
        pair(0, 1, 1)
        merge(1)
        push(2).start()
        merge(2)
        push(3).start()
        merge(0)

    def pass_on():
        push(0).wait_recv()
        plus(kept.at[2, low], rcv_d.at[low])
        push(4).start()
        push(1).wait_recv()
        plus(kept.at[1, high], rcv_d.at[high])
        push(5).start()

    def along():
        for i in (2, 3, 4, 5):
            push(i).wait_recv()
        plus(kept.at[0], rcv_x, rcv_y)
        for b in range(4):
            pl.when(s != b)(lambda b=b: straight(b).start())

    def end(out_ref):
        out_ref[...] = kept[0, s].astype(F32)
        for b in range(4):

            @pl.when(s != b)
            def _(b=b):
                from_line(b).wait_recv()
                out_ref[...] += rcv_z[b].astype(F32)

        for b in range(4):
            pl.when(s != b)(lambda b=b: straight(b).wait_send())
        crossing(2, 0).wait_send()
        crossing(0, 1).wait_send()
        for i in range(6):
            push(i).wait_send()

    return far, near, pass_on, along, end


def weight_sums_scratch(rows, columns):
    dma = pltpu.SemaphoreType.DMA
    buffer = lambda *lead: pltpu.VMEM((*lead, rows, columns), BF16)
    return [
        buffer(4, 4),
        buffer(2, 4),
        buffer(4, 4),
        buffer(4),
        buffer(4),
        buffer(4),
        buffer(4),
        dma((4,)),
        dma((4,)),
        dma((6,)),
        dma((6,)),
        dma((4,)),
        dma((4,)),
    ]


def normed_back(dy, x, gain):
    inverse = lax.rsqrt(jnp.mean(x * x, axis=1, keepdims=True) + epsilon)
    gy = dy * gain
    x = x * inverse
    return inverse * (gy - x * jnp.mean(gy * x, axis=1, keepdims=True))


def middle_back_kernel(out_rows, dy_ref, mid_ref, g_ref, gain_ref, w_ref, dm_ref, low_ref, dh_ref, acc):
    dm = g_ref[...].astype(F32)
    dm += normed_back(dy_ref[...].astype(F32), mid_ref[...], gain_ref[...])
    dm_ref[...] = dm
    low = dm.astype(BF16)
    low_ref[...] = low
    tall = w_ref.shape[0] // 32
    heads = back_product(w_ref[...], low)
    for i in range(32):
        acc[i * out_rows : (i + 1) * out_rows, :] = heads[i * tall : i * tall + out_rows]
    dh_ref[...] = acc[...].astype(BF16)


def middle_back(dy, middle, g, gain, w, out_rows):
    count, width = middle.shape
    block = 256
    rows = pl.BlockSpec((block, width), lambda i: (i, 0))
    whole = lambda x: pl.BlockSpec(x.shape, lambda i: (0, 0))
    return pl.pallas_call(
        functools.partial(middle_back_kernel, out_rows),
        grid=(count // block,),
        in_specs=[rows] * 3 + [whole(gain), whole(w)],
        out_specs=[rows, rows, pl.BlockSpec((32 * out_rows, block), lambda i: (0, i))],
        out_shape=[
            jax.ShapeDtypeStruct((count, width), F32),
            jax.ShapeDtypeStruct((count, width), BF16),
            jax.ShapeDtypeStruct((32 * out_rows, count), BF16),
        ],
        scratch_shapes=[pltpu.VMEM((32 * out_rows, block), F32)],
        compiler_params=pltpu.CompilerParams(vmem_limit_bytes=56 * 2**20),
        name="middle_back",
    )(dy, middle, g, gain, w)


def sum_weights_kernel(n_ref, p_ref, h_ref, a_ref, few_ref, own_ref, *refs):
    w_ref, x_ref, dm_ref, back_0_ref, back_1_ref, gain_ref, wide_ref, *refs = refs
    qkv_out, small_out, out_out, dx_ref, wide_out, *refs = refs
    w_v, qkv_sum, out_sum, back_v, w_sem, own_sem, sent_w, got_w, *refs = refs
    w_load = pltpu.make_async_copy(w_ref, w_v, w_sem)
    w_load.start()
    place = places()
    d, s, d_c, d_x, d_y, line = place
    flip, d_d = d_c - d, d_x + d_y - d
    plane = (d, d_c, d_x, d_x + flip, d_y, d_y + flip, d_d, d_d + flip)
    greet([(other, s) for other in plane[1:]] + [(d, (s + i) % 4) for i in (1, 2, 3)])

    def exchange(k, i):
        src, dst = (back_0_ref, back_1_ref)[i].at[plane[k]], back_v.at[i, d]
        if k == 0:
            return pltpu.make_async_copy(src, dst, own_sem.at[i])
        return remote(src, dst, sent_w.at[k, i], got_w.at[k, i], (plane[k], s))

    width, chunk = p_ref.shape[0], 512

    def chunks(make, dst):
        @pl.loop(0, width // chunk, unroll=2)
        def _(c):
            span = pl.ds(pl.multiple_of(c * chunk, chunk), chunk)
            dst[:, :, span] = make(span).astype(BF16).reshape(*dst.shape[:2], chunk)

    def qkv_product(k, dst):
        tall = dst.shape[0] * dst.shape[1]
        rows = n_ref[:, pl.ds(pl.multiple_of(k * tall, tall), tall)].T
        chunks(lambda span: back_product(rows, p_ref[span, :]), dst)
        for b in range(4):
            dst[b, :16, -128:] = few_ref[k * 4 + b].astype(BF16)

    def out_product(k, dst):
        tall = dst.shape[0] * dst.shape[1]
        rows = h_ref[pl.ds(pl.multiple_of(k * tall, 16), tall), :]
        chunks(lambda span: dot(rows, a_ref[:, span]), dst)

    far, near, pass_on, along, end = weight_sums(qkv_product, refs[:13], place)
    far_2, near_2, pass_on_2, along_2, end_2 = weight_sums(out_product, refs[13:], place)
    block = 128

    def token_grads(first, count):
        def body(x_tile, dm_tile, dx_tile):
            i = pl.program_id(0) + first
            span = pl.ds(pl.multiple_of(i * block, block), block)
            dy = back_product(p_ref[:, span].T, w_v[...])
            dx_tile[...] = dm_tile[...] + normed_back(dy, x_tile[...].astype(F32), gain_ref[...])

        spec = lambda: pl.BlockSpec((block, x_ref.shape[1]), lambda i: (i + first, 0))
        pltpu.emit_pipeline(body, grid=(count,), in_specs=[spec(), spec()], out_specs=[spec()])(
            x_ref, dm_ref, dx_ref
        )

    blocks = x_ref.shape[0] // block
    far()
    near()
    w_load.wait()
    token_grads(0, 1)
    pass_on()
    far_2()
    near_2()
    token_grads(1, 2)
    along()
    pass_on_2()
    for k in range(8):
        exchange(k, 0).start()
        exchange(k, 1).start()
    token_grads(3, blocks - 3)
    along_2()
    end(qkv_sum)
    for i in (0, 1):
        exchange(0, i).wait()
        for k in range(1, 8):
            exchange(k, i).wait_recv()
            exchange(k, i).wait_send()
    part = back_v.shape[3]
    total = jnp.zeros((wide_out.shape[0], 1), F32)
    for j in range(16):
        half_j, holder = j // 8, j % 8
        span = slice(j * part, (j + 1) * part)
        grad = back_v[half_j, holder].astype(F32)
        wide_out[:, span] = grad
        total += jnp.sum(grad * wide_ref[:, span].astype(F32), axis=1, keepdims=True)
    tall = wide_out.shape[0]

    def as_row(column):
        return jnp.broadcast_to(column, (column.shape[0], 128)).T[0:1]

    small_out[...] = jnp.zeros_like(small_out)
    small_out[1:2, :tall] = as_row(total)
    inner = QW + 2 * KW
    total = jnp.sum(qkv_sum[:, :inner] * own_ref[:, :inner].astype(F32), axis=1, keepdims=True)
    small_out[0:1, :tall] = as_row(total)
    small_out[2:3, :16] = as_row(qkv_sum[:16, inner : inner + 1])
    qkv_out[...] = qkv_sum[:, :inner]
    end_2(out_sum)
    out_out[...] = out_sum[: out_out.shape[0]]


def sum_weights(normed, dprojected, heads, dattend, few, own, w, x, dmiddle, gain, back, back_1, wide, out_rows):
    dma, anywhere = pltpu.SemaphoreType.DMA, pl.BlockSpec(memory_space=pl.ANY)
    vmem = pl.BlockSpec(memory_space=pltpu.VMEM)
    rows, width = own.shape
    tall = heads.shape[0] // 32
    scratch = [
        pltpu.VMEM(w.shape, BF16),
        pltpu.VMEM(own.shape, F32),
        pltpu.VMEM((tall, width), F32),
        pltpu.VMEM((2, *back.shape), BF16),
        dma,
        dma((2,)),
        dma((8, 2)),
        dma((8, 2)),
    ]
    scratch += weight_sums_scratch(rows, width) + weight_sums_scratch(tall, width)
    return pl.pallas_call(
        sum_weights_kernel,
        out_shape=[
            jax.ShapeDtypeStruct((rows, QW + 2 * KW), F32),
            jax.ShapeDtypeStruct((8, 128), F32),
            jax.ShapeDtypeStruct((out_rows, width), F32),
            jax.ShapeDtypeStruct(dmiddle.shape, F32),
            jax.ShapeDtypeStruct(wide.shape, F32),
        ],
        in_specs=[vmem] * 6 + [anywhere] * 5 + [vmem] * 2,
        out_specs=[vmem] * 3 + [anywhere, vmem],
        scratch_shapes=scratch,
        compiler_params=pltpu.CompilerParams(
            collective_id=6, has_side_effects=True, vmem_limit_bytes=63 * 2**20
        ),
        name="sum_weights",
    )(normed, dprojected, heads, dattend, few, own, w, x, dmiddle, back, back_1, gain, wide)


def plane_kernel(rows, heads_ref, w_ref, x_ref, gain_ref, g_ref, down_ref, *refs):
    out_ref, dh_ref, mid_ref, w_v, x_v, down_v, mid_v, n_v, load, mid_sem, *refs = refs
    place = places()
    d, s, d_c, d_x, d_y, line = place
    w_load = pltpu.make_async_copy(w_ref, w_v, load.at[0])
    x_load = pltpu.make_async_copy(x_ref, x_v, load.at[1])
    down_load = pltpu.make_async_copy(down_ref, down_v, load.at[2])
    w_load.start()
    x_load.start()
    down_load.start()
    greet([(d_c, s), (d_x, s), (d_y, s)])
    begin, first, second, end = plane_stages(n_v, out_ref, *refs, place)
    w_load.wait()
    x_load.wait()
    width, chunk = mid_v.shape[1], 512

    def stored(row):
        tokens = pl.ds(row * (mid_v.shape[0] // rows), mid_v.shape[0] // rows)
        return pltpu.make_async_copy(mid_v.at[tokens], mid_ref.at[tokens], mid_sem.at[row])

    for row in range(rows):
        tokens = slice(row * (mid_v.shape[0] // rows), (row + 1) * (mid_v.shape[0] // rows))
        heads = heads_ref[:, tokens].T

        @pl.loop(0, width // chunk)
        def _(c):
            span = pl.ds(pl.multiple_of(c * chunk, chunk), chunk)
            weight = w_v[:, :, :, span].reshape(heads.shape[1], chunk)
            mid_v[tokens, span] = x_v[tokens, span].astype(F32) + dot(heads, weight)

        stored(row).start()
        mid = mid_v[tokens, :]
        inverse = lax.rsqrt(jnp.mean(mid * mid, axis=1, keepdims=True) + epsilon)
        n_v[tokens, :] = (mid * inverse * gain_ref[...]).astype(BF16)
        begin(row)
    down_load.wait()

    def body(g_tile, dh_tile):
        dh_tile[...] = back_product(g_tile[...], down_v[...]).astype(BF16)

    pltpu.emit_pipeline(
        body,
        grid=(g_ref.shape[0] // 512,),
        in_specs=[pl.BlockSpec((512, down_v.shape[1]), lambda i: (i, 0))],
        out_specs=[pl.BlockSpec((512, down_v.shape[0]), lambda i: (i, 0))],
    )(g_ref, dh_ref)
    first()
    second()
    end()
    for row in range(rows):
        stored(row).wait()


def plane_gather(heads, w, x, gain, g, down):
    dma, anywhere = pltpu.SemaphoreType.DMA, pl.BlockSpec(memory_space=pl.ANY)
    vmem = pl.BlockSpec(memory_space=pltpu.VMEM)
    everyone, dhidden, middle = pl.pallas_call(
        functools.partial(plane_kernel, 2),
        out_shape=[
            jax.ShapeDtypeStruct((8, *x.shape), BF16),
            jax.ShapeDtypeStruct((g.shape[0], down.shape[0]), BF16),
            jax.ShapeDtypeStruct(x.shape, F32),
        ],
        in_specs=[vmem, anywhere, anywhere, vmem, anywhere, anywhere],
        out_specs=[anywhere] * 3,
        scratch_shapes=[
            pltpu.VMEM(w.shape, BF16),
            pltpu.VMEM(x.shape, BF16),
            pltpu.VMEM(down.shape, BF16),
            pltpu.VMEM(x.shape, F32),
            pltpu.VMEM(x.shape, BF16),
            dma((3,)),
            dma((2,)),
            dma,
            dma((8, 2)),
            dma((8, 2)),
        ],
        compiler_params=pltpu.CompilerParams(
            collective_id=4, has_side_effects=True, vmem_limit_bytes=48 * 2**20
        ),
        name="plane_gather",
    )(heads, w, x, gain, g, down)
    return everyone.reshape(8 * x.shape[0], x.shape[1]), dhidden, middle


def transposed_kernel(x_ref, g_ref, out_ref):
    n_seq, n_dp, rows, _ = out_ref.shape
    total = outer_sum(x_ref[...], g_ref[...])
    for i in range(n_dp * n_seq):
        out_ref[i % n_seq, i // n_seq] = total[i * rows : (i + 1) * rows].astype(BF16)


def transposed_product(x, g, n_dp, n_seq, parts):
    (tokens, width), wide = x.shape, g.shape[1] // parts
    rows, tall = width // (n_dp * n_seq), 512
    return pl.pallas_call(
        transposed_kernel,
        grid=(width // tall,),
        in_specs=[
            pl.BlockSpec((tokens, tall), lambda i: (0, i)),
            pl.BlockSpec((tokens, wide), lambda i: (0, 0)),
        ],
        out_specs=pl.BlockSpec(
            (n_seq, tall // (n_seq * rows), rows, wide), lambda i: (0, i, 0, 0)
        ),
        out_shape=jax.ShapeDtypeStruct((n_seq, n_dp, rows, wide), BF16),
        compiler_params=pltpu.CompilerParams(vmem_limit_bytes=60 * 2**20),
        cost_estimate=pl.CostEstimate(
            flops=2 * tokens * width * wide,
            bytes_accessed=2 * (tokens * width + tokens * wide + width * wide),
            transcendentals=0,
        ),
        name="transposed_product",
    )(x, g)


def plane_sums(kept, leaving, rcv_c, rcv_d, rcv_x, rcv_y, sent_c, got_c, sent_p, got_p, place):
    d, s, d_c, d_x, d_y, line = place
    rows = kept.shape[1]
    low, high = pl.ds(0, rows // 2), pl.ds(rows // 2, rows // 2)

    def crossing(i, slot):
        return remote(leaving.at[slot], rcv_c.at[i], sent_c.at[i], got_c.at[i], (d_c, s))

    def merge(i):
        crossing(i, 0).wait_recv()
        plus(kept.at[i], rcv_c.at[i])

    def push(i):
        src, dst, peer = (
            (kept.at[3, low], rcv_d.at[low], d_x),
            (kept.at[3, high], rcv_d.at[high], d_y),
            (kept.at[1, low], rcv_x.at[low], d_x),
            (kept.at[2, high], rcv_y.at[high], d_y),
            (kept.at[2, low], rcv_y.at[low], d_y),
            (kept.at[1, high], rcv_x.at[high], d_x),
        )[i]
        return remote(src, dst, sent_p.at[i], got_p.at[i], (peer, s))

    def far():
        merge(3)
        push(0).start()
        push(1).start()

    def near(i):
        merge(i)
        if i:
            push(i + 1).start()

    def pass_on():
        push(0).wait_recv()
        plus(kept.at[2, low], rcv_d.at[low])
        push(4).start()
        push(1).wait_recv()
        plus(kept.at[1, high], rcv_d.at[high])
        push(5).start()

    def end():
        for i in (2, 3, 4, 5):
            push(i).wait_recv()
        plus(kept.at[0], rcv_x, rcv_y)
        for i in range(6):
            push(i).wait_send()

    return crossing, far, near, pass_on, end


def sums_scratch(rows, width):
    dma = pltpu.SemaphoreType.DMA
    buffer = lambda *lead: pltpu.VMEM((*lead, rows, width), BF16)
    return [
        buffer(4),
        buffer(2),
        buffer(4),
        buffer(),
        buffer(),
        buffer(),
        dma((4,)),
        dma((4,)),
        dma((6,)),
        dma((6,)),
    ]


ORDER = (7, 6, 3, 2, 5, 4, 1, 0)


def block_products(g_ref, g_v, g_sem, multiply):
    rows = g_v.shape[1]

    def load(turn):
        block = pl.ds(ORDER[turn] * rows, rows)
        return pltpu.make_async_copy(g_ref.at[block], g_v.at[turn % 2], g_sem.at[turn % 2])

    def product(turn, dst):
        if turn + 1 < 8:
            load(turn + 1).start()
        load(turn).wait()
        chunk = 512

        @pl.loop(0, dst.shape[1] // chunk, unroll=2)
        def _(c):
            span = pl.ds(pl.multiple_of(c * chunk, chunk), chunk)
            dst[:, span] = multiply(g_v[turn % 2], span).astype(BF16)

    return load, product


def plane_sum_kernel(
    g_ref, w_ref, h_ref, t_ref, x_ref, out_ref, grad_ref, wide_ref, w_v, g_v, h_v, *refs
):
    w_sem, g_sem, h_sem, out_sem, *refs = refs
    place = places()
    d, s, d_c, d_x, d_y, line = place
    kept, leaving = refs[:2]
    w_wait = load_rows(w_ref, w_v, w_sem, 8, 4)
    load, product = block_products(
        g_ref, g_v, g_sem, lambda g, span: back_product(g, w_v[span, :])
    )
    load(0).start()
    h_load = pltpu.make_async_copy(h_ref, h_v, h_sem)
    h_load.start()
    greet([(d_c, s), (d_x, s), (d_y, s)])
    crossing, far, near, pass_on, end = plane_sums(*refs, place)
    w_wait()

    def pair(turn, i):
        slot = turn // 2 % 2
        if turn >= 4:
            crossing(3 if slot == 0 else 1, slot).wait_send()
        product(turn, leaving.at[slot])
        crossing(i, slot).start()
        product(turn + 1, kept.at[i])

    pair(0, 3)
    far()
    pair(2, 1)
    pair(4, 2)
    near(1)
    near(2)
    pair(6, 0)
    near(0)
    h_load.wait()

    def grad_body(t_tile, grad_tile):
        grad_tile[...] = outer_sum(h_v[...], t_tile[...]).astype(BF16)

    tokens, deep = h_v.shape
    wide = 256

    def grad_tiles(first, count):
        pltpu.emit_pipeline(
            grad_body,
            grid=(count,),
            in_specs=[pl.BlockSpec((tokens, wide), lambda i: (0, first + i))],
            out_specs=[pl.BlockSpec((deep, wide), lambda i: (0, first + i))],
        )(t_ref, grad_ref)

    def wide_body(x_tile, wide_tile):
        total = outer_sum(x_tile[...], h_v[...])
        high = wide_tile.shape[2]
        for j in range(4):
            wide_tile[j, 0] = total[j * high : (j + 1) * high].astype(BF16)

    grad_tiles(0, 2)
    pass_on()
    grad_tiles(2, t_ref.shape[1] // wide - 2)
    h_load = pltpu.make_async_copy(g_ref.at[:, pl.ds(deep, deep)], h_v, h_sem)
    h_load.start()
    h_load.wait()
    pltpu.emit_pipeline(
        wide_body,
        grid=(8,),
        in_specs=[pl.BlockSpec((tokens, x_ref.shape[1] // 8), lambda i: (0, i))],
        out_specs=[
            pl.BlockSpec((4, 1, x_ref.shape[1] // 32, deep), lambda i: (0, i, 0, 0))
        ],
    )(x_ref, wide_ref)
    end()
    out = pltpu.make_async_copy(kept.at[0], out_ref, out_sem)
    out.start()
    crossing(2, 0).wait_send()
    crossing(0, 1).wait_send()
    out.wait()


def plane_sum(g, w, h, t, x, rows):
    dma, anywhere = pltpu.SemaphoreType.DMA, pl.BlockSpec(memory_space=pl.ANY)
    width, deep = w.shape
    return pl.pallas_call(
        plane_sum_kernel,
        out_shape=[
            jax.ShapeDtypeStruct((rows, width), BF16),
            jax.ShapeDtypeStruct((h.shape[1], t.shape[1]), BF16),
            jax.ShapeDtypeStruct((4, 8, width // 32, h.shape[1]), BF16),
        ],
        in_specs=[anywhere] * 5,
        out_specs=[anywhere] * 3,
        scratch_shapes=[
            pltpu.VMEM((width, deep), BF16),
            pltpu.VMEM((2, rows, deep), BF16),
            pltpu.VMEM(h.shape, BF16),
            dma,
            dma((2,)),
            dma,
            dma,
            *sums_scratch(rows, width),
        ],
        compiler_params=pltpu.CompilerParams(
            collective_id=5, has_side_effects=True, vmem_limit_bytes=62 * 2**20
        ),
        name="plane_sum",
    )(g, w, h, t, x)


def sigmoid(v):
    return 1.0 / (1.0 + jnp.exp(-v))


def load_rows(w_ref, w_v, sem, n_dp, n_seq):
    rows = w_v.shape[0] // (n_dp * n_seq)

    @pl.loop(0, n_dp * n_seq)
    def _(i):
        src = pl.ds(pl.multiple_of(i * rows, rows), rows)
        place = (i % n_dp) * n_seq + i // n_dp
        dst = pl.ds(pl.multiple_of(place * rows, rows), rows)
        pltpu.make_async_copy(w_ref.at[src], w_v.at[dst], sem).start()

    return pltpu.make_async_copy(w_ref, w_v, sem).wait


def gate_up_kernel(n_dp, n_seq, x_ref, dh_ref, w_ref, hidden_ref, dgu_ref, w_v, sem):
    pl.when(pl.program_id(0) == 0)(lambda: load_rows(w_ref, w_v, sem, n_dp, n_seq)())
    part = hidden_ref.shape[1]
    step = 256 if part % 256 == 0 else 128
    for c in range(0, part, step):
        first, second = slice(c, c + step), slice(part + c, part + c + step)
        gate, up = dot(x_ref[...], w_v[:, first]), dot(x_ref[...], w_v[:, second])
        dhidden = dh_ref[:, first].astype(F32)
        sig = sigmoid(gate)
        silu = gate * sig
        hidden_ref[:, first] = (silu * up).astype(BF16)
        dgu_ref[:, first] = (dhidden * up * (sig + silu * (1.0 - sig))).astype(BF16)
        dgu_ref[:, second] = (dhidden * silu).astype(BF16)


def gate_up_product(x, dhidden, w, n_dp, n_seq):
    tokens, width = x.shape
    wide = w.shape[1]
    block = 512
    span = lambda columns: pl.BlockSpec((block, columns), lambda i: (i, 0))
    return pl.pallas_call(
        functools.partial(gate_up_kernel, n_dp, n_seq),
        grid=(tokens // block,),
        in_specs=[span(width), span(wide // 2), pl.BlockSpec(memory_space=pl.ANY)],
        out_specs=[span(wide // 2), span(wide)],
        out_shape=[
            jax.ShapeDtypeStruct((tokens, wide // 2), BF16),
            jax.ShapeDtypeStruct((tokens, wide), BF16),
        ],
        scratch_shapes=[pltpu.VMEM(w.shape, BF16), pltpu.SemaphoreType.DMA],
        compiler_params=pltpu.CompilerParams(vmem_limit_bytes=56 * 2**20),
        cost_estimate=pl.CostEstimate(
            flops=2 * tokens * width * wide,
            bytes_accessed=2 * (tokens * width + width * wide + tokens * wide * 2),
            transcendentals=tokens * wide // 2,
        ),
        name="gate_up",
    )(x, dhidden, w)


def mm(a, b):
    return jnp.dot(a, b, preferred_element_type=F32)


def outer_sum(left, right):
    return lax.dot_general(left, right, (((0,), (0,)), ((), ())), preferred_element_type=F32)


def back_product(rows, weight):
    return lax.dot_general(rows, weight, (((1,), (1,)), ((), ())), preferred_element_type=F32)


def gather(x, axes):
    return lax.all_gather(x, axes, axis=0, tiled=True)


def scatter(x, axes):
    return lax.psum_scatter(x, axes, scatter_dimension=0, tiled=True)


def shards(
    tokens, lengths, w_qkv, w_out, w_gate_up, w_down, attn_gain, ffn_gain, head_gains, out_grad
):
    n_dp, n_seq = lax.axis_size("dp"), lax.axis_size("seq")
    rows, length, width = tokens.shape
    count = rows * length
    ff = w_gate_up.shape[1] // 2
    part = ff // n_dp
    wr = w_gate_up.shape[0]
    offset = lax.axis_index("seq") * length
    local_pos = offset + jnp.arange(length, dtype=jnp.int32)
    cosine, sine = rope_tables(jnp.concatenate([local_pos] * rows))
    ends = jnp.cumsum(lengths, axis=1, dtype=jnp.int32)
    start = jnp.sum(
        jnp.where(local_pos[None, :, None] >= ends[:, None, :], lengths[:, None, :], 0), axis=2
    ).reshape(1, count)
    start = jnp.broadcast_to(start, (8, count))

    full = (n_dp, n_seq) == (8, 4)
    qkv_w = w_qkv.shape[1]
    spare = width - qkv_w
    gains = jnp.concatenate([attn_gain, ffn_gain])
    gains = [jnp.pad(g, (0, spare - g.shape[0]))[None] for g in (gains, head_gains)]
    gains.append(jnp.zeros((wr - 2, spare), BF16))
    own_qkv = jnp.concatenate([w_qkv, jnp.concatenate(gains, axis=0)], axis=1)
    out_rows = w_out.shape[0]
    own_out = jnp.pad(w_out, ((0, -out_rows % 16), (0, 0)))
    all_qkv, some_out, spread = gather_weights(own_qkv, [own_out], w_gate_up, n_dp, n_seq)
    qkv_full = all_qkv.reshape(width, width)
    attn_gain_full = all_qkv[:, 0, qkv_w : qkv_w + wr].reshape(-1).astype(F32)
    ffn_gain_full = all_qkv[:, 0, qkv_w + wr : qkv_w + 2 * wr].reshape(-1).astype(F32)
    head_full = all_qkv[:, 1, qkv_w : qkv_w + head_gains.shape[0]].reshape(-1).astype(F32)

    attn_gain_full, ffn_gain_full, head_full = lax.optimization_barrier(
        (attn_gain_full[None], ffn_gain_full[None], head_full)
    )

    w_down, qkv_full = lax.optimization_barrier((w_down, qkv_full))
    down_w = gather(w_down, "seq")
    cotangent_low = out_grad.reshape(count, width)

    x_rows = tokens.reshape(count, width).astype(F32)
    normed_low = norm_rows(x_rows, attn_gain_full).astype(BF16)
    projected = lax.dot_general(
        qkv_full, normed_low, (((0,), (1,)), ((), ())), preferred_element_type=F32
    )

    queries, pairs = prepare(projected, head_full[:, None], cosine, sine)
    more = [cotangent_low, some_out] if full else []
    heads_out, lse, held, *planes = attend(start, queries, pairs, rows, n_seq, more, out_rows)
    gate_up_w = gather(spread.reshape(n_dp * wr, 2 * part), "seq")
    if full:
        cotangent_all, all_out, heads_full = planes
        cotangent_all = cotangent_all.reshape(n_dp * count, width)
        out_full = all_out.reshape(-1, width)
        normed2_all, dhidden, middle = plane_gather(
            heads_full, all_out, tokens.reshape(count, width), ffn_gain_full,
            cotangent_all, down_w,
        )
    else:
        cotangent_all, all_out = gather(cotangent_low, "dp"), some_out
        out_full = all_out.reshape(-1, width)
        fill = ((0, 0), (0, all_out.shape[1] - out_rows), (0, 0))
        heads_full = jnp.pad(heads_out.reshape(n_dp * n_seq, out_rows, count), fill)
        heads_full = heads_full.reshape(-1, count)
        middle = x_rows + outer_sum(heads_full, out_full)
        normed2_all = gather(norm_rows(middle, ffn_gain_full).astype(BF16), "dp")
        dhidden = back_product(cotangent_all, down_w).astype(BF16)
    hidden, dgate_up = gate_up_product(normed2_all, dhidden, gate_up_w, n_dp, n_seq)
    gate_grad = transposed_product(normed2_all, dgate_up, n_dp, n_seq, 2 if full else 1)
    gate_grad, dgate_up = lax.optimization_barrier((gate_grad, dgate_up))
    gate_grad = scatter(gate_grad.reshape(width, -1), "seq")
    if full:
        dnormed2, down_grad, up_grad = plane_sum(
            dgate_up, gate_up_w, hidden, cotangent_all, normed2_all, count
        )
        gate_grad, up_grad, dnormed2 = lax.optimization_barrier((gate_grad, up_grad, dnormed2))
        up_grad = scatter(up_grad.reshape(width, part), "seq")
    else:
        ordered = gate_up_w.reshape(n_seq, n_dp, wr, 2 * part).transpose(1, 0, 2, 3)
        ordered = ordered.reshape(width, 2 * part)
        dnormed2 = scatter(back_product(dgate_up, ordered).astype(BF16), "dp")
        down_grad = outer_sum(hidden, cotangent_all).astype(BF16)
    if full:
        dmiddle, dattend, dheads = middle_back(
            dnormed2, middle, cotangent_low, ffn_gain_full, out_full, out_rows
        )
    else:
        dmiddle = cotangent_low.astype(F32)
        dmiddle += normed_back(dnormed2.astype(F32), middle, ffn_gain_full)
        dattend = dmiddle.astype(BF16)
        dheads = back_product(out_full, dattend).astype(BF16).reshape(n_dp * n_seq, -1, count)
        dheads = dheads[:, :out_rows].reshape(QW, count)
    if full:
        dqueries, dpairs, mixed = attend_back(
            start, queries, dheads, heads_out, lse, pairs, held, rows, n_seq,
            [hidden, down_w, middle],
        )
    else:
        dqueries, dpairs = attend_back(
            start, queries, dheads, heads_out, lse, pairs, held, rows, n_seq, []
        )
        mixed = middle + scatter(mm(hidden, down_w).astype(BF16), "dp").astype(F32)
    if full:
        gate_grad, up_grad, dqueries = lax.optimization_barrier((gate_grad, up_grad, dqueries))
        up_grad = up_grad.reshape(n_dp, wr, part)
    gate_grad = gate_grad.reshape(n_dp, wr, -1)
    down_grad, dqueries = lax.optimization_barrier((down_grad, dqueries))
    down_grad = scatter(down_grad, "seq")
    dprojected_low, head_grad = prepare_back(
        projected, head_full[:, None], cosine, sine, dqueries, dpairs, width, n_dp * n_seq
    )
    few = head_gains.shape[0]
    if full:
        qkv_grad, small, out_weight_grad, tokens_grad, gate_up_grad = (
            sum_weights(
                normed_low,
                dprojected_low,
                heads_full,
                dattend,
                head_grad,
                own_qkv,
                qkv_full,
                tokens.reshape(count, width),
                dmiddle,
                attn_gain_full,
                gate_grad,
                up_grad,
                w_gate_up,
                out_rows,
            )
        )
        qkv_products, ffn_products, head_out = small[0, :wr], small[1, :wr], small[2, :few]
    else:
        qkv_grad = lax.dot_general(
            normed_low, dprojected_low, (((0,), (1,)), ((), ())), preferred_element_type=F32
        ).astype(BF16)
        out_grads = mm(heads_full, dattend).astype(BF16)
        qkv_grad, out_weight_grad = (
            scatter(scatter(g, "dp"), "seq").astype(F32) for g in (qkv_grad, out_grads)
        )
        head_out = jnp.sum(
            lax.all_to_all(head_grad[:, :few, 0], BOTH, 0, 0, tiled=True), axis=0
        )
        qkv_products = jnp.sum(own_qkv[:, :qkv_w].astype(F32) * qkv_grad[:, :qkv_w], axis=1)
        qkv_grad = qkv_grad[:, :qkv_w]
        gate_up_grad = lax.all_to_all(gate_grad, "dp", 0, 0, tiled=True)
        gate_up_grad = gate_up_grad.reshape(n_dp, wr, 2, part).transpose(1, 2, 0, 3)
        gate_up_grad = gate_up_grad.reshape(wr, 2 * ff).astype(F32)
        ffn_products = jnp.sum(w_gate_up.astype(F32) * gate_up_grad, axis=1)
        dnormed = back_product(dprojected_low.T, qkv_full)
        tokens_grad = dmiddle + normed_back(dnormed, x_rows, attn_gain_full)
    attn_gain_out = qkv_products / attn_gain.astype(F32)
    ffn_gain_out = ffn_products / ffn_gain.astype(F32)
    return (
        mixed.astype(BF16).reshape(rows, length, width),
        tokens_grad.reshape(rows, length, width),
        qkv_grad,
        out_weight_grad[:out_rows],
        gate_up_grad,
        down_grad.astype(F32),
        attn_gain_out,
        ffn_gain_out,
        head_out,
    )


def solution(mesh):
    in_specs = (
        P("dp", "seq", None),
        P("dp", None),
        P(("dp", "seq"), None),
        P(("dp", "seq"), None),
        P(("dp", "seq"), None),
        P(("dp", "seq"), None),
        P(("dp", "seq")),
        P(("dp", "seq")),
        P(("dp", "seq")),
        P("dp", "seq", None),
    )
    out_specs = (
        P("dp", "seq", None),
        P("dp", "seq", None),
        P(("dp", "seq"), None),
        P(("dp", "seq"), None),
        P(("dp", "seq"), None),
        P(("dp", "seq"), None),
        P(("dp", "seq")),
        P(("dp", "seq")),
        P(("dp", "seq")),
    )
    return jax.shard_map(shards, mesh=mesh, in_specs=in_specs, out_specs=out_specs, check_vma=False)
```
